32 devices in a mesh: dp: 4 (over y, x), pipe: 8 (over z, core).
Axes of the slice: x: 2, y: 2, z: 4, core: 2. Of those that a mesh axis runs over, the one named last changes fastest.
Arguments:
- activations: bfloat16 [8, 2048, 8192], P('pipe', 'dp'), may hold values from -6 to 6
- cotangent: bfloat16 [2048, 8192], P('dp'), may hold values from -6 to 6
- adapter_down: bfloat16 [8, 8192, 512], P('pipe'), may hold values from -0.0625 to 0.0625
- adapter_expand: bfloat16 [8, 512, 8192], P('pipe'), may hold values from -0.25 to 0.25
- value_rows: bfloat16 [8, 32, 8192], P('pipe', 'dp'), may hold values from -0.0625 to 0.0625
- input_rows: bfloat16 [8, 32, 8192], P('pipe', 'dp'), may hold values from -0.0625 to 0.0625
- hidden_cols: bfloat16 [8, 32, 512], P('pipe'), may hold values from -0.25 to 0.25
- inner_cols: bfloat16 [8, 32, 512], P('pipe'), may hold values from -0.25 to 0.25
- lengths: int32 [16], P('dp'), may hold values from 1 to 128, as said below
- query_example: int32 [32], replicated, may hold values from 0 to 15
Outputs:
- scores: float32 [16, 32], P('dp')
The draws below stay inside these ranges and needn't reach their ends.
Inputs may be any that keep to these rules, and one draw needn't show every extreme that they name: `lengths`: live tokens of each example; the rest of its 128 positions is padding.
All inputs are finite; a program needn't handle non-finite values.
Results may differ from the reference program's by a relative error of at most 0.022.
Values may be sent and summed in bfloat16 or wider, within the bound.
No kernel may reach another device: no remote copies, remote signals or barrier semaphores. Data moves between devices by JAX's collectives and lax.ppermute only.
A program may use at most 128 MiB of HBM per device.

```python
import jax
import jax.numpy as jnp

D = 8192
R = 512
Q = 32
SLOT = 128
LAYERS = 8
TOKENS = 2048
EXAMPLES = 16


def draw_lengths(key, part):
    drawn = jax.random.randint(key, (EXAMPLES,), SLOT // 2, 2 * SLOT, dtype=jnp.int32)
    return jnp.minimum(drawn, SLOT).astype(jnp.int32)


def plant(result, stream_key, least, high):
    spot = [jax.random.randint(jax.random.fold_in(stream_key, axis), (), 0, length) for axis, length in enumerate(result.shape)]
    widest = result.shape.index(max(result.shape))
    neighbour = spot[:widest] + [(spot[widest] + 1) % result.shape[widest]] + spot[widest + 1:]
    return result.at[tuple(spot)].set(least).at[tuple(neighbour)].set(high)


def block_scale(stream_key, dims, shards, smallest, top_value):
    factor_of = 1.0
    for position, shards_of in shards:
        steps = jax.random.uniform(jax.random.fold_in(jax.random.fold_in(stream_key, 6), position), (shards_of,), jnp.float32, smallest / len(shards), top_value / len(shards))
        factor_of = factor_of * jnp.repeat(jnp.exp(steps), dims[position] // shards_of).reshape((-1,) + (1,) * (len(dims) - 1 - position))
    return factor_of


def centred(own_key, dims, width, bound, pieces=(), kind=jnp.bfloat16):
    entries = jax.random.normal(own_key, dims, jnp.float32) * width
    if len(pieces) > 0:
        entries = block_scale(own_key, dims, pieces, -0.22, 0.18) * entries
    return jnp.clip(entries, min=-bound, max=bound).astype(kind)


def setup_inputs(seed: int = 0) -> dict:
    key_of = jax.random.split(jax.random.key(seed), 11)
    return {
        "activations": centred(key_of[0], (LAYERS, TOKENS, D), 1.0, 6.0, ((0, 8), (1, 4))),
        "cotangent": centred(key_of[1], (TOKENS, D), 1.0, 6.0, ((0, 4),)),
        "adapter_down": centred(key_of[2], (LAYERS, D, R), D ** -0.5, 0.0625, ((0, 8),)),
        "adapter_expand": centred(key_of[3], (LAYERS, R, D), R ** -0.5, 0.25, ((0, 8),)),
        "value_rows": centred(key_of[4], (LAYERS, Q, D), D ** -0.5, 0.0625, ((0, 8), (1, 4))),
        "input_rows": centred(key_of[5], (LAYERS, Q, D), D ** -0.5, 0.0625, ((0, 8), (1, 4))),
        "hidden_cols": centred(key_of[6], (LAYERS, Q, R), R ** -0.5, 0.25, ((0, 8),)),
        "inner_cols": centred(key_of[7], (LAYERS, Q, R), R ** -0.5, 0.25, ((0, 8),)),
        "lengths": draw_lengths(jax.random.fold_in(key_of[10], 71), 0),
        "query_example": plant(jax.random.randint(key_of[9], (Q,), 0, EXAMPLES), jax.random.fold_in(key_of[9], 1), 0, EXAMPLES - 1).astype(jnp.int32),
    }


adapter_scale = 0.25


def reference(activations, cotangent, adapter_down, adapter_expand, value_rows, input_rows, hidden_cols, inner_cols, lengths, query_example):
    offsets = jnp.arange(TOKENS, dtype=jnp.int32) % SLOT
    live_mask = (offsets < jnp.repeat(lengths, SLOT, total_repeat_length=TOKENS)).astype(jnp.float32)
    gradient_leaving = cotangent
    totals = jnp.zeros((EXAMPLES, Q), jnp.float32)
    for layer_weights in reversed(range(LAYERS)):
        act_rows = activations[layer_weights]
        hidden = jnp.dot(act_rows, adapter_down[layer_weights], preferred_element_type=jnp.float32).astype(jnp.bfloat16)
        inner_gradient = (adapter_scale * jnp.dot(gradient_leaving, adapter_expand[layer_weights].T, preferred_element_type=jnp.float32)).astype(jnp.bfloat16)
        gradient_entering = (gradient_leaving.astype(jnp.float32) + jnp.dot(inner_gradient, adapter_down[layer_weights].T, preferred_element_type=jnp.float32)).astype(jnp.bfloat16)
        hidden_projection = jnp.dot(hidden, hidden_cols[layer_weights].T, preferred_element_type=jnp.float32)
        value_projection = jnp.dot(gradient_leaving, value_rows[layer_weights].T, preferred_element_type=jnp.float32)
        input_projection = jnp.dot(act_rows, input_rows[layer_weights].T, preferred_element_type=jnp.float32)
        inner_projection = jnp.dot(inner_gradient, inner_cols[layer_weights].T, preferred_element_type=jnp.float32)
        summand_rows = adapter_scale * hidden_projection * value_projection + input_projection * inner_projection
        masked = summand_rows * live_mask[:, None]
        totals = totals + jnp.sum(masked.reshape(EXAMPLES, SLOT, Q), axis=1)
        gradient_leaving = gradient_entering
    totals = totals * (SLOT ** -0.5)
    example_ids = jnp.arange(EXAMPLES, dtype=jnp.int32)
    keep_mask = (example_ids[:, None] != query_example[None, :]).astype(jnp.float32)
    return totals * keep_mask
```

```python
import jax
import jax.numpy as jnp
from jax import lax
from jax.sharding import PartitionSpec as P

SLOT = 128


adapter_scale = 0.25


def dot_nn(a, b):
    return lax.dot_general(a, b, (((1,), (0,)), ((), ())), preferred_element_type=jnp.float32)


def dot_nt(a, b):
    return lax.dot_general(a, b, (((1,), (1,)), ((), ())), preferred_element_type=jnp.float32)


def swap(value, axis, distance):
    count = lax.axis_size(axis)
    return lax.ppermute(value, axis, [(source, source ^ distance) for source in range(count)])


def upward(value, axis):
    count = lax.axis_size(axis)
    return lax.ppermute(value, axis, [(source, source + 1) for source in range(count - 1)])


def local(
    activations,
    cotangent,
    adapter_down,
    adapter_expand,
    value_rows,
    input_rows,
    hidden_cols,
    inner_cols,
    lengths,
    query_example,
):
    columns = lax.axis_size("dp")
    layers = lax.axis_size("pipe")
    column = lax.axis_index("dp")
    layer = lax.axis_index("pipe")
    tok_dev = activations.shape[1]
    ex_dev = tok_dev // SLOT
    q_dev = value_rows.shape[1]
    act = activations[0]
    down = adapter_down[0]
    expand = adapter_expand[0]
    values = value_rows[0]
    inputs = input_rows[0]
    bf16 = jnp.bfloat16

    def relative(rows):
        return [
            lax.dynamic_slice_in_dim(rows, (column ^ d) * q_dev, q_dev, 0) for d in range(columns)
        ]

    hid_blocks = relative(hidden_cols[0])
    inn_blocks = relative(inner_cols[0])
    own = jnp.concatenate([values, inputs])
    blocks = [own] + [swap(own, "dp", d) for d in range(1, columns)]
    value_all = jnp.concatenate([b[:q_dev] for b in blocks])
    input_all = jnp.concatenate([b[q_dev:] for b in blocks])
    hid_all = jnp.concatenate(hid_blocks)
    inn_all = jnp.concatenate(inn_blocks)

    raised = (adapter_scale * dot_nn(inn_blocks[0], expand)).astype(bf16)
    moving = jnp.concatenate([values, raised])
    seen = []
    for step in range(layers - 1):
        arrived = upward(moving, "pipe")
        ranks = dot_nn(arrived, down).astype(bf16)
        seen.append(ranks)
        if step < layers - 2:
            moving = (
                arrived.astype(jnp.float32) + adapter_scale * dot_nn(ranks, expand)
            ).astype(bf16)

    hidden = dot_nn(act, down).astype(bf16)
    offsets = lax.broadcasted_iota(jnp.int32, (ex_dev, SLOT, 1), 1)
    live = (offsets < lengths[:, None, None]).astype(jnp.float32).reshape(tok_dev, 1)
    weight = live * SLOT ** (-0.5)
    left = jnp.concatenate(
        [adapter_scale * dot_nt(hidden, hid_all), dot_nt(act, input_all)], axis=1
    ) * weight
    lifted = (adapter_scale * dot_nt(cotangent, expand)).astype(bf16)
    right = jnp.concatenate([dot_nt(cotangent, value_all), dot_nt(lifted, inn_all)], axis=1)
    terms = left * right

    stack = left.astype(bf16)[None]
    order = 1
    while order < layers:
        stack = jnp.concatenate([stack, swap(stack, "pipe", order)])
        order *= 2

    for step, ranks in enumerate(seen):
        every = [ranks] + [swap(ranks, "dp", d) for d in range(1, columns)]
        every = jnp.concatenate([b[:q_dev] for b in every] + [b[q_dev:] for b in every])
        source = jnp.maximum(layer - 1 - step, 0)
        weights = lax.dynamic_index_in_dim(stack, source ^ layer, 0, keepdims=False)
        terms = terms + weights.astype(jnp.float32) * dot_nt(lifted, every)

    sums = jnp.sum(terms.reshape(ex_dev, SLOT, -1), axis=1)
    q_all = columns * q_dev
    sums = sums[:, :q_all] + sums[:, q_all:]
    order = 1
    while order < layers:
        sums = sums + swap(sums, "pipe", order)
        order *= 2

    sums = sums.reshape(ex_dev, columns, q_dev)
    totals = jnp.concatenate(
        [lax.dynamic_index_in_dim(sums, column ^ c, 1, keepdims=False) for c in range(columns)],
        axis=1,
    )
    example_ids = column * ex_dev + lax.broadcasted_iota(jnp.int32, (ex_dev,), 0)
    keep_mask = (example_ids[:, None] != query_example[None, :]).astype(jnp.float32)
    return totals * keep_mask


def solution(mesh):
    in_specs = (
        P("pipe", "dp", None),
        P("dp", None),
        P("pipe", None, None),
        P("pipe", None, None),
        P("pipe", "dp", None),
        P("pipe", "dp", None),
        P("pipe", None, None),
        P("pipe", None, None),
        P("dp"),
        P(),
    )
    out_specs = P("dp", None)
    return jax.shard_map(local, mesh=mesh, in_specs=in_specs, out_specs=out_specs, check_vma=False)
```

```python
import jax
import jax.numpy as jnp
from jax import lax
from jax.sharding import PartitionSpec as P

SLOT = 128


adapter_scale = 0.25


def dot_nn(a, b):
    return lax.dot_general(a, b, (((1,), (0,)), ((), ())), preferred_element_type=jnp.float32)


def dot_nt(a, b):
    return lax.dot_general(a, b, (((1,), (1,)), ((), ())), preferred_element_type=jnp.float32)


def swap(value, axis, distance):
    count = lax.axis_size(axis)
    return lax.ppermute(value, axis, [(source, source ^ distance) for source in range(count)])


def spread(value, axis):
    return [value] + [swap(value, axis, d) for d in range(1, lax.axis_size(axis))]


def upward(value, first, hop, stride):
    count = lax.axis_size("pipe")
    return lax.ppermute(
        value, "pipe", [(source, source + hop) for source in range(first, count - hop, stride)]
    )


def tie(values, token):
    *values, _ = lax.optimization_barrier((*values, token))
    return values


def local(
    activations,
    cotangent,
    adapter_down,
    adapter_expand,
    value_rows,
    input_rows,
    hidden_cols,
    inner_cols,
    lengths,
    query_example,
):
    bf16 = jnp.bfloat16
    columns = lax.axis_size("dp")
    chips = lax.axis_size("pipe") // 2
    column = lax.axis_index("dp")
    upper = lax.axis_index("pipe") % 2 == 1
    tok_dev = activations.shape[1]
    ex_dev = tok_dev // SLOT
    q_dev = value_rows.shape[1]
    rows = 2 * q_dev
    act = activations[0]
    down = adapter_down[0]
    expand = adapter_expand[0]

    def blocks_of(cols):
        return jnp.concatenate(
            [lax.dynamic_slice_in_dim(cols, (column ^ d) * q_dev, q_dev, 0) for d in range(columns)]
        )

    def weave(first, second):
        parts = []
        for d in range(columns):
            parts += [first[d], second[d]]
        return jnp.concatenate(parts)

    def cut(stacked, size):
        return [stacked[d * size : (d + 1) * size] for d in range(columns)]

    def through(arrived):
        ranks = dot_nn(arrived, down).astype(bf16)
        leaving = arrived.astype(jnp.float32) + adapter_scale * dot_nn(ranks, expand)
        return ranks, leaving.astype(bf16)

    raised = (adapter_scale * dot_nn(blocks_of(inner_cols[0]), expand)).astype(bf16)
    raised = cut(raised, q_dev)
    own = jnp.concatenate([value_rows[0], raised[0]])

    arrived = upward(own, 0, 1, 2)
    ranks, leaving = through(arrived)
    lower_ranks = ranks
    moving = jnp.concatenate([leaving, own])

    arrived = upward(moving, 1, 1, 2)
    width_rows, cot = tie([jnp.concatenate([value_rows[0], input_rows[0]]), cotangent], moving)
    width_rows = spread(width_rows, "dp")
    lifted = (adapter_scale * dot_nt(cot, expand)).astype(bf16)
    arrived, lifted = lax.optimization_barrier((arrived, lifted))

    slots = []
    left = right = None
    for slot in range(1, chips):
        ranks_even, leaving = through(arrived)
        arrived = upward(leaving, 0, 1, 2)
        ranks_odd, leaving = through(arrived)
        slots.append(jnp.where(upper, ranks_odd, ranks_even))
        if slot == chips - 1:
            break
        arrived = upward(leaving, 1, 1, 2)
        if slot == 1:
            x, hid = tie([act, blocks_of(hidden_cols[0])], leaving)
            hid = (adapter_scale * dot_nt(hid, down)).astype(bf16)
            inputs = [b[q_dev:] for b in width_rows]
            left = dot_nt(x, weave(cut(hid, q_dev), inputs))
            offsets = lax.broadcasted_iota(jnp.int32, (ex_dev, SLOT, 1), 1)
            live = (offsets < lengths[:, None, None]).astype(jnp.float32).reshape(tok_dev, 1)
            left = left * live
            left_own = left.astype(bf16)
            left_up = [left_own] + [
                upward(left_own, 0, 2 * hop, 1) for hop in range(1, chips)
            ]
            arrived, left_own = lax.optimization_barrier((arrived, left_own))
        if slot == 2 or chips == 3:
            (cot,) = tie([cotangent], leaving)
            right = dot_nt(cot, weave([b[:q_dev] for b in width_rows], raised))
            left_up = jnp.stack(left_up)
            left_other = swap(left_up, "pipe", 1)
            left_even = jnp.where(upper, left_other, left_up)
            left_odd = jnp.where(upper, left_up, left_other)
            arrived, right = lax.optimization_barrier((arrived, right))

    def weighed(weights, ranks):
        return weights.astype(jnp.float32) * dot_nt(lifted, ranks)

    early = jnp.concatenate([lower_ranks] + slots[:-1])
    early = spread(early, "dp")
    terms = left * right + weighed(left_even[0], jnp.concatenate([b[:rows] for b in early]))
    for slot in range(1, chips - 1):
        at = rows * (2 * slot - 1)
        terms += weighed(left_even[slot], jnp.concatenate([b[at : at + rows] for b in early]))
        at += rows
        terms += weighed(left_odd[slot], jnp.concatenate([b[at : at + rows] for b in early]))

    late = spread(slots[-1], "dp")
    terms += weighed(left_even[-1], jnp.concatenate([b[:rows] for b in late]))
    terms += weighed(left_odd[-1], jnp.concatenate([b[rows:] for b in late]))

    sums = jnp.sum(terms.reshape(ex_dev, SLOT, columns, 2, q_dev), axis=(1, 3))
    sums = sums.reshape(ex_dev, columns * q_dev)
    sums = sums + swap(sums, "pipe", 1)
    parts = [swap(sums, "pipe", 2 * hop) for hop in range(1, chips)]
    for part in parts:
        sums = sums + part

    sums = sums.reshape(ex_dev, columns, q_dev)
    totals = jnp.concatenate(
        [lax.dynamic_index_in_dim(sums, column ^ c, 1, keepdims=False) for c in range(columns)],
        axis=1,
    )
    example_ids = column * ex_dev + lax.broadcasted_iota(jnp.int32, (ex_dev,), 0)
    keep_mask = (example_ids[:, None] != query_example[None, :]).astype(jnp.float32)
    return totals * SLOT ** (-0.5) * keep_mask


def solution(mesh):
    in_specs = (
        P("pipe", "dp", None),
        P("dp", None),
        P("pipe", None, None),
        P("pipe", None, None),
        P("pipe", "dp", None),
        P("pipe", "dp", None),
        P("pipe", None, None),
        P("pipe", None, None),
        P("dp"),
        P(),
    )
    out_specs = P("dp", None)
    return jax.shard_map(local, mesh=mesh, in_specs=in_specs, out_specs=out_specs, check_vma=False)
```

```python
import functools

import jax
import jax.numpy as jnp
from jax import lax
from jax.experimental import pallas as pl
from jax.experimental.pallas import tpu as pltpu
from jax.sharding import PartitionSpec as P

SLOT = 128


adapter_scale = 0.25
bf16 = jnp.bfloat16
f32 = jnp.float32
VMEM = pltpu.VMEM


def dot_nn(a, b):
    return lax.dot_general(a, b, (((1,), (0,)), ((), ())), preferred_element_type=f32)


def dot_nt(a, b):
    return lax.dot_general(a, b, (((1,), (1,)), ((), ())), preferred_element_type=f32)


def swap(value, axis, distance):
    count = lax.axis_size(axis)
    return lax.ppermute(value, axis, [(source, source ^ distance) for source in range(count)])


def spread(value, axis):
    return [value] + [swap(value, axis, d) for d in range(1, lax.axis_size(axis))]


def upward(value, first, hop, stride):
    count = lax.axis_size("pipe")
    return lax.ppermute(
        value, "pipe", [(source, source + hop) for source in range(first, count - hop, stride)]
    )


def tie(values, token):
    *values, _ = lax.optimization_barrier((*values, token))
    return values


def held(value):
    return pltpu.with_memory_space_constraint(value, VMEM)


def call(kernel, operands, places, outs, scratch, flops, moved):
    space = {"v": VMEM, "s": pltpu.SMEM, "a": pl.ANY}
    operands = [held(x) if place == "v" else x for x, place in zip(operands, places)]
    return pl.pallas_call(
        kernel,
        in_specs=[pl.BlockSpec(memory_space=space[place]) for place in places],
        out_specs=[pl.BlockSpec(memory_space=VMEM) for _ in outs],
        out_shape=[VMEM(shape, dtype) for shape, dtype in outs],
        scratch_shapes=scratch,
        cost_estimate=pl.CostEstimate(flops=flops, bytes_accessed=moved, transcendentals=0),
        compiler_params=pltpu.CompilerParams(vmem_limit_bytes=24 * 2**20),
    )(*operands)


PARTS = 8


def prime_kernel(cols, padded, expand, kept, raised, own, sems):
    width = expand.shape[1] // PARTS
    copies = []
    for part in range(PARTS):
        span = pl.ds(part * width, width)
        copy = pltpu.make_async_copy(expand.at[:, span], kept.at[:, span], sems.at[part])
        copy.start()
        copies.append(copy)
    rows = own.shape[0]
    for part in range(PARTS):
        copies[part].wait()
        span = slice(part * width, (part + 1) * width)
        found = adapter_scale * dot_nn(cols[...], kept[:, span])
        raised[:, span] = found.astype(bf16)
        own[:, span] = (found[:rows] + padded[:, span]).astype(bf16)


def keep_kernel(down, kept, sem):
    copy = pltpu.make_async_copy(down, kept, sem)
    copy.start()
    copy.wait()


def through_kernel(flag, arrived, before, down, expand, ranks, leaving):
    depth, width = down.shape
    step = 2 * width

    @pl.when(flag[0] == 0)
    def _():
        ranks[...] = before[...]

    @pl.when(flag[0] != 0)
    def _():
        total = jnp.zeros(ranks.shape, f32)
        for at in range(0, depth, step):
            total += dot_nn(arrived[:, at : at + step], down[at : at + step, :])
        found = total.astype(bf16)
        ranks[...] = found
        for at in range(0, depth, step):
            more = adapter_scale * dot_nn(found, expand[:, at : at + step])
            leaving[:, at : at + step] = (arrived[:, at : at + step].astype(f32) + more).astype(bf16)


def last_kernel(flag, arrived, before, down, ranks):
    depth, width = down.shape
    step = 2 * width

    @pl.when(flag[0] == 0)
    def _():
        ranks[...] = before[...]

    @pl.when(flag[0] != 0)
    def _():
        total = jnp.zeros(ranks.shape, f32)
        for at in range(0, depth, step):
            total += dot_nn(arrived[:, at : at + step], down[at : at + step, :])
        ranks[...] = total.astype(bf16)


def start_rows(source, buffer, sems):
    copies = []
    for part in range(source.shape[0] // SLOT):
        span = pl.ds(part * SLOT, SLOT)
        copy = pltpu.make_async_copy(source.at[span], buffer.at[span], sems.at[part])
        copy.start()
        copies.append(copy)
    return copies


def lift_kernel(cotangent, expand, lifted, buffer, sems):
    copies = start_rows(cotangent, buffer, sems)
    ranks = expand.shape[0]
    half = ranks // 2
    for pair in range(0, len(copies), 2):
        copies[pair].wait()
        copies[pair + 1].wait()
        span = slice(pair * SLOT, (pair + 2) * SLOT)
        for at in range(0, ranks, half):
            found = adapter_scale * dot_nt(buffer[span, :], expand[at : at + half, :])
            lifted[span, at : at + half] = found.astype(bf16)


def value_row(shape, q_dev):
    return (lax.broadcasted_iota(jnp.int32, shape, 0) // q_dev) % 2 == 0


def right_kernel(q_dev, cotangent, rows, raised, right, buffer, woven, sems):
    copies = start_rows(cotangent, buffer, sems)
    depth = rows.shape[1]
    step = depth // PARTS
    for at in range(0, depth, step):
        span = slice(at, at + step)
        first = value_row((rows.shape[0], step), q_dev)
        woven[:, span] = jnp.where(
            first, rows[:, span].astype(f32), raised[:, span].astype(f32)
        ).astype(bf16)
    for part, copy in enumerate(copies):
        copy.wait()
        span = slice(part * SLOT, (part + 1) * SLOT)
        right[span, :] = dot_nt(buffer[span, :], woven[...])


def left_kernel(q_dev, lengths, act, cols, down, rows, left, left_sent, buffer, woven, sems):
    copies = start_rows(act, buffer, sems)
    depth = rows.shape[1]
    step = depth // PARTS
    for at in range(0, depth, step):
        span = slice(at, at + step)
        first = value_row((rows.shape[0], step), q_dev)
        found = adapter_scale * dot_nt(cols[...], down[span, :])
        woven[:, span] = jnp.where(first, found, rows[:, span].astype(f32)).astype(bf16)
    for part, copy in enumerate(copies):
        copy.wait()
        span = slice(part * SLOT, (part + 1) * SLOT)
        found = dot_nt(buffer[span, :], woven[...])
        live = lax.broadcasted_iota(jnp.int32, found.shape, 0) < lengths[part]
        found = jnp.where(live, found, 0.0)
        left[span, :] = found
        left_sent[span, :] = found.astype(bf16)


def local(
    activations,
    cotangent,
    adapter_down,
    adapter_expand,
    value_rows,
    input_rows,
    hidden_cols,
    inner_cols,
    lengths,
    query_example,
):
    columns = lax.axis_size("dp")
    layers = lax.axis_size("pipe")
    chips = layers // 2
    top = chips - 1
    column = lax.axis_index("dp")
    layer = lax.axis_index("pipe")
    upper = (layer % 2).astype(jnp.int32)[None]
    lower = 1 - upper
    tok_dev = activations.shape[1]
    ex_dev = tok_dev // SLOT
    q_dev = value_rows.shape[1]
    rows = 2 * q_dev
    width, rank = adapter_down.shape[1:]
    act = activations[0]
    weight_bytes = 2 * width * rank
    row_sems = pltpu.SemaphoreType.DMA((ex_dev,))

    def woven(cols, place):
        empty = jnp.zeros((q_dev, rank), bf16)
        parts = []
        for d in range(columns):
            block = lax.dynamic_slice_in_dim(cols, (column ^ d) * q_dev, q_dev, 0)
            parts += [block, empty] if place == 0 else [empty, block]
        return jnp.concatenate(parts)

    def through(flag, arrived, before):
        return call(
            through_kernel,
            (flag, arrived, before, down, expand),
            "svvvv",
            [(before.shape, bf16), (arrived.shape, bf16)],
            [],
            4 * arrived.shape[0] * width * rank,
            2 * weight_bytes,
        )

    padded = jnp.concatenate([value_rows[0], jnp.zeros_like(input_rows[0])])
    expand, raised, own = call(
        prime_kernel,
        (woven(inner_cols[0], 1), padded, adapter_expand[0]),
        "vva",
        [((rank, width), bf16), ((columns * rows, width), bf16), ((rows, width), bf16)],
        [pltpu.SemaphoreType.DMA((PARTS,))],
        2 * columns * rows * width * rank,
        2 * weight_bytes,
    )

    arrived = upward(own, 0, 1, 2)
    (source,) = tie([adapter_down[0]], own)
    (down,) = call(
        keep_kernel,
        (source,),
        "a",
        [((width, rank), bf16)],
        [pltpu.SemaphoreType.DMA],
        0,
        2 * weight_bytes,
    )
    empty = jnp.zeros((rows, rank), bf16)
    lower_ranks, leaving = through(upper, arrived, empty)
    moving = jnp.concatenate([leaving, own])

    arrived = upward(moving, 1, 1, 2)
    width_rows, cot = tie([jnp.concatenate([value_rows[0], input_rows[0]]), cotangent], moving)
    width_rows = spread(width_rows, "dp")
    (lifted,) = call(
        lift_kernel,
        (cot, expand),
        "av",
        [((tok_dev, rank), bf16)],
        [VMEM((tok_dev, width), bf16), row_sems],
        2 * tok_dev * width * rank,
        2 * weight_bytes,
    )
    arrived, lifted = lax.optimization_barrier((arrived, lifted))

    slots = []
    empty = jnp.zeros((2 * rows, rank), bf16)
    for slot in range(1, chips):
        found, leaving = through(lower, arrived, empty)
        arrived = upward(leaving, 0, 1, 2)
        if slot == 1:
            width_rows = jnp.concatenate(width_rows)
            arrived, width_rows = lax.optimization_barrier((arrived, width_rows))
        if slot == top:
            break
        found, leaving = through(upper, arrived, found)
        slots.append(found)
        arrived = upward(leaving, 1, 1, 2)
        if slot == 1:
            (x,) = tie([act], leaving)
            left, left_own = call(
                functools.partial(left_kernel, q_dev),
                (lengths, x, woven(hidden_cols[0], 0), down, width_rows),
                "savvv",
                [((tok_dev, columns * rows), f32), ((tok_dev, columns * rows), bf16)],
                [
                    VMEM((tok_dev, width), bf16),
                    VMEM((columns * rows, width), bf16),
                    row_sems,
                ],
                2 * columns * rows * width * (rank + tok_dev),
                2 * weight_bytes,
            )
            left_up = [left_own] + [upward(left_own, 0, 2 * hop, 1) for hop in range(1, chips)]
            arrived, left_own = lax.optimization_barrier((arrived, left_own))
        if slot == top - 1:
            early = jnp.concatenate([lower_ranks] + slots)
            cot, early = tie([cotangent, early], leaving)
            early = spread(early, "dp")
            (right,) = call(
                functools.partial(right_kernel, q_dev),
                (cot, width_rows, raised),
                "avv",
                [((tok_dev, columns * rows), f32)],
                [
                    VMEM((tok_dev, width), bf16),
                    VMEM((columns * rows, width), bf16),
                    row_sems,
                ],
                2 * columns * rows * width * tok_dev,
                weight_bytes,
            )
            left_up = jnp.stack(left_up)
            left_other = swap(left_up, "pipe", 1)
            left_even = jnp.where(upper > 0, left_other, left_up)
            left_odd = jnp.where(upper > 0, left_up, left_other)
            arrived, right = lax.optimization_barrier((arrived, right))

    def weighed(weights, ranks):
        return weights.astype(f32) * dot_nt(lifted, ranks)

    def summed(terms):
        terms = jnp.sum(terms.reshape(ex_dev, SLOT, columns, 2, q_dev), axis=(1, 3))
        return terms.reshape(ex_dev, columns * q_dev)

    terms = left * right + weighed(left_even[0], jnp.concatenate([b[:rows] for b in early]))
    for slot in range(1, top):
        at = rows * (2 * slot - 1)
        terms += weighed(left_even[slot], jnp.concatenate([b[at : at + rows] for b in early]))
        at += rows
        terms += weighed(left_odd[slot], jnp.concatenate([b[at : at + rows] for b in early]))
    sums = summed(terms)
    arrived, sums = lax.optimization_barrier((arrived, sums))

    def between(value, steps):
        pairs = [(2 * a + core, 2 * b + core) for a, b in steps for core in range(2)]
        return lax.ppermute(value, "pipe", pairs)

    parts = [between(sums, [(chip, top)]) for chip in range(top)]
    for part in parts:
        sums = sums + part

    (late,) = call(
        last_kernel,
        (upper, arrived, found, down),
        "svvv",
        [((2 * rows, rank), bf16)],
        [],
        2 * arrived.shape[0] * width * rank,
        weight_bytes,
    )
    late = spread(late, "dp")
    terms = weighed(left_even[-1], jnp.concatenate([b[:rows] for b in late]))
    terms += weighed(left_odd[-1], jnp.concatenate([b[rows:] for b in late]))
    sums = sums + summed(terms)
    sums = sums + lax.ppermute(
        sums, "pipe", [(2 * top, 2 * top + 1), (2 * top + 1, 2 * top)]
    )
    received = [between(sums, [(top, chip)]) for chip in range(top)]
    elsewhere = received[0]
    for part in received[1:]:
        elsewhere = elsewhere + part
    sums = jnp.where(layer >= 2 * top, sums, elsewhere)

    sums = sums.reshape(ex_dev, columns, q_dev)
    totals = jnp.concatenate(
        [lax.dynamic_index_in_dim(sums, column ^ c, 1, keepdims=False) for c in range(columns)],
        axis=1,
    )
    example_ids = column * ex_dev + lax.broadcasted_iota(jnp.int32, (ex_dev,), 0)
    keep_mask = (example_ids[:, None] != query_example[None, :]).astype(f32)
    return totals * SLOT ** (-0.5) * keep_mask


def solution(mesh):
    in_specs = (
        P("pipe", "dp", None),
        P("dp", None),
        P("pipe", None, None),
        P("pipe", None, None),
        P("pipe", "dp", None),
        P("pipe", "dp", None),
        P("pipe", None, None),
        P("pipe", None, None),
        P("dp"),
        P(),
    )
    out_specs = P("dp", None)
    return jax.shard_map(local, mesh=mesh, in_specs=in_specs, out_specs=out_specs, check_vma=False)
```

```python
import functools

import jax
import jax.numpy as jnp
from jax import lax
from jax.experimental import pallas as pl
from jax.experimental.pallas import tpu as pltpu
from jax.sharding import PartitionSpec as P

SLOT = 128
PARTS = 8


adapter_scale = 0.25
bf16 = jnp.bfloat16
f32 = jnp.float32
VMEM = pltpu.VMEM


def dot_nn(a, b, precision=None):
    return lax.dot_general(
        a, b, (((1,), (0,)), ((), ())), preferred_element_type=f32, precision=precision
    )


def dot_nt(a, b, precision=None):
    return lax.dot_general(
        a, b, (((1,), (1,)), ((), ())), preferred_element_type=f32, precision=precision
    )


def swap(value, axis, distance):
    count = lax.axis_size(axis)
    return lax.ppermute(value, axis, [(source, source ^ distance) for source in range(count)])


def spread(value, axis):
    return [value] + [swap(value, axis, d) for d in range(1, lax.axis_size(axis))]


def upward(value, first, hop, stride):
    count = lax.axis_size("pipe")
    return lax.ppermute(
        value, "pipe", [(source, source + hop) for source in range(first, count - hop, stride)]
    )


def between(value, source, target):
    return lax.ppermute(
        value, "pipe", [(2 * source + core, 2 * target + core) for core in range(2)]
    )


def tie(values, token):
    *values, _ = lax.optimization_barrier((*values, token))
    return values


def call(kernel, operands, places, outs, scratch=(), flops=0, moved=0):
    space = {"v": VMEM, "s": pltpu.SMEM, "h": pltpu.HBM}
    operands = [
        x if place == "s" else pltpu.with_memory_space_constraint(x, space[place])
        for x, place in zip(operands, places)
    ]
    return pl.pallas_call(
        kernel,
        in_specs=[pl.BlockSpec(memory_space=space[place]) for place in places],
        out_specs=[pl.BlockSpec(memory_space=VMEM) for _ in outs],
        out_shape=[VMEM(shape, dtype) for shape, dtype in outs],
        scratch_shapes=list(scratch),
        cost_estimate=pl.CostEstimate(flops=flops, bytes_accessed=moved, transcendentals=0),
        compiler_params=pltpu.CompilerParams(vmem_limit_bytes=16 * 2**20),
    )(*operands)


def picks(shape, q_dev, place):
    row = lax.broadcasted_iota(jnp.int32, shape, 0)
    query = lax.broadcasted_iota(jnp.int32, shape, 1)
    block = lax.axis_index("dp") ^ (row // (2 * q_dev))
    wanted = block * q_dev + row % q_dev
    found = (query == wanted) & ((row // q_dev) % 2 == place)
    return jnp.where(found, 1.0, 0.0)


def halves(shape, q_dev, place):
    row = lax.broadcasted_iota(jnp.int32, shape, 0)
    source = lax.broadcasted_iota(jnp.int32, shape, 1)
    return jnp.where(row == source + place * q_dev, 1.0, 0.0).astype(bf16)


def prime_kernel(cols, values, inputs, expand, kept, raised, own, wide, sems):
    step = expand.shape[1] // PARTS
    copies = []
    for part in range(PARTS):
        span = pl.ds(part * step, step)
        copy = pltpu.make_async_copy(expand.at[:, span], kept.at[:, span], sems.at[part])
        copy.start()
        copies.append(copy)
    rows = own.shape[0]
    q_dev = rows // 2
    laid = picks((raised.shape[0], cols.shape[0]), q_dev, 1).astype(bf16)
    laid = dot_nn(laid, cols[...]).astype(bf16)
    first = halves((rows, q_dev), q_dev, 0)
    second = halves((rows, q_dev), q_dev, 1)
    for part in range(PARTS):
        span = slice(part * step, (part + 1) * step)
        above = dot_nn(first, values[:, span])
        wide[:, span] = (above + dot_nn(second, inputs[:, span])).astype(bf16)
        copies[part].wait()
        found = adapter_scale * dot_nn(laid, kept[:, span])
        raised[:, span] = found.astype(bf16)
        own[:, span] = (found[:rows] + above).astype(bf16)


def keep_kernel(down, kept, sem):
    copy = pltpu.make_async_copy(down, kept, sem)
    copy.start()
    copy.wait()


def through_kernel(turn, arrived, before, down, expand, ranks, leaving):
    depth, width = down.shape
    step = 2 * width
    mine = lax.axis_index("pipe") % 2 == turn

    @pl.when(jnp.logical_not(mine))
    def _():
        ranks[...] = before[...]

    @pl.when(mine)
    def _():
        total = jnp.zeros(ranks.shape, f32)
        for at in range(0, depth, step):
            total += dot_nn(arrived[:, at : at + step], down[at : at + step, :])
        found = total.astype(bf16)
        ranks[...] = found
        for at in range(0, depth, step):
            more = adapter_scale * dot_nn(found, expand[:, at : at + step])
            leaving[:, at : at + step] = (arrived[:, at : at + step].astype(f32) + more).astype(bf16)


def last_kernel(arrived, before, down, ranks):
    depth, width = down.shape
    step = 2 * width
    mine = lax.axis_index("pipe") % 2 == 1

    @pl.when(jnp.logical_not(mine))
    def _():
        ranks[...] = before[...]

    @pl.when(mine)
    def _():
        total = jnp.zeros(ranks.shape, f32)
        for at in range(0, depth, step):
            total += dot_nn(arrived[:, at : at + step], down[at : at + step, :])
        ranks[...] = total.astype(bf16)


def lift_kernel(cotangent, expand, lifted, buffer, sems):
    copies = []
    for part in range(cotangent.shape[0] // SLOT):
        span = pl.ds(part * SLOT, SLOT)
        copy = pltpu.make_async_copy(cotangent.at[span], buffer.at[span], sems.at[part])
        copy.start()
        copies.append(copy)
    ranks = expand.shape[0]
    half = ranks // 2
    for pair in range(0, len(copies), 2):
        copies[pair].wait()
        copies[pair + 1].wait()
        span = slice(pair * SLOT, (pair + 2) * SLOT)
        for at in range(0, ranks, half):
            found = adapter_scale * dot_nt(buffer[span, :], expand[at : at + half, :])
            lifted[span, at : at + half] = found.astype(bf16)


def weave_kernel(q_dev, cols, down, rows, raised, left_rows, right_rows):
    count, depth = rows.shape
    step = depth // PARTS
    laid = picks((count, cols.shape[0]), q_dev, 0).astype(bf16)
    laid = dot_nn(laid, cols[...]).astype(bf16)
    place = lax.broadcasted_iota(jnp.int32, (count, step), 0) // q_dev
    first = place % 2 == 0
    for at in range(0, depth, step):
        span = slice(at, at + step)
        found = adapter_scale * dot_nt(laid, down[span, :])
        given = rows[:, span].astype(f32)
        left_rows[:, span] = jnp.where(first, found, given).astype(bf16)
        right_rows[:, span] = jnp.where(first, given, raised[:, span].astype(f32)).astype(bf16)


def summed(terms, shape):
    example = lax.broadcasted_iota(jnp.int32, (shape[0], terms.shape[1]), 0)
    position = lax.broadcasted_iota(jnp.int32, (shape[0], terms.shape[1]), 1)
    ones = jnp.where(position // SLOT == example, 1.0, 0.0)
    return dot_nt(ones, terms, lax.Precision.HIGHEST)


def weighed(weights, blocks, at, rows, lifted):
    ranks = jnp.concatenate([block[at : at + rows, :].astype(f32) for block in blocks])
    return weights.astype(f32) * dot_nt(ranks.astype(bf16), lifted[...])


def by_layer(own, other):
    upper = jnp.full(own.shape, lax.axis_index("pipe") % 2, jnp.int32) == 1
    own, other = own.astype(f32), other.astype(f32)
    return jnp.where(upper, other, own), jnp.where(upper, own, other)


def early_kernel(chips, rows, left, right, lifted, others, *refs):
    ups, blocks, sums = refs[:chips], refs[chips:-1], refs[-1]
    terms = left[...] * right[...]
    for slot in range(chips - 1):
        lower, upper = by_layer(ups[slot][...], others[slot])
        if slot == 0:
            terms += weighed(lower, blocks, 0, rows, lifted)
        else:
            at = rows * (2 * slot - 1)
            terms += weighed(lower, blocks, at, rows, lifted)
            terms += weighed(upper, blocks, at + rows, rows, lifted)
    sums[...] = summed(terms, sums.shape)


def late_kernel(chips, rows, own, others, lifted, *refs):
    parts, blocks, sums = refs[:chips], refs[chips:-1], refs[-1]
    lower, upper = by_layer(own[...], others[chips - 1])
    terms = weighed(lower, blocks, 0, rows, lifted)
    terms += weighed(upper, blocks, rows, rows, lifted)
    total = summed(terms, sums.shape)
    for part in parts:
        total += part[...]
    sums[...] = total


def final_kernel(chips, q_dev, queries, top_sums, *refs):
    received, scores = refs[:-1], refs[-1]
    total = received[0][...]
    for part in received[1:]:
        total += part[...]
    layer = jnp.full(total.shape, lax.axis_index("pipe"), jnp.int32)
    total = jnp.where(layer >= 2 * (chips - 1), top_sums[...], total)
    ex_dev, q_all = scores.shape
    shape = (total.shape[1], q_all)
    laid = picks(shape, q_dev, 0) + picks(shape, q_dev, 1)
    total = dot_nn(total, laid, lax.Precision.HIGHEST)[:ex_dev]
    example = lax.axis_index("dp") * ex_dev + lax.broadcasted_iota(jnp.int32, scores.shape, 0)
    keep = example != jnp.broadcast_to(queries[...], scores.shape)
    scores[...] = jnp.where(keep, total * SLOT ** (-0.5), 0.0)


def local(
    activations,
    cotangent,
    adapter_down,
    adapter_expand,
    value_rows,
    input_rows,
    hidden_cols,
    inner_cols,
    lengths,
    query_example,
):
    columns = lax.axis_size("dp")
    chips = lax.axis_size("pipe") // 2
    top = chips - 1
    tok_dev = activations.shape[1]
    ex_dev = tok_dev // SLOT
    q_dev = value_rows.shape[1]
    rows = 2 * q_dev
    count = columns * rows
    width, rank = adapter_down.shape[1:]
    weight_bytes = 2 * width * rank
    pass_flops = 2 * rows * width * rank

    offsets = lax.broadcasted_iota(jnp.int32, (ex_dev, SLOT), 1)
    live = (offsets < lengths[:, None]).astype(f32).reshape(1, tok_dev)

    def through(turn, arrived, before):
        return call(
            functools.partial(through_kernel, turn),
            (arrived, before, down, expand),
            "vvvv",
            [(before.shape, bf16), (arrived.shape, bf16)],
            flops=2 * pass_flops,
            moved=weight_bytes,
        )

    expand, raised, own, wide = call(
        prime_kernel,
        (inner_cols[0], value_rows[0], input_rows[0], adapter_expand[0]),
        "vvvh",
        [((rank, width), bf16), ((count, width), bf16), ((rows, width), bf16), ((rows, width), bf16)],
        [pltpu.SemaphoreType.DMA((PARTS,))],
        flops=pass_flops,
        moved=2 * weight_bytes,
    )

    arrived = upward(own, 0, 1, 2)
    (source,) = tie([adapter_down[0]], own)
    (down,) = call(
        keep_kernel,
        (source,),
        "h",
        [((width, rank), bf16)],
        [pltpu.SemaphoreType.DMA],
        moved=2 * weight_bytes,
    )
    arrived, down = lax.optimization_barrier((arrived, down))
    lower_ranks, leaving = through(1, arrived, jnp.zeros((rows, rank), bf16))
    moving = jnp.concatenate([leaving, own])

    arrived = upward(moving, 1, 1, 2)
    wide, cot = tie([wide, cotangent], moving)
    wide = spread(wide, "dp")
    (lifted,) = call(
        lift_kernel,
        (cot, expand),
        "hv",
        [((tok_dev, rank), bf16)],
        [VMEM((tok_dev, width), bf16), pltpu.SemaphoreType.DMA((ex_dev,))],
        flops=2 * tok_dev * width * rank,
        moved=2 * weight_bytes,
    )
    arrived, lifted = lax.optimization_barrier((arrived, lifted))

    slots = []
    empty = jnp.zeros((2 * rows, rank), bf16)
    for slot in range(1, chips):
        found, leaving = through(0, arrived, empty)
        arrived = upward(leaving, 0, 1, 2)
        if slot == 1:
            wide, hid = tie([jnp.concatenate(wide), hidden_cols[0]], leaving)
            left_rows, right_rows = call(
                functools.partial(weave_kernel, q_dev),
                (hid, down, wide, raised),
                "vvvv",
                [((count, width), bf16), ((count, width), bf16)],
                flops=2 * count * width * rank,
                moved=weight_bytes,
            )
            arrived, left_rows = lax.optimization_barrier((arrived, left_rows))
        if slot == 2 or top == 1:
            (cot,) = tie([cotangent], leaving)
            right = dot_nt(right_rows, cot)
            arrived, right = lax.optimization_barrier((arrived, right))
        if slot == top:
            break
        found, leaving = through(1, arrived, found)
        slots.append(found)
        arrived = upward(leaving, 1, 1, 2)
        if slot == 1:
            (act,) = tie([activations[0]], leaving)
            left = dot_nt(left_rows, act) * live
            left_own = left.astype(bf16)
            left_up = [left_own] + [upward(left_own, 0, 2 * hop, 1) for hop in range(1, chips)]
            arrived, left_own = lax.optimization_barrier((arrived, left_own))
        if slot == top - 1:
            early = jnp.concatenate([lower_ranks] + slots)
            early, *left_up = tie([early, *left_up], leaving)
            early = spread(early, "dp")
            others = swap(jnp.stack(left_up), "pipe", 1)
            (sums,) = call(
                functools.partial(early_kernel, chips, rows),
                (left, right, lifted, others, *left_up, *early),
                "v" * (4 + chips + columns),
                [((max(ex_dev, 8), count), f32)],
                flops=2 * count * rank * tok_dev * (2 * chips),
                moved=weight_bytes,
            )
            arrived, sums = lax.optimization_barrier((arrived, sums))

    parts = [sums] + [between(sums, chip, top) for chip in range(top)]
    (late,) = call(
        last_kernel,
        (arrived, found, down),
        "vvv",
        [((2 * rows, rank), bf16)],
        flops=pass_flops,
        moved=weight_bytes,
    )
    late, *parts = lax.optimization_barrier((late, *parts))
    late = spread(late, "dp")
    (sums,) = call(
        functools.partial(late_kernel, chips, rows),
        (left_up[-1], others, lifted, *parts, *late),
        "v" * (3 + chips + columns),
        [(sums.shape, f32)],
        flops=2 * count * rank * tok_dev * 2,
        moved=weight_bytes // 8,
    )
    sums = sums + lax.ppermute(
        sums, "pipe", [(2 * top, 2 * top + 1), (2 * top + 1, 2 * top)]
    )
    received = [between(sums, top, chip) for chip in range(top)]
    (scores,) = call(
        functools.partial(final_kernel, chips, q_dev),
        (query_example[None], sums, *received),
        "v" * (2 + top),
        [((ex_dev, columns * q_dev), f32)],
    )
    return scores


def solution(mesh):
    in_specs = (
        P("pipe", "dp", None),
        P("dp", None),
        P("pipe", None, None),
        P("pipe", None, None),
        P("pipe", "dp", None),
        P("pipe", "dp", None),
        P("pipe", None, None),
        P("pipe", None, None),
        P("dp"),
        P(),
    )
    out_specs = P("dp", None)
    return jax.shard_map(local, mesh=mesh, in_specs=in_specs, out_specs=out_specs, check_vma=False)
```

```python
import functools

import jax
import jax.numpy as jnp
from jax import lax
from jax.experimental import pallas as pl
from jax.experimental.pallas import tpu as pltpu
from jax.sharding import PartitionSpec as P

SLOT = 128
PARTS = 8


adapter_scale = 0.25
bf16 = jnp.bfloat16
f32 = jnp.float32
VMEM = pltpu.VMEM


def dot_nn(a, b, precision=None):
    return lax.dot_general(
        a, b, (((1,), (0,)), ((), ())), preferred_element_type=f32, precision=precision
    )


def dot_nt(a, b, precision=None):
    return lax.dot_general(
        a, b, (((1,), (1,)), ((), ())), preferred_element_type=f32, precision=precision
    )


def swap(value, axis, distance):
    count = lax.axis_size(axis)
    return lax.ppermute(value, axis, [(source, source ^ distance) for source in range(count)])


def spread(value, axis):
    return [value] + [swap(value, axis, d) for d in range(1, lax.axis_size(axis))]


def upward(value, first, hop, stride):
    count = lax.axis_size("pipe")
    return lax.ppermute(
        value, "pipe", [(source, source + hop) for source in range(first, count - hop, stride)]
    )


def around(value, hop):
    count = lax.axis_size("pipe")
    return lax.ppermute(
        value, "pipe", [(source, (source + 2 * hop) % count) for source in range(count)]
    )


def tie(values, token):
    *values, _ = lax.optimization_barrier((*values, token))
    return values


def call(kernel, operands, places, outs, scratch=(), flops=0, moved=0):
    space = {"v": VMEM, "s": pltpu.SMEM, "h": pltpu.HBM}
    operands = [
        x if place == "s" else pltpu.with_memory_space_constraint(x, space[place])
        for x, place in zip(operands, places)
    ]
    return pl.pallas_call(
        kernel,
        in_specs=[pl.BlockSpec(memory_space=space[place]) for place in places],
        out_specs=[pl.BlockSpec(memory_space=VMEM) for _ in outs],
        out_shape=[VMEM(shape, dtype) for shape, dtype in outs],
        scratch_shapes=list(scratch),
        cost_estimate=pl.CostEstimate(flops=flops, bytes_accessed=moved, transcendentals=0),
        compiler_params=pltpu.CompilerParams(vmem_limit_bytes=16 * 2**20),
    )(*operands)


def picks(shape, q_dev, place):
    row = lax.broadcasted_iota(jnp.int32, shape, 0)
    query = lax.broadcasted_iota(jnp.int32, shape, 1)
    block = lax.axis_index("dp") ^ (row // (2 * q_dev))
    wanted = block * q_dev + row % q_dev
    found = (query == wanted) & ((row // q_dev) % 2 == place)
    return jnp.where(found, 1.0, 0.0)


def halves(shape, q_dev, place):
    row = lax.broadcasted_iota(jnp.int32, shape, 0)
    source = lax.broadcasted_iota(jnp.int32, shape, 1)
    return jnp.where(row == source + place * q_dev, 1.0, 0.0).astype(bf16)


def fetch(pairs, sems):
    copies = [
        pltpu.make_async_copy(source, target, sems.at[at])
        for at, (source, target) in enumerate(pairs)
    ]
    for copy in copies:
        copy.start()
    return copies


def prime_kernel(
    cols_hbm, values_hbm, inputs_hbm, expand, kept, raised, own, wide, cols, values, inputs, few, sems
):
    step = expand.shape[1] // PARTS
    small = fetch([(cols_hbm, cols), (values_hbm, values), (inputs_hbm, inputs)], few)
    spans = [pl.ds(part * step, step) for part in range(PARTS)]
    copies = fetch([(expand.at[:, span], kept.at[:, span]) for span in spans], sems)
    rows = own.shape[0]
    q_dev = rows // 2
    first = halves((rows, q_dev), q_dev, 0)
    second = halves((rows, q_dev), q_dev, 1)
    laid = picks((raised.shape[0], cols.shape[0]), q_dev, 1).astype(bf16)
    for copy in small:
        copy.wait()
    laid = dot_nn(laid, cols[...]).astype(bf16)
    for part in range(PARTS):
        span = slice(part * step, (part + 1) * step)
        above = dot_nn(first, values[:, span])
        wide[:, span] = (above + dot_nn(second, inputs[:, span])).astype(bf16)
        copies[part].wait()
        found = adapter_scale * dot_nn(laid, kept[:, span])
        raised[:, span] = found.astype(bf16)
        own[:, span] = (found[:rows] + above).astype(bf16)


def keep_kernel(q_dev, cols_hbm, down, kept, raised, cols, few, sems):
    step = down.shape[0] // PARTS
    small = fetch([(cols_hbm, cols)], few)
    spans = [pl.ds(part * step, step) for part in range(PARTS)]
    copies = fetch([(down.at[span], kept.at[span]) for span in spans], sems)
    laid = picks((raised.shape[0], cols.shape[0]), q_dev, 0).astype(bf16)
    small[0].wait()
    laid = dot_nn(laid, cols[...]).astype(bf16)
    for part in range(PARTS):
        span = slice(part * step, (part + 1) * step)
        copies[part].wait()
        raised[:, span] = (adapter_scale * dot_nt(laid, kept[span, :])).astype(bf16)


def through_kernel(turn, arrived, before, down, expand, ranks, leaving):
    depth, width = down.shape
    step = 2 * width
    mine = lax.axis_index("pipe") % 2 == turn

    @pl.when(jnp.logical_not(mine))
    def _():
        ranks[...] = before[...]

    @pl.when(mine)
    def _():
        total = jnp.zeros(ranks.shape, f32)
        for at in range(0, depth, step):
            total += dot_nn(arrived[:, at : at + step], down[at : at + step, :])
        found = total.astype(bf16)
        ranks[...] = found
        for at in range(0, depth, step):
            more = adapter_scale * dot_nn(found, expand[:, at : at + step])
            leaving[:, at : at + step] = (arrived[:, at : at + step].astype(f32) + more).astype(bf16)


def last_kernel(arrived, before, down, ranks):
    depth, width = down.shape
    step = 2 * width
    mine = lax.axis_index("pipe") % 2 == 1

    @pl.when(jnp.logical_not(mine))
    def _():
        ranks[...] = before[...]

    @pl.when(mine)
    def _():
        total = jnp.zeros(ranks.shape, f32)
        for at in range(0, depth, step):
            total += dot_nn(arrived[:, at : at + step], down[at : at + step, :])
        ranks[...] = total.astype(bf16)


def lift_kernel(start, cotangent, expand, lifted, buffer, total, sems):
    count, depth = buffer.shape
    parts = PARTS // 2
    step = depth // parts
    spans = [pl.ds(part * step, step) for part in range(parts)]
    rows = pl.ds(start, count)
    copies = fetch([(cotangent.at[rows, span], buffer.at[:, span]) for span in spans], sems)
    for part in range(parts):
        span = slice(part * step, (part + 1) * step)
        copies[part].wait()
        found = dot_nt(buffer[:, span], expand[:, span])
        if part == 0:
            total[...] = found
        elif part < parts - 1:
            total[...] += found
        else:
            lifted[...] = (adapter_scale * (total[...] + found)).astype(bf16)


def weave_kernel(q_dev, hidden, rows, raised, left_rows, right_rows):
    count, depth = rows.shape
    step = depth // PARTS
    place = lax.broadcasted_iota(jnp.int32, (count, step), 0) // q_dev
    first = place % 2 == 0
    for at in range(0, depth, step):
        span = slice(at, at + step)
        given = rows[:, span].astype(f32)
        left_rows[:, span] = jnp.where(first, hidden[:, span].astype(f32), given).astype(bf16)
        right_rows[:, span] = jnp.where(first, given, raised[:, span].astype(f32)).astype(bf16)


def summed(terms, shape):
    example = lax.broadcasted_iota(jnp.int32, (shape[0], terms.shape[1]), 0)
    position = lax.broadcasted_iota(jnp.int32, (shape[0], terms.shape[1]), 1)
    ones = jnp.where(position // SLOT == example, 1.0, 0.0)
    return dot_nt(ones, terms, lax.Precision.HIGHEST)


def weighed(weights, blocks, at, rows, lifted):
    ranks = jnp.concatenate([block[at : at + rows, :].astype(f32) for block in blocks])
    ranks = ranks.astype(bf16)
    return weights * jnp.concatenate([dot_nt(ranks, part[...]) for part in lifted], axis=1)


def by_layer(own, other):
    upper = jnp.full(own.shape, lax.axis_index("pipe") % 2, jnp.int32) == 1
    own, other = own.astype(f32), other.astype(f32)
    return jnp.where(upper, other, own), jnp.where(upper, own, other)


def early_kernel(chips, rows, left, right, others, *refs):
    lifted, ups, blocks, sums = refs[:2], refs[2 : 2 + chips], refs[2 + chips : -1], refs[-1]
    terms = left[...] * right[...]
    for slot in range(chips - 1):
        lower, upper = by_layer(ups[slot][...], others[slot])
        if slot == 0:
            terms += weighed(lower, blocks, 0, rows, lifted)
        else:
            at = rows * (2 * slot - 1)
            terms += weighed(lower, blocks, at, rows, lifted)
            terms += weighed(upper, blocks, at + rows, rows, lifted)
    sums[...] = summed(terms, sums.shape)


def late_kernel(chips, rows, own, others, early, *refs):
    lifted, blocks, sums = refs[:2], refs[2:-1], refs[-1]
    lower, upper = by_layer(own[...], others[chips - 1])
    terms = weighed(lower, blocks, 0, rows, lifted)
    terms += weighed(upper, blocks, rows, rows, lifted)
    sums[...] = early[...] + summed(terms, sums.shape)


def final_kernel(q_dev, queries, *refs):
    parts, scores = refs[:-1], refs[-1]
    total = parts[0][...]
    for part in parts[1:]:
        total += part[...]
    ex_dev, q_all = scores.shape
    shape = (total.shape[1], q_all)
    laid = picks(shape, q_dev, 0) + picks(shape, q_dev, 1)
    total = dot_nn(total, laid, lax.Precision.HIGHEST)[:ex_dev]
    example = lax.axis_index("dp") * ex_dev + lax.broadcasted_iota(jnp.int32, scores.shape, 0)
    keep = example != jnp.broadcast_to(queries[...], scores.shape)
    scores[...] = jnp.where(keep, total * SLOT ** (-0.5), 0.0)


def local(
    activations,
    cotangent,
    adapter_down,
    adapter_expand,
    value_rows,
    input_rows,
    hidden_cols,
    inner_cols,
    lengths,
    query_example,
):
    columns = lax.axis_size("dp")
    chips = lax.axis_size("pipe") // 2
    top = chips - 1
    tok_dev = activations.shape[1]
    ex_dev = tok_dev // SLOT
    q_dev = value_rows.shape[1]
    rows = 2 * q_dev
    count = columns * rows
    width, rank = adapter_down.shape[1:]
    weight_bytes = 2 * width * rank
    pass_flops = 2 * rows * width * rank

    offsets = lax.broadcasted_iota(jnp.int32, (ex_dev, SLOT), 1)
    live = (offsets < lengths[:, None]).astype(f32).reshape(1, tok_dev)

    def through(turn, arrived, before):
        return call(
            functools.partial(through_kernel, turn),
            (arrived, before, down, expand),
            "vvvv",
            [(before.shape, bf16), (arrived.shape, bf16)],
            flops=2 * pass_flops,
            moved=weight_bytes,
        )

    expand, raised, own, wide = call(
        prime_kernel,
        (inner_cols[0], value_rows[0], input_rows[0], adapter_expand[0]),
        "hhhh",
        [((rank, width), bf16), ((count, width), bf16), ((rows, width), bf16), ((rows, width), bf16)],
        [
            VMEM(inner_cols.shape[1:], bf16),
            VMEM((q_dev, width), bf16),
            VMEM((q_dev, width), bf16),
            pltpu.SemaphoreType.DMA((3,)),
            pltpu.SemaphoreType.DMA((PARTS,)),
        ],
        flops=pass_flops,
        moved=2 * weight_bytes,
    )

    arrived = upward(own, 0, 1, 2)
    hid, source = tie([hidden_cols[0], adapter_down[0]], own)
    down, hidden = call(
        functools.partial(keep_kernel, q_dev),
        (hid, source),
        "hh",
        [((width, rank), bf16), ((count, width), bf16)],
        [
            VMEM(hidden_cols.shape[1:], bf16),
            pltpu.SemaphoreType.DMA((1,)),
            pltpu.SemaphoreType.DMA((PARTS,)),
        ],
        flops=2 * count * width * rank,
        moved=2 * weight_bytes,
    )
    arrived, down = lax.optimization_barrier((arrived, down))
    lower_ranks, leaving = through(1, arrived, jnp.zeros((rows, rank), bf16))
    moving = jnp.concatenate([leaving, own])

    half = tok_dev // 2

    def lift(part, token):
        (cot,) = tie([cotangent], token)
        return call(
            functools.partial(lift_kernel, part * half),
            (cot, expand),
            "hv",
            [((half, rank), bf16)],
            [
                VMEM((half, width), bf16),
                VMEM((half, rank), f32),
                pltpu.SemaphoreType.DMA((PARTS // 2,)),
            ],
            flops=2 * half * width * rank,
            moved=weight_bytes,
        )[0]

    arrived = upward(moving, 1, 1, 2)
    (wide,) = tie([wide], moving)
    wide = spread(wide, "dp")
    lifted = [lift(0, moving)]
    arrived, lifted[0] = lax.optimization_barrier((arrived, lifted[0]))

    slots = []
    empty = jnp.zeros((2 * rows, rank), bf16)
    for slot in range(1, chips):
        found, leaving = through(0, arrived, empty)
        arrived = upward(leaving, 0, 1, 2)
        if slot == 1:
            lifted.append(lift(1, leaving))
            arrived, lifted[1] = lax.optimization_barrier((arrived, lifted[1]))
        if slot == 2:
            (cot,) = tie([cotangent], leaving)
            right = dot_nt(right_rows, cot)
            arrived, right, *left_up = lax.optimization_barrier((arrived, right, *left_up))
        if slot == top:
            (sums,) = call(
                functools.partial(early_kernel, chips, rows),
                (left, right, others, *lifted, *left_up, *early),
                "v" * (5 + chips + columns),
                [((max(ex_dev, 8), count), f32)],
                flops=2 * count * rank * tok_dev * (2 * chips),
                moved=weight_bytes,
            )
            arrived, sums = lax.optimization_barrier((arrived, sums))
            break
        found, leaving = through(1, arrived, found)
        slots.append(found)
        arrived = upward(leaving, 1, 1, 2)
        if slot == 1:
            wide = jnp.concatenate(tie(wide, leaving))
            left_rows, right_rows = call(
                functools.partial(weave_kernel, q_dev),
                (hidden, wide, raised),
                "vvv",
                [((count, width), bf16), ((count, width), bf16)],
                flops=2 * count * width,
                moved=weight_bytes // 2,
            )
            left = dot_nt(left_rows, activations[0]) * live
            left_own = left.astype(bf16)
            left_up = [left_own] + [upward(left_own, 0, 2 * hop, 1) for hop in range(1, chips)]
            arrived, left_own = lax.optimization_barrier((arrived, left_own))
        if slot == top - 1:
            early = jnp.concatenate([lower_ranks] + slots)
            early, *left_up = tie([early, *left_up], leaving)
            early = spread(early, "dp")
            others = swap(jnp.stack(left_up), "pipe", 1)
            arrived, others, *early = lax.optimization_barrier((arrived, others, *early))

    (late,) = call(
        last_kernel,
        (arrived, found, down),
        "vvv",
        [((2 * rows, rank), bf16)],
        flops=pass_flops,
        moved=weight_bytes,
    )
    late = spread(late, "dp")
    (sums,) = call(
        functools.partial(late_kernel, chips, rows),
        (left_up[-1], others, sums, *lifted, *late),
        "v" * (5 + columns),
        [(sums.shape, f32)],
        flops=2 * count * rank * tok_dev * 2,
        moved=weight_bytes // 8,
    )
    sums = sums + swap(sums, "pipe", 1)
    parts = [sums] + [around(sums, hop) for hop in range(1, chips)]
    (scores,) = call(
        functools.partial(final_kernel, q_dev),
        (query_example[None], *parts),
        "v" * (1 + chips),
        [((ex_dev, columns * q_dev), f32)],
    )
    return scores


def solution(mesh):
    in_specs = (
        P("pipe", "dp", None),
        P("dp", None),
        P("pipe", None, None),
        P("pipe", None, None),
        P("pipe", "dp", None),
        P("pipe", "dp", None),
        P("pipe", None, None),
        P("pipe", None, None),
        P("dp"),
        P(),
    )
    out_specs = P("dp", None)
    return jax.shard_map(local, mesh=mesh, in_specs=in_specs, out_specs=out_specs, check_vma=False)
```

```python
import functools

import jax
import jax.numpy as jnp
from jax import lax
from jax.experimental import pallas as pl
from jax.experimental.pallas import tpu as pltpu
from jax.sharding import PartitionSpec as P

SLOT = 128
PARTS = 16
AHEAD = 6


adapter_scale = 0.25
bf16 = jnp.bfloat16
f32 = jnp.float32
VMEM = pltpu.VMEM


def dot_nn(a, b, precision=None):
    return lax.dot_general(
        a, b, (((1,), (0,)), ((), ())), preferred_element_type=f32, precision=precision
    )


def dot_nt(a, b, precision=None):
    return lax.dot_general(
        a, b, (((1,), (1,)), ((), ())), preferred_element_type=f32, precision=precision
    )


def swap(value, axis, distance):
    count = lax.axis_size(axis)
    return lax.ppermute(value, axis, [(source, source ^ distance) for source in range(count)])


def spread(value, axis):
    return [value] + [swap(value, axis, d) for d in range(1, lax.axis_size(axis))]


def upward(value, first, hop, stride):
    count = lax.axis_size("pipe")
    return lax.ppermute(
        value, "pipe", [(source, source + hop) for source in range(first, count - hop, stride)]
    )


def around(value, hop):
    count = lax.axis_size("pipe")
    return lax.ppermute(
        value, "pipe", [(source, (source + 2 * hop) % count) for source in range(count)]
    )


def tie(values, token):
    *values, _ = lax.optimization_barrier((*values, token))
    return values


def call(kernel, operands, places, outs, scratch=(), flops=0, moved=0, kept=VMEM):
    space = {"v": VMEM, "s": pltpu.SMEM, "h": pltpu.HBM}
    operands = [
        x if place == "s" else pltpu.with_memory_space_constraint(x, space[place])
        for x, place in zip(operands, places)
    ]
    return pl.pallas_call(
        kernel,
        in_specs=[pl.BlockSpec(memory_space=space[place]) for place in places],
        out_specs=[pl.BlockSpec(memory_space=VMEM) for _ in outs],
        out_shape=[kept(shape, dtype) for shape, dtype in outs],
        scratch_shapes=list(scratch),
        cost_estimate=pl.CostEstimate(flops=flops, bytes_accessed=moved, transcendentals=0),
        compiler_params=pltpu.CompilerParams(vmem_limit_bytes=16 * 2**20),
    )(*operands)


def picks(shape, q_dev, place):
    row = lax.broadcasted_iota(jnp.int32, shape, 0)
    query = lax.broadcasted_iota(jnp.int32, shape, 1)
    block = lax.axis_index("dp") ^ (row // (2 * q_dev))
    wanted = block * q_dev + row % q_dev
    found = (query == wanted) & ((row // q_dev) % 2 == place)
    return jnp.where(found, 1.0, 0.0)


def fetch(pairs, sems):
    return [
        pltpu.make_async_copy(source, target, sems.at[at])
        for at, (source, target) in enumerate(pairs)
    ]


def begin(copies):
    for copy in copies[:AHEAD]:
        copy.start()


def arrive(copies, part):
    copies[part].wait()
    if part + AHEAD < len(copies):
        copies[part + AHEAD].start()


def prime_kernel(
    cols_hbm, values_hbm, expand, kept, raised, own, cols, values, few, sems
):
    step = expand.shape[1] // PARTS
    small = fetch([(cols_hbm, cols), (values_hbm, values)], few)
    begin(small)
    spans = [pl.ds(part * step, step) for part in range(PARTS)]
    copies = fetch([(expand.at[:, span], kept.at[:, span]) for span in spans], sems)
    begin(copies)
    rows = own.shape[0]
    q_dev = rows // 2
    laid = picks((raised.shape[0], cols.shape[0]), q_dev, 1).astype(bf16)
    for copy in small:
        copy.wait()
    laid = dot_nn(laid, cols[...]).astype(bf16)
    for part in range(PARTS):
        span = slice(part * step, (part + 1) * step)
        arrive(copies, part)
        found = adapter_scale * dot_nn(laid, kept[:, span])
        raised[:, span] = found.astype(bf16)
        above = jnp.concatenate([values[:, span].astype(f32), found[q_dev:rows]])
        own[:, span] = above.astype(bf16)


def keep_kernel(q_dev, cols_hbm, down, kept, raised, cols, few, sems):
    step = down.shape[0] // PARTS
    small = fetch([(cols_hbm, cols)], few)
    begin(small)
    spans = [pl.ds(part * step, step) for part in range(PARTS)]
    copies = fetch([(down.at[span], kept.at[span]) for span in spans], sems)
    begin(copies)
    laid = picks((raised.shape[0], cols.shape[0]), q_dev, 0).astype(bf16)
    small[0].wait()
    laid = dot_nn(laid, cols[...]).astype(bf16)
    for part in range(PARTS):
        span = slice(part * step, (part + 1) * step)
        arrive(copies, part)
        raised[:, span] = (adapter_scale * dot_nt(laid, kept[span, :])).astype(bf16)


def through_kernel(turn, arrived, before, down, expand, ranks, leaving):
    depth, width = down.shape
    step = 2 * width
    mine = lax.axis_index("pipe") % 2 == turn

    @pl.when(jnp.logical_not(mine))
    def _():
        ranks[...] = before[...]

    @pl.when(mine)
    def _():
        total = jnp.zeros(ranks.shape, f32)
        for at in range(0, depth, step):
            total += dot_nn(arrived[:, at : at + step], down[at : at + step, :])
        found = total.astype(bf16)
        ranks[...] = found
        for at in range(0, depth, step):
            more = adapter_scale * dot_nn(found, expand[:, at : at + step])
            leaving[:, at : at + step] = (arrived[:, at : at + step].astype(f32) + more).astype(bf16)


def last_kernel(arrived, before, down, ranks):
    depth, width = down.shape
    step = 2 * width
    mine = lax.axis_index("pipe") % 2 == 1

    @pl.when(jnp.logical_not(mine))
    def _():
        ranks[...] = before[...]

    @pl.when(mine)
    def _():
        total = jnp.zeros(ranks.shape, f32)
        for at in range(0, depth, step):
            total += dot_nn(arrived[:, at : at + step], down[at : at + step, :])
        ranks[...] = total.astype(bf16)


def lift_kernel(start, cotangent, expand, lifted, buffer, total, sems):
    count, depth = buffer.shape
    parts = PARTS // 2
    step = depth // parts
    spans = [pl.ds(part * step, step) for part in range(parts)]
    rows = pl.ds(start, count)
    copies = fetch([(cotangent.at[rows, span], buffer.at[:, span]) for span in spans], sems)
    begin(copies)
    for part in range(parts):
        span = slice(part * step, (part + 1) * step)
        arrive(copies, part)
        found = dot_nt(buffer[:, span], expand[:, span])
        if part == 0:
            total[...] = found
        elif part < parts - 1:
            total[...] += found
        else:
            lifted[...] = (adapter_scale * (total[...] + found)).astype(bf16)


def weave_kernel(q_dev, hidden, rows, raised, left_rows, right_rows):
    count, depth = rows.shape
    step = depth // PARTS
    place = lax.broadcasted_iota(jnp.int32, (count, step), 0) // q_dev
    first = place % 2 == 0
    for at in range(0, depth, step):
        span = slice(at, at + step)
        given = rows[:, span].astype(f32)
        left_rows[:, span] = jnp.where(first, hidden[:, span].astype(f32), given).astype(bf16)
        right_rows[:, span] = jnp.where(first, given, raised[:, span].astype(f32)).astype(bf16)


def summed(terms, shape):
    example = lax.broadcasted_iota(jnp.int32, (shape[0], terms.shape[1]), 0)
    position = lax.broadcasted_iota(jnp.int32, (shape[0], terms.shape[1]), 1)
    ones = jnp.where(position // SLOT == example, 1.0, 0.0)
    return dot_nt(ones, terms, lax.Precision.HIGHEST)


def weighed(weights, blocks, at, rows, lifted):
    ranks = jnp.concatenate([block[at : at + rows, :].astype(f32) for block in blocks])
    ranks = ranks.astype(bf16)
    return weights * jnp.concatenate([dot_nt(ranks, part[...]) for part in lifted], axis=1)


def by_layer(own, other):
    upper = jnp.full(own.shape, lax.axis_index("pipe") % 2, jnp.int32) == 1
    own, other = own.astype(f32), other.astype(f32)
    return jnp.where(upper, other, own), jnp.where(upper, own, other)


def early_kernel(chips, rows, left, right, others, *refs):
    lifted, ups, blocks, sums = refs[:2], refs[2 : 2 + chips], refs[2 + chips : -1], refs[-1]
    terms = left[...] * right[...]
    for slot in range(chips - 1):
        lower, upper = by_layer(ups[slot][...], others[slot])
        if slot == 0:
            terms += weighed(lower, blocks, 0, rows, lifted)
        else:
            at = rows * (2 * slot - 1)
            terms += weighed(lower, blocks, at, rows, lifted)
            terms += weighed(upper, blocks, at + rows, rows, lifted)
    sums[...] = summed(terms, sums.shape)


def late_kernel(chips, rows, own, others, early, *refs):
    lifted, blocks, sums = refs[:2], refs[2:-1], refs[-1]
    lower, upper = by_layer(own[...], others[chips - 1])
    terms = weighed(lower, blocks, 0, rows, lifted)
    terms += weighed(upper, blocks, rows, rows, lifted)
    sums[...] = early[...] + summed(terms, sums.shape)


def final_kernel(q_dev, queries, *refs):
    parts, scores = refs[:-1], refs[-1]
    total = parts[0][...]
    for part in parts[1:]:
        total += part[...]
    ex_dev, q_all = scores.shape
    shape = (total.shape[1], q_all)
    laid = picks(shape, q_dev, 0) + picks(shape, q_dev, 1)
    total = dot_nn(total, laid, lax.Precision.HIGHEST)[:ex_dev]
    example = lax.axis_index("dp") * ex_dev + lax.broadcasted_iota(jnp.int32, scores.shape, 0)
    keep = example != jnp.broadcast_to(queries[...], scores.shape)
    scores[...] = jnp.where(keep, total * SLOT ** (-0.5), 0.0)


def local(
    activations,
    cotangent,
    adapter_down,
    adapter_expand,
    value_rows,
    input_rows,
    hidden_cols,
    inner_cols,
    lengths,
    query_example,
):
    columns = lax.axis_size("dp")
    chips = lax.axis_size("pipe") // 2
    top = chips - 1
    tok_dev = activations.shape[1]
    ex_dev = tok_dev // SLOT
    q_dev = value_rows.shape[1]
    rows = 2 * q_dev
    count = columns * rows
    width, rank = adapter_down.shape[1:]
    weight_bytes = 2 * width * rank
    pass_flops = 2 * rows * width * rank

    offsets = lax.broadcasted_iota(jnp.int32, (ex_dev, SLOT), 1)
    live = (offsets < lengths[:, None]).astype(f32).reshape(1, tok_dev)

    def through(turn, arrived, before):
        return call(
            functools.partial(through_kernel, turn),
            (arrived, before, down, expand),
            "vvvv",
            [(before.shape, bf16), (arrived.shape, bf16)],
            flops=2 * pass_flops,
            moved=weight_bytes,
        )

    expand, raised, own = call(
        prime_kernel,
        (inner_cols[0], value_rows[0], adapter_expand[0]),
        "hhh",
        [((rank, width), bf16), ((count, width), bf16), ((rows, width), bf16)],
        [
            VMEM(inner_cols.shape[1:], bf16),
            VMEM((q_dev, width), bf16),
            pltpu.SemaphoreType.DMA((2,)),
            pltpu.SemaphoreType.DMA((PARTS,)),
        ],
        flops=pass_flops,
        moved=2 * weight_bytes,
    )

    arrived = upward(own, 0, 1, 2)
    hid, source = tie([hidden_cols[0], adapter_down[0]], own)
    down, hidden = call(
        functools.partial(keep_kernel, q_dev),
        (hid, source),
        "hh",
        [((width, rank), bf16), ((count, width), bf16)],
        [
            VMEM(hidden_cols.shape[1:], bf16),
            pltpu.SemaphoreType.DMA((1,)),
            pltpu.SemaphoreType.DMA((PARTS,)),
        ],
        flops=2 * count * width * rank,
        moved=2 * weight_bytes,
    )
    arrived, down = lax.optimization_barrier((arrived, down))
    lower_ranks, leaving = through(1, arrived, jnp.zeros((rows, rank), bf16))
    moving = jnp.concatenate([leaving, own])

    half = tok_dev // 2

    def lift(part, token):
        (cot,) = tie([cotangent], token)
        return call(
            functools.partial(lift_kernel, part * half),
            (cot, expand),
            "hv",
            [((half, rank), bf16)],
            [
                VMEM((half, width), bf16),
                VMEM((half, rank), f32),
                pltpu.SemaphoreType.DMA((PARTS // 2,)),
            ],
            flops=2 * half * width * rank,
            moved=weight_bytes,
        )[0]

    arrived = upward(moving, 1, 1, 2)
    wide = tie([value_rows[0], input_rows[0]], moving)
    wide = spread(jnp.concatenate(wide), "dp")
    lifted = [lift(0, moving)]
    arrived, lifted[0] = lax.optimization_barrier((arrived, lifted[0]))

    slots = []
    empty = jnp.zeros((2 * rows, rank), bf16)
    for slot in range(1, chips):
        found, leaving = through(0, arrived, empty)
        arrived = upward(leaving, 0, 1, 2)
        if slot == 1:
            lifted.append(lift(1, leaving))
            wide = jnp.concatenate(tie(wide, lifted[1]))
            arrived, wide = lax.optimization_barrier((arrived, wide))
        if slot == 2:
            (cot,) = tie([cotangent], leaving)
            right = dot_nt(right_rows, cot)
            arrived, right, *left_up = lax.optimization_barrier((arrived, right, *left_up))
        if slot == top:
            (sums,) = call(
                functools.partial(early_kernel, chips, rows),
                (left, right, others, *lifted, *left_up, *early),
                "v" * (5 + chips + columns),
                [((max(ex_dev, 8), count), f32)],
                flops=2 * count * rank * tok_dev * (2 * chips),
                moved=weight_bytes,
            )
            arrived, sums = lax.optimization_barrier((arrived, sums))
            break
        found, leaving = through(1, arrived, found)
        slots.append(found)
        arrived = upward(leaving, 1, 1, 2)
        if slot == 1:
            left_rows, right_rows = call(
                functools.partial(weave_kernel, q_dev),
                (hidden, wide, raised),
                "vvv",
                [((count, width), bf16), ((count, width), bf16)],
                flops=2 * count * width,
                moved=weight_bytes // 2,
            )
            left = dot_nt(left_rows, activations[0]) * live
            left_own = left.astype(bf16)
            left_up = [left_own] + [upward(left_own, 0, 2 * hop, 1) for hop in range(1, chips)]
            arrived, left_own = lax.optimization_barrier((arrived, left_own))
        if slot == top - 1:
            (early,) = tie([jnp.concatenate([lower_ranks] + slots)], leaving)
            early = spread(early, "dp")
            arrived, *early = lax.optimization_barrier((arrived, *early))
            others = swap(jnp.stack(tie(left_up, early[-1])), "pipe", 1)

    (late,) = call(
        last_kernel,
        (arrived, found, down),
        "vvv",
        [((2 * rows, rank), bf16)],
        flops=pass_flops,
        moved=weight_bytes,
    )
    late = spread(late, "dp")
    (sums,) = call(
        functools.partial(late_kernel, chips, rows),
        (left_up[-1], others, sums, *lifted, *late),
        "v" * (5 + columns),
        [(sums.shape, f32)],
        flops=2 * count * rank * tok_dev * 2,
        moved=weight_bytes // 8,
    )
    sums = sums + swap(sums, "pipe", 1)
    parts = [sums] + [around(sums, hop) for hop in range(1, chips)]
    (scores,) = call(
        functools.partial(final_kernel, q_dev),
        (query_example[None], *parts),
        "v" * (1 + chips),
        [((ex_dev, columns * q_dev), f32)],
        kept=jax.ShapeDtypeStruct,
    )
    return scores


def solution(mesh):
    in_specs = (
        P("pipe", "dp", None),
        P("dp", None),
        P("pipe", None, None),
        P("pipe", None, None),
        P("pipe", "dp", None),
        P("pipe", "dp", None),
        P("pipe", None, None),
        P("pipe", None, None),
        P("dp"),
        P(),
    )
    out_specs = P("dp", None)
    return jax.shard_map(local, mesh=mesh, in_specs=in_specs, out_specs=out_specs, check_vma=False)
```

```python
import functools

import jax
import jax.numpy as jnp
from jax import lax
from jax.experimental import pallas as pl
from jax.experimental.pallas import tpu as pltpu
from jax.sharding import PartitionSpec as P

SLOT = 128
PARTS = 4
AHEAD = 2


adapter_scale = 0.25
bf16 = jnp.bfloat16
f32 = jnp.float32
VMEM = pltpu.VMEM


def dot_nn(a, b, precision=None):
    return lax.dot_general(
        a, b, (((1,), (0,)), ((), ())), preferred_element_type=f32, precision=precision
    )


def dot_nt(a, b, precision=None):
    return lax.dot_general(
        a, b, (((1,), (1,)), ((), ())), preferred_element_type=f32, precision=precision
    )


def swap(value, axis, distance):
    count = lax.axis_size(axis)
    return lax.ppermute(value, axis, [(source, source ^ distance) for source in range(count)])


def spread(value, axis):
    return [value] + [swap(value, axis, d) for d in range(1, lax.axis_size(axis))]


def upward(value, first, hop, stride):
    count = lax.axis_size("pipe")
    return lax.ppermute(
        value, "pipe", [(source, source + hop) for source in range(first, count - hop, stride)]
    )


def around(value, hop):
    count = lax.axis_size("pipe")
    return lax.ppermute(
        value, "pipe", [(source, (source + 2 * hop) % count) for source in range(count)]
    )


def tie(values, token):
    *values, _ = lax.optimization_barrier((*values, token))
    return values


def call(kernel, operands, places, outs, scratch=(), flops=0, moved=0, kept=VMEM):
    space = {"v": VMEM, "s": pltpu.SMEM, "h": pltpu.HBM}
    operands = [
        x if place == "s" else pltpu.with_memory_space_constraint(x, space[place])
        for x, place in zip(operands, places)
    ]
    return pl.pallas_call(
        kernel,
        in_specs=[pl.BlockSpec(memory_space=space[place]) for place in places],
        out_specs=[pl.BlockSpec(memory_space=VMEM) for _ in outs],
        out_shape=[kept(shape, dtype) for shape, dtype in outs],
        scratch_shapes=list(scratch),
        cost_estimate=pl.CostEstimate(flops=flops, bytes_accessed=moved, transcendentals=0),
        compiler_params=pltpu.CompilerParams(vmem_limit_bytes=16 * 2**20),
    )(*operands)


def picks(shape, q_dev, place):
    row = lax.broadcasted_iota(jnp.int32, shape, 0)
    query = lax.broadcasted_iota(jnp.int32, shape, 1)
    block = lax.axis_index("dp") ^ (row // (2 * q_dev))
    wanted = block * q_dev + row % q_dev
    found = (query == wanted) & ((row // q_dev) % 2 == place)
    return jnp.where(found, 1.0, 0.0)


def fetch(pairs, sems):
    return [
        pltpu.make_async_copy(source, target, sems.at[at])
        for at, (source, target) in enumerate(pairs)
    ]


def begin(copies):
    for copy in copies[:AHEAD]:
        copy.start()


def arrive(copies, part):
    copies[part].wait()
    if part + AHEAD < len(copies):
        copies[part + AHEAD].start()


def prime_kernel(
    cols_hbm, values_hbm, expand, kept, raised, own, cols, values, few, sems
):
    step = expand.shape[1] // PARTS
    small = fetch([(cols_hbm, cols), (values_hbm, values)], few)
    begin(small)
    spans = [pl.ds(part * step, step) for part in range(PARTS)]
    copies = fetch([(expand.at[:, span], kept.at[:, span]) for span in spans], sems)
    begin(copies)
    rows = own.shape[0]
    q_dev = rows // 2
    laid = picks((raised.shape[0], cols.shape[0]), q_dev, 1).astype(bf16)
    for copy in small:
        copy.wait()
    laid = dot_nn(laid, cols[...]).astype(bf16)
    for part in range(PARTS):
        span = slice(part * step, (part + 1) * step)
        arrive(copies, part)
        found = adapter_scale * dot_nn(laid, kept[:, span])
        raised[:, span] = found.astype(bf16)
        above = jnp.concatenate([values[:, span].astype(f32), found[q_dev:rows]])
        own[:, span] = above.astype(bf16)


def keep_kernel(q_dev, cols_hbm, down, kept, raised, cols, few, sems):
    step = down.shape[0] // PARTS
    small = fetch([(cols_hbm, cols)], few)
    begin(small)
    spans = [pl.ds(part * step, step) for part in range(PARTS)]
    copies = fetch([(down.at[span], kept.at[span]) for span in spans], sems)
    begin(copies)
    laid = picks((raised.shape[0], cols.shape[0]), q_dev, 0).astype(bf16)
    small[0].wait()
    laid = dot_nn(laid, cols[...]).astype(bf16)
    for part in range(PARTS):
        span = slice(part * step, (part + 1) * step)
        arrive(copies, part)
        raised[:, span] = (adapter_scale * dot_nt(laid, kept[span, :])).astype(bf16)


def through_kernel(turn, arrived, before, down, expand, ranks, leaving):
    depth, width = down.shape
    step = 2 * width
    mine = lax.axis_index("pipe") % 2 == turn

    @pl.when(jnp.logical_not(mine))
    def _():
        ranks[...] = before[...]

    @pl.when(mine)
    def _():
        total = jnp.zeros(ranks.shape, f32)
        for at in range(0, depth, step):
            total += dot_nn(arrived[:, at : at + step], down[at : at + step, :])
        found = total.astype(bf16)
        ranks[...] = found
        for at in range(0, depth, step):
            more = adapter_scale * dot_nn(found, expand[:, at : at + step])
            leaving[:, at : at + step] = (arrived[:, at : at + step].astype(f32) + more).astype(bf16)


def last_kernel(arrived, before, down, ranks):
    depth, width = down.shape
    step = 2 * width
    mine = lax.axis_index("pipe") % 2 == 1

    @pl.when(jnp.logical_not(mine))
    def _():
        ranks[...] = before[...]

    @pl.when(mine)
    def _():
        total = jnp.zeros(ranks.shape, f32)
        for at in range(0, depth, step):
            total += dot_nn(arrived[:, at : at + step], down[at : at + step, :])
        ranks[...] = total.astype(bf16)


def lift_kernel(start, cotangent, expand, lifted, buffer, total, sems):
    count, depth = buffer.shape
    parts = PARTS
    step = depth // parts
    spans = [pl.ds(part * step, step) for part in range(parts)]
    rows = pl.ds(start, count)
    copies = fetch([(cotangent.at[rows, span], buffer.at[:, span]) for span in spans], sems)
    begin(copies)
    for part in range(parts):
        span = slice(part * step, (part + 1) * step)
        arrive(copies, part)
        found = dot_nt(buffer[:, span], expand[:, span])
        if part == 0:
            total[...] = found
        elif part < parts - 1:
            total[...] += found
        else:
            lifted[...] = (adapter_scale * (total[...] + found)).astype(bf16)


def weave_kernel(q_dev, hidden, rows, raised, left_rows, right_rows):
    count, depth = rows.shape
    step = depth // 8
    place = lax.broadcasted_iota(jnp.int32, (count, step), 0) // q_dev
    first = place % 2 == 0
    for at in range(0, depth, step):
        span = slice(at, at + step)
        given = rows[:, span].astype(f32)
        left_rows[:, span] = jnp.where(first, hidden[:, span].astype(f32), given).astype(bf16)
        right_rows[:, span] = jnp.where(first, given, raised[:, span].astype(f32)).astype(bf16)


def summed(terms, shape):
    example = lax.broadcasted_iota(jnp.int32, (shape[0], terms.shape[1]), 0)
    position = lax.broadcasted_iota(jnp.int32, (shape[0], terms.shape[1]), 1)
    ones = jnp.where(position // SLOT == example, 1.0, 0.0)
    return dot_nt(ones, terms, lax.Precision.HIGHEST)


def weighed(weights, blocks, at, rows, lifted):
    ranks = jnp.concatenate([block[at : at + rows, :].astype(f32) for block in blocks])
    ranks = ranks.astype(bf16)
    return weights * jnp.concatenate([dot_nt(ranks, part[...]) for part in lifted], axis=1)


def by_layer(own, other):
    upper = jnp.full(own.shape, lax.axis_index("pipe") % 2, jnp.int32) == 1
    own, other = own.astype(f32), other.astype(f32)
    return jnp.where(upper, other, own), jnp.where(upper, own, other)


def early_kernel(chips, rows, left, right, others, *refs):
    lifted, ups, blocks, sums = refs[:2], refs[2 : 2 + chips], refs[2 + chips : -1], refs[-1]
    terms = left[...] * right[...]
    for slot in range(chips - 1):
        lower, upper = by_layer(ups[slot][...], others[slot])
        if slot == 0:
            terms += weighed(lower, blocks, 0, rows, lifted)
        else:
            at = rows * (2 * slot - 1)
            terms += weighed(lower, blocks, at, rows, lifted)
            terms += weighed(upper, blocks, at + rows, rows, lifted)
    sums[...] = summed(terms, sums.shape)


def late_kernel(chips, rows, own, others, early, *refs):
    lifted, blocks, sums = refs[:2], refs[2:-1], refs[-1]
    lower, upper = by_layer(own[...], others[chips - 1])
    terms = weighed(lower, blocks, 0, rows, lifted)
    terms += weighed(upper, blocks, rows, rows, lifted)
    sums[...] = early[...] + summed(terms, sums.shape)


def final_kernel(q_dev, queries, *refs):
    parts, scores = refs[:-1], refs[-1]
    total = parts[0][...]
    for part in parts[1:]:
        total += part[...]
    ex_dev, q_all = scores.shape
    shape = (total.shape[1], q_all)
    laid = picks(shape, q_dev, 0) + picks(shape, q_dev, 1)
    total = dot_nn(total, laid, lax.Precision.HIGHEST)[:ex_dev]
    example = lax.axis_index("dp") * ex_dev + lax.broadcasted_iota(jnp.int32, scores.shape, 0)
    keep = example != jnp.broadcast_to(queries[...], scores.shape)
    scores[...] = jnp.where(keep, total * SLOT ** (-0.5), 0.0)


def local(
    activations,
    cotangent,
    adapter_down,
    adapter_expand,
    value_rows,
    input_rows,
    hidden_cols,
    inner_cols,
    lengths,
    query_example,
):
    columns = lax.axis_size("dp")
    chips = lax.axis_size("pipe") // 2
    top = chips - 1
    tok_dev = activations.shape[1]
    ex_dev = tok_dev // SLOT
    q_dev = value_rows.shape[1]
    rows = 2 * q_dev
    count = columns * rows
    width, rank = adapter_down.shape[1:]
    weight_bytes = 2 * width * rank
    pass_flops = 2 * rows * width * rank

    offsets = lax.broadcasted_iota(jnp.int32, (ex_dev, SLOT), 1)
    live = (offsets < lengths[:, None]).astype(f32).reshape(1, tok_dev)

    def through(turn, arrived, before):
        return call(
            functools.partial(through_kernel, turn),
            (arrived, before, down, expand),
            "vvvv",
            [(before.shape, bf16), (arrived.shape, bf16)],
            flops=2 * pass_flops,
            moved=weight_bytes,
        )

    expand, raised, own = call(
        prime_kernel,
        (inner_cols[0], value_rows[0], adapter_expand[0]),
        "hhh",
        [((rank, width), bf16), ((count, width), bf16), ((rows, width), bf16)],
        [
            VMEM(inner_cols.shape[1:], bf16),
            VMEM((q_dev, width), bf16),
            pltpu.SemaphoreType.DMA((2,)),
            pltpu.SemaphoreType.DMA((PARTS,)),
        ],
        flops=pass_flops,
        moved=2 * weight_bytes,
    )

    arrived = upward(own, 0, 1, 2)
    hid, source = tie([hidden_cols[0], adapter_down[0]], own)
    down, hidden = call(
        functools.partial(keep_kernel, q_dev),
        (hid, source),
        "hh",
        [((width, rank), bf16), ((count, width), bf16)],
        [
            VMEM(hidden_cols.shape[1:], bf16),
            pltpu.SemaphoreType.DMA((1,)),
            pltpu.SemaphoreType.DMA((PARTS,)),
        ],
        flops=2 * count * width * rank,
        moved=2 * weight_bytes,
    )
    arrived, down = lax.optimization_barrier((arrived, down))
    lower_ranks, leaving = through(1, arrived, jnp.zeros((rows, rank), bf16))
    moving = jnp.concatenate([leaving, own])

    half = tok_dev // 2

    def lift(part, token):
        (cot,) = tie([cotangent], token)
        return call(
            functools.partial(lift_kernel, part * half),
            (cot, expand),
            "hv",
            [((half, rank), bf16)],
            [
                VMEM((half, width), bf16),
                VMEM((half, rank), f32),
                pltpu.SemaphoreType.DMA((PARTS,)),
            ],
            flops=2 * half * width * rank,
            moved=weight_bytes,
        )[0]

    arrived = upward(moving, 1, 1, 2)
    wide = tie([value_rows[0], input_rows[0]], moving)
    wide = spread(jnp.concatenate(wide), "dp")
    lifted = [lift(0, moving)]
    arrived, lifted[0] = lax.optimization_barrier((arrived, lifted[0]))

    slots = []
    empty = jnp.zeros((2 * rows, rank), bf16)
    for slot in range(1, chips):
        found, leaving = through(0, arrived, empty)
        arrived = upward(leaving, 0, 1, 2)
        if slot == 1:
            lifted.append(lift(1, leaving))
            wide = jnp.concatenate(tie(wide, lifted[1]))
            arrived, wide = lax.optimization_barrier((arrived, wide))
        if slot == 2:
            (cot,) = tie([cotangent], leaving)
            right = dot_nt(right_rows, cot)
            arrived, right, *left_up = lax.optimization_barrier((arrived, right, *left_up))
        if slot == top:
            (sums,) = call(
                functools.partial(early_kernel, chips, rows),
                (left, right, others, *lifted, *left_up, *early),
                "v" * (5 + chips + columns),
                [((max(ex_dev, 8), count), f32)],
                flops=2 * count * rank * tok_dev * (2 * chips),
                moved=weight_bytes,
            )
            arrived, sums = lax.optimization_barrier((arrived, sums))
            break
        found, leaving = through(1, arrived, found)
        slots.append(found)
        arrived = upward(leaving, 1, 1, 2)
        if slot == 1:
            left_rows, right_rows = call(
                functools.partial(weave_kernel, q_dev),
                (hidden, wide, raised),
                "vvv",
                [((count, width), bf16), ((count, width), bf16)],
                flops=2 * count * width,
                moved=weight_bytes // 2,
            )
            left = dot_nt(left_rows, activations[0]) * live
            left_own = left.astype(bf16)
            left_up = [left_own] + [upward(left_own, 0, 2 * hop, 1) for hop in range(1, chips)]
            arrived, left_own = lax.optimization_barrier((arrived, left_own))
        if slot == top - 1:
            (early,) = tie([jnp.concatenate([lower_ranks] + slots)], leaving)
            early = spread(early, "dp")
            others = swap(jnp.stack(tie(left_up, early[1])), "pipe", 1)
            arrived, others, *early = lax.optimization_barrier((arrived, others, *early))

    (late,) = call(
        last_kernel,
        (arrived, found, down),
        "vvv",
        [((2 * rows, rank), bf16)],
        flops=pass_flops,
        moved=weight_bytes,
    )
    late = spread(late, "dp")
    (sums,) = call(
        functools.partial(late_kernel, chips, rows),
        (left_up[-1], others, sums, *lifted, *late),
        "v" * (5 + columns),
        [(sums.shape, f32)],
        flops=2 * count * rank * tok_dev * 2,
        moved=weight_bytes // 8,
    )
    sums = sums + swap(sums, "pipe", 1)
    parts = [sums] + [around(sums, hop) for hop in range(1, chips)]
    (scores,) = call(
        functools.partial(final_kernel, q_dev),
        (query_example[None], *parts),
        "v" * (1 + chips),
        [((ex_dev, columns * q_dev), f32)],
        kept=jax.ShapeDtypeStruct,
    )
    return scores


def solution(mesh):
    in_specs = (
        P("pipe", "dp", None),
        P("dp", None),
        P("pipe", None, None),
        P("pipe", None, None),
        P("pipe", "dp", None),
        P("pipe", "dp", None),
        P("pipe", None, None),
        P("pipe", None, None),
        P("dp"),
        P(),
    )
    out_specs = P("dp", None)
    return jax.shard_map(local, mesh=mesh, in_specs=in_specs, out_specs=out_specs, check_vma=False)
```

```python
import functools

import jax
import jax.numpy as jnp
from jax import lax
from jax.experimental import pallas as pl
from jax.experimental.pallas import tpu as pltpu
from jax.sharding import PartitionSpec as P

SLOT = 128
PARTS = 4
AHEAD = 3


adapter_scale = 0.25
bf16 = jnp.bfloat16
f32 = jnp.float32
VMEM = pltpu.VMEM


def dot_nn(a, b, precision=None):
    return lax.dot_general(
        a, b, (((1,), (0,)), ((), ())), preferred_element_type=f32, precision=precision
    )


def dot_nt(a, b, precision=None):
    return lax.dot_general(
        a, b, (((1,), (1,)), ((), ())), preferred_element_type=f32, precision=precision
    )


def swap(value, axis, distance):
    count = lax.axis_size(axis)
    return lax.ppermute(value, axis, [(source, source ^ distance) for source in range(count)])


def spread(value, axis):
    return [value] + [swap(value, axis, d) for d in range(1, lax.axis_size(axis))]


def upward(value, first, hop, stride):
    count = lax.axis_size("pipe")
    return lax.ppermute(
        value, "pipe", [(source, source + hop) for source in range(first, count - hop, stride)]
    )


def around(value, hop):
    count = lax.axis_size("pipe")
    return lax.ppermute(
        value, "pipe", [(source, (source + 2 * hop) % count) for source in range(count)]
    )


def tie(values, token):
    *values, _ = lax.optimization_barrier((*values, token))
    return values


def call(kernel, operands, places, outs, scratch=(), flops=0, moved=0, kept=VMEM):
    space = {"v": VMEM, "s": pltpu.SMEM, "h": pltpu.HBM}
    operands = [
        x if place == "s" else pltpu.with_memory_space_constraint(x, space[place])
        for x, place in zip(operands, places)
    ]
    return pl.pallas_call(
        kernel,
        in_specs=[pl.BlockSpec(memory_space=space[place]) for place in places],
        out_specs=[pl.BlockSpec(memory_space=VMEM) for _ in outs],
        out_shape=[kept(shape, dtype) for shape, dtype in outs],
        scratch_shapes=list(scratch),
        cost_estimate=pl.CostEstimate(flops=flops, bytes_accessed=moved, transcendentals=0),
        compiler_params=pltpu.CompilerParams(vmem_limit_bytes=16 * 2**20),
    )(*operands)


def picks(shape, q_dev, place):
    row = lax.broadcasted_iota(jnp.int32, shape, 0)
    query = lax.broadcasted_iota(jnp.int32, shape, 1)
    block = lax.axis_index("dp") ^ (row // (2 * q_dev))
    wanted = block * q_dev + row % q_dev
    found = (query == wanted) & ((row // q_dev) % 2 == place)
    return jnp.where(found, 1.0, 0.0)


def fetch(pairs, sems):
    return [
        pltpu.make_async_copy(source, target, sems.at[at])
        for at, (source, target) in enumerate(pairs)
    ]


def begin(copies):
    for copy in copies[:AHEAD]:
        copy.start()


def arrive(copies, part):
    copies[part].wait()
    if part + AHEAD < len(copies):
        copies[part + AHEAD].start()


def prime_kernel(
    cols_hbm, values_hbm, expand, down, kept, kept_down, raised, own, cols, values, few, sems
):
    step = expand.shape[1] // PARTS
    deep = down.shape[0] // PARTS
    small = fetch([(cols_hbm, cols), (values_hbm, values)], few)
    begin(small)
    wide = [pl.ds(part * step, step) for part in range(PARTS)]
    tall = [pl.ds(part * deep, deep) for part in range(PARTS)]
    copies = fetch(
        [(expand.at[:, span], kept.at[:, span]) for span in wide]
        + [(down.at[span], kept_down.at[span]) for span in tall],
        sems,
    )
    begin(copies)
    rows = own.shape[0]
    q_dev = rows // 2
    laid = picks((raised.shape[0], cols.shape[0]), q_dev, 1).astype(bf16)
    for copy in small:
        copy.wait()
    laid = dot_nn(laid, cols[...]).astype(bf16)
    for part in range(PARTS):
        span = slice(part * step, (part + 1) * step)
        arrive(copies, part)
        found = adapter_scale * dot_nn(laid, kept[:, span])
        raised[:, span] = found.astype(bf16)
        above = jnp.concatenate([values[:, span].astype(f32), found[q_dev:rows]])
        own[:, span] = above.astype(bf16)
    for part in range(PARTS, 2 * PARTS):
        arrive(copies, part)


def hidden_kernel(q_dev, cols_hbm, down, raised, cols, few):
    step = down.shape[0] // PARTS
    small = fetch([(cols_hbm, cols)], few)
    begin(small)
    laid = picks((raised.shape[0], cols.shape[0]), q_dev, 0).astype(bf16)
    small[0].wait()
    laid = dot_nn(laid, cols[...]).astype(bf16)
    for part in range(PARTS):
        span = slice(part * step, (part + 1) * step)
        raised[:, span] = (adapter_scale * dot_nt(laid, down[span, :])).astype(bf16)


def through_kernel(turn, arrived, before, down, expand, ranks, leaving):
    depth, width = down.shape
    step = 2 * width
    mine = lax.axis_index("pipe") % 2 == turn

    @pl.when(jnp.logical_not(mine))
    def _():
        ranks[...] = before[...]

    @pl.when(mine)
    def _():
        total = jnp.zeros(ranks.shape, f32)
        for at in range(0, depth, step):
            total += dot_nn(arrived[:, at : at + step], down[at : at + step, :])
        found = total.astype(bf16)
        ranks[...] = found
        for at in range(0, depth, step):
            more = adapter_scale * dot_nn(found, expand[:, at : at + step])
            leaving[:, at : at + step] = (arrived[:, at : at + step].astype(f32) + more).astype(bf16)


def last_kernel(arrived, before, down, ranks):
    depth, width = down.shape
    step = 2 * width
    mine = lax.axis_index("pipe") % 2 == 1

    @pl.when(jnp.logical_not(mine))
    def _():
        ranks[...] = before[...]

    @pl.when(mine)
    def _():
        total = jnp.zeros(ranks.shape, f32)
        for at in range(0, depth, step):
            total += dot_nn(arrived[:, at : at + step], down[at : at + step, :])
        ranks[...] = total.astype(bf16)


def lift_kernel(start, cotangent, expand, lifted, buffer, total, sems):
    count, depth = buffer.shape
    parts = PARTS
    step = depth // parts
    spans = [pl.ds(part * step, step) for part in range(parts)]
    rows = pl.ds(start, count)
    copies = fetch([(cotangent.at[rows, span], buffer.at[:, span]) for span in spans], sems)
    begin(copies)
    for part in range(parts):
        span = slice(part * step, (part + 1) * step)
        arrive(copies, part)
        found = dot_nt(buffer[:, span], expand[:, span])
        if part == 0:
            total[...] = found
        elif part < parts - 1:
            total[...] += found
        else:
            lifted[...] = (adapter_scale * (total[...] + found)).astype(bf16)


def weave_kernel(q_dev, hidden, rows, raised, left_rows, right_rows):
    count, depth = rows.shape
    step = depth // 8
    place = lax.broadcasted_iota(jnp.int32, (count, step), 0) // q_dev
    first = place % 2 == 0
    for at in range(0, depth, step):
        span = slice(at, at + step)
        given = rows[:, span].astype(f32)
        left_rows[:, span] = jnp.where(first, hidden[:, span].astype(f32), given).astype(bf16)
        right_rows[:, span] = jnp.where(first, given, raised[:, span].astype(f32)).astype(bf16)


def summed(terms, shape):
    example = lax.broadcasted_iota(jnp.int32, (shape[0], terms.shape[1]), 0)
    position = lax.broadcasted_iota(jnp.int32, (shape[0], terms.shape[1]), 1)
    ones = jnp.where(position // SLOT == example, 1.0, 0.0)
    return dot_nt(ones, terms, lax.Precision.HIGHEST)


def weighed(weights, blocks, at, rows, lifted):
    ranks = jnp.concatenate([block[at : at + rows, :].astype(f32) for block in blocks])
    ranks = ranks.astype(bf16)
    return weights * jnp.concatenate([dot_nt(ranks, part[...]) for part in lifted], axis=1)


def by_layer(own, other):
    upper = jnp.full(own.shape, lax.axis_index("pipe") % 2, jnp.int32) == 1
    own, other = own.astype(f32), other.astype(f32)
    return jnp.where(upper, other, own), jnp.where(upper, own, other)


def early_kernel(chips, rows, left, right, others, *refs):
    lifted, ups, blocks, sums = refs[:2], refs[2 : 2 + chips], refs[2 + chips : -1], refs[-1]
    terms = left[...] * right[...]
    for slot in range(chips - 1):
        lower, upper = by_layer(ups[slot][...], others[slot])
        if slot == 0:
            terms += weighed(lower, blocks, 0, rows, lifted)
        else:
            at = rows * (2 * slot - 1)
            terms += weighed(lower, blocks, at, rows, lifted)
            terms += weighed(upper, blocks, at + rows, rows, lifted)
    sums[...] = summed(terms, sums.shape)


def late_kernel(chips, rows, own, others, early, *refs):
    lifted, blocks, sums = refs[:2], refs[2:-1], refs[-1]
    lower, upper = by_layer(own[...], others[chips - 1])
    terms = weighed(lower, blocks, 0, rows, lifted)
    terms += weighed(upper, blocks, rows, rows, lifted)
    sums[...] = early[...] + summed(terms, sums.shape)


def final_kernel(q_dev, queries, *refs):
    parts, scores = refs[:-1], refs[-1]
    total = parts[0][...]
    for part in parts[1:]:
        total += part[...]
    ex_dev, q_all = scores.shape
    shape = (total.shape[1], q_all)
    laid = picks(shape, q_dev, 0) + picks(shape, q_dev, 1)
    total = dot_nn(total, laid, lax.Precision.HIGHEST)[:ex_dev]
    example = lax.axis_index("dp") * ex_dev + lax.broadcasted_iota(jnp.int32, scores.shape, 0)
    keep = example != jnp.broadcast_to(queries[...], scores.shape)
    scores[...] = jnp.where(keep, total * SLOT ** (-0.5), 0.0)


def local(
    activations,
    cotangent,
    adapter_down,
    adapter_expand,
    value_rows,
    input_rows,
    hidden_cols,
    inner_cols,
    lengths,
    query_example,
):
    columns = lax.axis_size("dp")
    chips = lax.axis_size("pipe") // 2
    top = chips - 1
    tok_dev = activations.shape[1]
    ex_dev = tok_dev // SLOT
    q_dev = value_rows.shape[1]
    rows = 2 * q_dev
    count = columns * rows
    width, rank = adapter_down.shape[1:]
    weight_bytes = 2 * width * rank
    pass_flops = 2 * rows * width * rank

    offsets = lax.broadcasted_iota(jnp.int32, (ex_dev, SLOT), 1)
    live = (offsets < lengths[:, None]).astype(f32).reshape(1, tok_dev)

    def through(turn, arrived, before):
        return call(
            functools.partial(through_kernel, turn),
            (arrived, before, down, expand),
            "vvvv",
            [(before.shape, bf16), (arrived.shape, bf16)],
            flops=2 * pass_flops,
            moved=weight_bytes,
        )

    expand, down, raised, own = call(
        prime_kernel,
        (inner_cols[0], value_rows[0], adapter_expand[0], adapter_down[0]),
        "hhhh",
        [
            ((rank, width), bf16),
            ((width, rank), bf16),
            ((count, width), bf16),
            ((rows, width), bf16),
        ],
        [
            VMEM(inner_cols.shape[1:], bf16),
            VMEM((q_dev, width), bf16),
            pltpu.SemaphoreType.DMA((2,)),
            pltpu.SemaphoreType.DMA((2 * PARTS,)),
        ],
        flops=pass_flops,
        moved=2 * weight_bytes,
    )

    arrived = upward(own, 0, 1, 2)
    (hid,) = tie([hidden_cols[0]], own)
    (hidden,) = call(
        functools.partial(hidden_kernel, q_dev),
        (hid, down),
        "hv",
        [((count, width), bf16)],
        [VMEM(hidden_cols.shape[1:], bf16), pltpu.SemaphoreType.DMA((1,))],
        flops=2 * count * width * rank,
        moved=weight_bytes,
    )
    arrived, hidden = lax.optimization_barrier((arrived, hidden))
    lower_ranks, leaving = through(1, arrived, jnp.zeros((rows, rank), bf16))
    moving = jnp.concatenate([leaving, own])

    cut = tok_dev * 5 // 8

    def lift(start, end, token):
        (cot,) = tie([cotangent], token)
        return call(
            functools.partial(lift_kernel, start),
            (cot, expand),
            "hv",
            [((end - start, rank), bf16)],
            [
                VMEM((end - start, width), bf16),
                VMEM((end - start, rank), f32),
                pltpu.SemaphoreType.DMA((PARTS,)),
            ],
            flops=2 * (end - start) * width * rank,
            moved=weight_bytes,
        )[0]

    arrived = upward(moving, 1, 1, 2)
    wide = tie([value_rows[0], input_rows[0]], moving)
    wide = spread(jnp.concatenate(wide), "dp")
    lifted = [lift(0, cut, moving)]
    arrived, lifted[0] = lax.optimization_barrier((arrived, lifted[0]))

    slots = []
    empty = jnp.zeros((2 * rows, rank), bf16)
    for slot in range(1, chips):
        found, leaving = through(0, arrived, empty)
        arrived = upward(leaving, 0, 1, 2)
        if slot == 1:
            lifted.append(lift(cut, tok_dev, leaving))
            wide = jnp.concatenate(tie(wide, lifted[1]))
            arrived, wide = lax.optimization_barrier((arrived, wide))
        if slot == 2:
            (cot,) = tie([cotangent], leaving)
            right = dot_nt(right_rows, cot)
            arrived, right, *left_up = lax.optimization_barrier((arrived, right, *left_up))
        if slot == top:
            others = swap(jnp.stack(tie(left_up, leaving)), "pipe", 1)
            arrived, others = lax.optimization_barrier((arrived, others))
            break
        found, leaving = through(1, arrived, found)
        slots.append(found)
        arrived = upward(leaving, 1, 1, 2)
        if slot == 1:
            left_rows, right_rows = call(
                functools.partial(weave_kernel, q_dev),
                (hidden, wide, raised),
                "vvv",
                [((count, width), bf16), ((count, width), bf16)],
                flops=2 * count * width,
                moved=weight_bytes // 2,
            )
            left = dot_nt(left_rows, activations[0]) * live
            left_own = left.astype(bf16)
            left_up = [left_own] + [upward(left_own, 0, 2 * hop, 1) for hop in range(1, chips)]
            arrived, left_own = lax.optimization_barrier((arrived, left_own))
        if slot == top - 1:
            (early,) = tie([jnp.concatenate([lower_ranks] + slots)], leaving)
            early = spread(early, "dp")
            arrived, *early = lax.optimization_barrier((arrived, *early))

    (late,) = call(
        last_kernel,
        (arrived, found, down),
        "vvv",
        [((2 * rows, rank), bf16)],
        flops=pass_flops,
        moved=weight_bytes,
    )
    (right,) = tie([right], late)
    (sums,) = call(
        functools.partial(early_kernel, chips, rows),
        (left, right, others, *lifted, *left_up, *early),
        "v" * (5 + chips + columns),
        [((max(ex_dev, 8), count), f32)],
        flops=2 * count * rank * tok_dev * (2 * chips),
        moved=weight_bytes,
    )
    late = spread(late, "dp")
    (sums,) = call(
        functools.partial(late_kernel, chips, rows),
        (left_up[-1], others, sums, *lifted, *late),
        "v" * (5 + columns),
        [(sums.shape, f32)],
        flops=2 * count * rank * tok_dev * 2,
        moved=weight_bytes // 8,
    )
    sums = sums + swap(sums, "pipe", 1)
    parts = [sums] + [around(sums, hop) for hop in range(1, chips)]
    (scores,) = call(
        functools.partial(final_kernel, q_dev),
        (query_example[None], *parts),
        "v" * (1 + chips),
        [((ex_dev, columns * q_dev), f32)],
        kept=jax.ShapeDtypeStruct,
    )
    return scores


def solution(mesh):
    in_specs = (
        P("pipe", "dp", None),
        P("dp", None),
        P("pipe", None, None),
        P("pipe", None, None),
        P("pipe", "dp", None),
        P("pipe", "dp", None),
        P("pipe", None, None),
        P("pipe", None, None),
        P("dp"),
        P(),
    )
    out_specs = P("dp", None)
    return jax.shard_map(local, mesh=mesh, in_specs=in_specs, out_specs=out_specs, check_vma=False)
```

```python
import functools

import jax
import jax.numpy as jnp
from jax import lax
from jax.experimental import pallas as pl
from jax.experimental.pallas import tpu as pltpu
from jax.sharding import PartitionSpec as P

SLOT = 128
PARTS = 4
AHEAD = 3


adapter_scale = 0.25
bf16 = jnp.bfloat16
f32 = jnp.float32
VMEM = pltpu.VMEM


def dot_nn(a, b, precision=None):
    return lax.dot_general(
        a, b, (((1,), (0,)), ((), ())), preferred_element_type=f32, precision=precision
    )


def dot_nt(a, b, precision=None):
    return lax.dot_general(
        a, b, (((1,), (1,)), ((), ())), preferred_element_type=f32, precision=precision
    )


def swap(value, axis, distance):
    count = lax.axis_size(axis)
    return lax.ppermute(value, axis, [(source, source ^ distance) for source in range(count)])


def spread(value, axis):
    return [value] + [swap(value, axis, d) for d in range(1, lax.axis_size(axis))]


def upward(value, first, hop, stride):
    count = lax.axis_size("pipe")
    return lax.ppermute(
        value, "pipe", [(source, source + hop) for source in range(first, count - hop, stride)]
    )


def around(value, hop):
    count = lax.axis_size("pipe")
    return lax.ppermute(
        value, "pipe", [(source, (source + 2 * hop) % count) for source in range(count)]
    )


def tie(values, token):
    *values, _ = lax.optimization_barrier((*values, token))
    return values


def call(kernel, operands, places, outs, scratch=(), flops=0, moved=0, kept=VMEM):
    space = {"v": VMEM, "s": pltpu.SMEM, "h": pltpu.HBM}
    operands = [
        x if place == "s" else pltpu.with_memory_space_constraint(x, space[place])
        for x, place in zip(operands, places)
    ]
    return pl.pallas_call(
        kernel,
        in_specs=[pl.BlockSpec(memory_space=space[place]) for place in places],
        out_specs=[pl.BlockSpec(memory_space=VMEM) for _ in outs],
        out_shape=[kept(shape, dtype) for shape, dtype in outs],
        scratch_shapes=list(scratch),
        cost_estimate=pl.CostEstimate(flops=flops, bytes_accessed=moved, transcendentals=0),
        compiler_params=pltpu.CompilerParams(vmem_limit_bytes=16 * 2**20),
    )(*operands)


def picks(shape, q_dev, place):
    row = lax.broadcasted_iota(jnp.int32, shape, 0)
    query = lax.broadcasted_iota(jnp.int32, shape, 1)
    block = lax.axis_index("dp") ^ (row // (2 * q_dev))
    wanted = block * q_dev + row % q_dev
    found = (query == wanted) & ((row // q_dev) % 2 == place)
    return jnp.where(found, 1.0, 0.0)


def fetch(pairs, sems):
    return [
        pltpu.make_async_copy(source, target, sems.at[at])
        for at, (source, target) in enumerate(pairs)
    ]


def begin(copies):
    for copy in copies[:AHEAD]:
        copy.start()


def arrive(copies, part):
    copies[part].wait()
    if part + AHEAD < len(copies):
        copies[part + AHEAD].start()


def prime_kernel(
    cols_hbm, values_hbm, expand, kept, raised, own, cols, values, few, sems
):
    step = expand.shape[1] // PARTS
    small = fetch([(cols_hbm, cols), (values_hbm, values)], few)
    begin(small)
    spans = [pl.ds(part * step, step) for part in range(PARTS)]
    copies = fetch([(expand.at[:, span], kept.at[:, span]) for span in spans], sems)
    begin(copies)
    rows = own.shape[0]
    q_dev = rows // 2
    laid = picks((raised.shape[0], cols.shape[0]), q_dev, 1).astype(bf16)
    for copy in small:
        copy.wait()
    laid = dot_nn(laid, cols[...]).astype(bf16)
    for part in range(PARTS):
        span = slice(part * step, (part + 1) * step)
        arrive(copies, part)
        found = adapter_scale * dot_nn(laid, kept[:, span])
        raised[:, span] = found.astype(bf16)
        above = jnp.concatenate([values[:, span].astype(f32), found[q_dev:rows]])
        own[:, span] = above.astype(bf16)


def keep_kernel(down, kept, sem):
    copy = pltpu.make_async_copy(down, kept, sem)
    copy.start()
    copy.wait()


def hidden_kernel(q_dev, cols_hbm, down, raised, cols, few):
    step = down.shape[0] // PARTS
    small = fetch([(cols_hbm, cols)], few)
    begin(small)
    laid = picks((raised.shape[0], cols.shape[0]), q_dev, 0).astype(bf16)
    small[0].wait()
    laid = dot_nn(laid, cols[...]).astype(bf16)
    for part in range(PARTS):
        span = slice(part * step, (part + 1) * step)
        raised[:, span] = (adapter_scale * dot_nt(laid, down[span, :])).astype(bf16)


def through_kernel(turn, arrived, before, down, expand, ranks, leaving):
    depth, width = down.shape
    step = 2 * width
    mine = lax.axis_index("pipe") % 2 == turn

    @pl.when(jnp.logical_not(mine))
    def _():
        ranks[...] = before[...]

    @pl.when(mine)
    def _():
        total = jnp.zeros(ranks.shape, f32)
        for at in range(0, depth, step):
            total += dot_nn(arrived[:, at : at + step], down[at : at + step, :])
        found = total.astype(bf16)
        ranks[...] = found
        for at in range(0, depth, step):
            more = adapter_scale * dot_nn(found, expand[:, at : at + step])
            leaving[:, at : at + step] = (arrived[:, at : at + step].astype(f32) + more).astype(bf16)


def last_kernel(arrived, before, down, ranks):
    depth, width = down.shape
    step = 2 * width
    mine = lax.axis_index("pipe") % 2 == 1

    @pl.when(jnp.logical_not(mine))
    def _():
        ranks[...] = before[...]

    @pl.when(mine)
    def _():
        total = jnp.zeros(ranks.shape, f32)
        for at in range(0, depth, step):
            total += dot_nn(arrived[:, at : at + step], down[at : at + step, :])
        ranks[...] = total.astype(bf16)


def lift_kernel(start, cotangent, expand, lifted, buffer, total, sems):
    count, depth = buffer.shape
    parts = PARTS
    step = depth // parts
    spans = [pl.ds(part * step, step) for part in range(parts)]
    rows = pl.ds(start, count)
    copies = fetch([(cotangent.at[rows, span], buffer.at[:, span]) for span in spans], sems)
    begin(copies)
    for part in range(parts):
        span = slice(part * step, (part + 1) * step)
        arrive(copies, part)
        found = dot_nt(buffer[:, span], expand[:, span])
        if part == 0:
            total[...] = found
        elif part < parts - 1:
            total[...] += found
        else:
            lifted[...] = (adapter_scale * (total[...] + found)).astype(bf16)


def weave_kernel(q_dev, hidden, rows, raised, left_rows, right_rows):
    count, depth = rows.shape
    step = depth // 8
    place = lax.broadcasted_iota(jnp.int32, (count, step), 0) // q_dev
    first = place % 2 == 0
    for at in range(0, depth, step):
        span = slice(at, at + step)
        given = rows[:, span].astype(f32)
        left_rows[:, span] = jnp.where(first, hidden[:, span].astype(f32), given).astype(bf16)
        right_rows[:, span] = jnp.where(first, given, raised[:, span].astype(f32)).astype(bf16)


def summed(terms, shape):
    example = lax.broadcasted_iota(jnp.int32, (shape[0], terms.shape[1]), 0)
    position = lax.broadcasted_iota(jnp.int32, (shape[0], terms.shape[1]), 1)
    ones = jnp.where(position // SLOT == example, 1.0, 0.0)
    return dot_nt(ones, terms, lax.Precision.HIGHEST)


def weighed(weights, blocks, at, rows, lifted):
    ranks = jnp.concatenate([block[at : at + rows, :].astype(f32) for block in blocks])
    ranks = ranks.astype(bf16)
    return weights * jnp.concatenate([dot_nt(ranks, part[...]) for part in lifted], axis=1)


def by_layer(own, other):
    upper = jnp.full(own.shape, lax.axis_index("pipe") % 2, jnp.int32) == 1
    own, other = own.astype(f32), other.astype(f32)
    return jnp.where(upper, other, own), jnp.where(upper, own, other)


def early_kernel(chips, rows, left, right, others, *refs):
    lifted, ups, blocks, sums = refs[:2], refs[2 : 2 + chips], refs[2 + chips : -1], refs[-1]
    terms = left[...] * right[...]
    for slot in range(chips - 1):
        lower, upper = by_layer(ups[slot][...], others[slot])
        if slot == 0:
            terms += weighed(lower, blocks, 0, rows, lifted)
        else:
            at = rows * (2 * slot - 1)
            terms += weighed(lower, blocks, at, rows, lifted)
            terms += weighed(upper, blocks, at + rows, rows, lifted)
    sums[...] = summed(terms, sums.shape)


def late_kernel(chips, rows, own, others, early, *refs):
    lifted, blocks, sums = refs[:2], refs[2:-1], refs[-1]
    lower, upper = by_layer(own[...], others[chips - 1])
    terms = weighed(lower, blocks, 0, rows, lifted)
    terms += weighed(upper, blocks, rows, rows, lifted)
    sums[...] = early[...] + summed(terms, sums.shape)


def final_kernel(q_dev, queries, *refs):
    parts, scores = refs[:-1], refs[-1]
    total = parts[0][...]
    for part in parts[1:]:
        total += part[...]
    ex_dev, q_all = scores.shape
    shape = (total.shape[1], q_all)
    laid = picks(shape, q_dev, 0) + picks(shape, q_dev, 1)
    total = dot_nn(total, laid, lax.Precision.HIGHEST)[:ex_dev]
    example = lax.axis_index("dp") * ex_dev + lax.broadcasted_iota(jnp.int32, scores.shape, 0)
    keep = example != jnp.broadcast_to(queries[...], scores.shape)
    scores[...] = jnp.where(keep, total * SLOT ** (-0.5), 0.0)


def local(
    activations,
    cotangent,
    adapter_down,
    adapter_expand,
    value_rows,
    input_rows,
    hidden_cols,
    inner_cols,
    lengths,
    query_example,
):
    columns = lax.axis_size("dp")
    chips = lax.axis_size("pipe") // 2
    top = chips - 1
    tok_dev = activations.shape[1]
    ex_dev = tok_dev // SLOT
    q_dev = value_rows.shape[1]
    rows = 2 * q_dev
    count = columns * rows
    width, rank = adapter_down.shape[1:]
    weight_bytes = 2 * width * rank
    pass_flops = 2 * rows * width * rank

    offsets = lax.broadcasted_iota(jnp.int32, (ex_dev, SLOT), 1)
    live = (offsets < lengths[:, None]).astype(f32).reshape(1, tok_dev)

    def through(turn, arrived, before):
        return call(
            functools.partial(through_kernel, turn),
            (arrived, before, down, expand),
            "vvvv",
            [(before.shape, bf16), (arrived.shape, bf16)],
            flops=2 * pass_flops,
            moved=weight_bytes,
        )

    expand, raised, own = call(
        prime_kernel,
        (inner_cols[0], value_rows[0], adapter_expand[0]),
        "hhh",
        [((rank, width), bf16), ((count, width), bf16), ((rows, width), bf16)],
        [
            VMEM(inner_cols.shape[1:], bf16),
            VMEM((q_dev, width), bf16),
            pltpu.SemaphoreType.DMA((2,)),
            pltpu.SemaphoreType.DMA((PARTS,)),
        ],
        flops=pass_flops,
        moved=2 * weight_bytes,
    )

    arrived = upward(own, 0, 1, 2)
    (source,) = tie([adapter_down[0]], own)
    (down,) = call(
        keep_kernel,
        (source,),
        "h",
        [((width, rank), bf16)],
        [pltpu.SemaphoreType.DMA],
        moved=2 * weight_bytes,
    )
    arrived, down = lax.optimization_barrier((arrived, down))
    lower_ranks, leaving = through(1, arrived, jnp.zeros((rows, rank), bf16))
    moving = jnp.concatenate([leaving, own])

    cut = tok_dev * 5 // 8

    def lift(start, end, token):
        (cot,) = tie([cotangent], token)
        return call(
            functools.partial(lift_kernel, start),
            (cot, expand),
            "hv",
            [((end - start, rank), bf16)],
            [
                VMEM((end - start, width), bf16),
                VMEM((end - start, rank), f32),
                pltpu.SemaphoreType.DMA((PARTS,)),
            ],
            flops=2 * (end - start) * width * rank,
            moved=weight_bytes,
        )[0]

    arrived = upward(moving, 1, 1, 2)
    wide = tie([value_rows[0], input_rows[0]], moving)
    wide = spread(jnp.concatenate(wide), "dp")
    lifted = [lift(0, cut, moving)]
    arrived, lifted[0] = lax.optimization_barrier((arrived, lifted[0]))

    slots = []
    empty = jnp.zeros((2 * rows, rank), bf16)
    for slot in range(1, chips):
        found, leaving = through(0, arrived, empty)
        arrived = upward(leaving, 0, 1, 2)
        if slot == 1:
            (hid,) = tie([hidden_cols[0]], leaving)
            (hidden,) = call(
                functools.partial(hidden_kernel, q_dev),
                (hid, down),
                "hv",
                [((count, width), bf16)],
                [VMEM(hidden_cols.shape[1:], bf16), pltpu.SemaphoreType.DMA((1,))],
                flops=2 * count * width * rank,
                moved=weight_bytes,
            )
            wide = jnp.concatenate(tie(wide, hidden))
            arrived, wide = lax.optimization_barrier((arrived, wide))
        if slot == 2:
            (cot,) = tie([cotangent], leaving)
            right = dot_nt(right_rows, cot)
            arrived, right, *left_up = lax.optimization_barrier((arrived, right, *left_up))
        if slot == top:
            others = swap(jnp.stack(tie(left_up, leaving)), "pipe", 1)
            arrived, others = lax.optimization_barrier((arrived, others))
            break
        found, leaving = through(1, arrived, found)
        slots.append(found)
        arrived = upward(leaving, 1, 1, 2)
        if slot == 1:
            left_rows, right_rows = call(
                functools.partial(weave_kernel, q_dev),
                (hidden, wide, raised),
                "vvv",
                [((count, width), bf16), ((count, width), bf16)],
                flops=2 * count * width,
                moved=weight_bytes // 2,
            )
            left = dot_nt(left_rows, activations[0]) * live
            left_own = left.astype(bf16)
            left_up = [left_own] + [upward(left_own, 0, 2 * hop, 1) for hop in range(1, chips)]
            arrived, left_own = lax.optimization_barrier((arrived, left_own))
        if slot == top - 1:
            (early,) = tie([jnp.concatenate([lower_ranks] + slots)], leaving)
            early = spread(early, "dp")
            lifted.append(lift(cut, tok_dev, leaving))
            arrived, lifted[1], *early = lax.optimization_barrier((arrived, lifted[1], *early))

    (late,) = call(
        last_kernel,
        (arrived, found, down),
        "vvv",
        [((2 * rows, rank), bf16)],
        flops=pass_flops,
        moved=weight_bytes,
    )
    (right,) = tie([right], late)
    (sums,) = call(
        functools.partial(early_kernel, chips, rows),
        (left, right, others, *lifted, *left_up, *early),
        "v" * (5 + chips + columns),
        [((max(ex_dev, 8), count), f32)],
        flops=2 * count * rank * tok_dev * (2 * chips),
        moved=weight_bytes,
    )
    late = spread(late, "dp")
    (sums,) = call(
        functools.partial(late_kernel, chips, rows),
        (left_up[-1], others, sums, *lifted, *late),
        "v" * (5 + columns),
        [(sums.shape, f32)],
        flops=2 * count * rank * tok_dev * 2,
        moved=weight_bytes // 8,
    )
    sums = sums + swap(sums, "pipe", 1)
    parts = [sums] + [around(sums, hop) for hop in range(1, chips)]
    (scores,) = call(
        functools.partial(final_kernel, q_dev),
        (query_example[None], *parts),
        "v" * (1 + chips),
        [((ex_dev, columns * q_dev), f32)],
        kept=jax.ShapeDtypeStruct,
    )
    return scores


def solution(mesh):
    in_specs = (
        P("pipe", "dp", None),
        P("dp", None),
        P("pipe", None, None),
        P("pipe", None, None),
        P("pipe", "dp", None),
        P("pipe", "dp", None),
        P("pipe", None, None),
        P("pipe", None, None),
        P("dp"),
        P(),
    )
    out_specs = P("dp", None)
    return jax.shard_map(local, mesh=mesh, in_specs=in_specs, out_specs=out_specs, check_vma=False)
```

```python
import functools

import jax
import jax.numpy as jnp
from jax import lax
from jax.experimental import pallas as pl
from jax.experimental.pallas import tpu as pltpu
from jax.sharding import PartitionSpec as P

SLOT = 128
PARTS = 4
AHEAD = 3


adapter_scale = 0.25
bf16 = jnp.bfloat16
f32 = jnp.float32
VMEM = pltpu.VMEM


def dot_nn(a, b, precision=None):
    return lax.dot_general(
        a, b, (((1,), (0,)), ((), ())), preferred_element_type=f32, precision=precision
    )


def dot_nt(a, b, precision=None):
    return lax.dot_general(
        a, b, (((1,), (1,)), ((), ())), preferred_element_type=f32, precision=precision
    )


def swap(value, axis, distance):
    count = lax.axis_size(axis)
    return lax.ppermute(value, axis, [(source, source ^ distance) for source in range(count)])


def spread(value, axis):
    far = [swap(value, axis, d) for d in reversed(range(1, lax.axis_size(axis)))]
    return [value] + far[::-1]


def upward(value, first, hop, stride):
    count = lax.axis_size("pipe")
    return lax.ppermute(
        value, "pipe", [(source, source + hop) for source in range(first, count - hop, stride)]
    )


def around(value, hop):
    count = lax.axis_size("pipe")
    return lax.ppermute(
        value, "pipe", [(source, (source + 2 * hop) % count) for source in range(count)]
    )


def tie(values, token):
    *values, _ = lax.optimization_barrier((*values, token))
    return values


def call(kernel, operands, places, outs, scratch=(), flops=0, moved=0, kept=VMEM):
    space = {"v": VMEM, "s": pltpu.SMEM, "h": pltpu.HBM}
    operands = [
        x if place == "s" else pltpu.with_memory_space_constraint(x, space[place])
        for x, place in zip(operands, places)
    ]
    return pl.pallas_call(
        kernel,
        in_specs=[pl.BlockSpec(memory_space=space[place]) for place in places],
        out_specs=[pl.BlockSpec(memory_space=VMEM) for _ in outs],
        out_shape=[kept(shape, dtype) for shape, dtype in outs],
        scratch_shapes=list(scratch),
        cost_estimate=pl.CostEstimate(flops=flops, bytes_accessed=moved, transcendentals=0),
        compiler_params=pltpu.CompilerParams(vmem_limit_bytes=16 * 2**20),
    )(*operands)


def picks(shape, q_dev, place):
    row = lax.broadcasted_iota(jnp.int32, shape, 0)
    query = lax.broadcasted_iota(jnp.int32, shape, 1)
    block = lax.axis_index("dp") ^ (row // (2 * q_dev))
    wanted = block * q_dev + row % q_dev
    found = (query == wanted) & ((row // q_dev) % 2 == place)
    return jnp.where(found, 1.0, 0.0)


def fetch(pairs, sems):
    return [
        pltpu.make_async_copy(source, target, sems.at[at])
        for at, (source, target) in enumerate(pairs)
    ]


def begin(copies):
    for copy in copies[:AHEAD]:
        copy.start()


def arrive(copies, part):
    copies[part].wait()
    if part + AHEAD < len(copies):
        copies[part + AHEAD].start()


def prime_kernel(
    cols_hbm, values_hbm, expand, down, kept, head, raised, own, cols, values, few, sems
):
    step = expand.shape[1] // PARTS
    small = fetch([(cols_hbm, cols), (values_hbm, values)], few)
    begin(small)
    spans = [pl.ds(part * step, step) for part in range(PARTS)]
    pairs = [(expand.at[:, span], kept.at[:, span]) for span in spans]
    copies = fetch(pairs + [(down.at[pl.ds(0, head.shape[0])], head)], sems)
    begin(copies)
    rows = own.shape[0]
    q_dev = rows // 2
    laid = picks((raised.shape[0], cols.shape[0]), q_dev, 1).astype(bf16)
    for copy in small:
        copy.wait()
    laid = dot_nn(laid, cols[...]).astype(bf16)
    for part in range(PARTS):
        span = slice(part * step, (part + 1) * step)
        arrive(copies, part)
        found = adapter_scale * dot_nn(laid, kept[:, span])
        raised[:, span] = found.astype(bf16)
        above = jnp.concatenate([values[:, span].astype(f32), found[q_dev:rows]])
        own[:, span] = above.astype(bf16)
    arrive(copies, PARTS)


def keep_kernel(down, rest, sem):
    count = rest.shape[0]
    copy = pltpu.make_async_copy(down.at[pl.ds(down.shape[0] - count, count)], rest, sem)
    copy.start()
    copy.wait()


def down_rows(head, rest, at, count):
    if at < head.shape[0]:
        return head[at : at + count, :]
    return rest[at - head.shape[0] : at - head.shape[0] + count, :]


def hidden_kernel(q_dev, cols_hbm, head, rest, raised, cols, few):
    step = raised.shape[1] // PARTS
    small = fetch([(cols_hbm, cols)], few)
    begin(small)
    laid = picks((raised.shape[0], cols.shape[0]), q_dev, 0).astype(bf16)
    small[0].wait()
    laid = dot_nn(laid, cols[...]).astype(bf16)
    for part in range(PARTS):
        span = slice(part * step, (part + 1) * step)
        raised[:, span] = (adapter_scale * dot_nt(laid, down_rows(head, rest, part * step, step))).astype(bf16)


def through_kernel(turn, arrived, before, head, rest, expand, ranks, leaving):
    depth = arrived.shape[1]
    step = 2 * ranks.shape[1]
    mine = lax.axis_index("pipe") % 2 == turn

    @pl.when(jnp.logical_not(mine))
    def _():
        ranks[...] = before[...]

    @pl.when(mine)
    def _():
        total = jnp.zeros(ranks.shape, f32)
        for at in range(0, depth, step):
            total += dot_nn(arrived[:, at : at + step], down_rows(head, rest, at, step))
        found = total.astype(bf16)
        ranks[...] = found
        for at in range(0, depth, step):
            more = adapter_scale * dot_nn(found, expand[:, at : at + step])
            leaving[:, at : at + step] = (arrived[:, at : at + step].astype(f32) + more).astype(bf16)


def last_kernel(arrived, before, head, rest, ranks):
    depth = arrived.shape[1]
    step = 2 * ranks.shape[1]
    mine = lax.axis_index("pipe") % 2 == 1

    @pl.when(jnp.logical_not(mine))
    def _():
        ranks[...] = before[...]

    @pl.when(mine)
    def _():
        total = jnp.zeros(ranks.shape, f32)
        for at in range(0, depth, step):
            total += dot_nn(arrived[:, at : at + step], down_rows(head, rest, at, step))
        ranks[...] = total.astype(bf16)


def lift_kernel(start, cotangent, expand, lifted, buffer, total, sems):
    count, depth = buffer.shape
    parts = PARTS
    step = depth // parts
    spans = [pl.ds(part * step, step) for part in range(parts)]
    rows = pl.ds(start, count)
    copies = fetch([(cotangent.at[rows, span], buffer.at[:, span]) for span in spans], sems)
    begin(copies)
    for part in range(parts):
        span = slice(part * step, (part + 1) * step)
        arrive(copies, part)
        found = dot_nt(buffer[:, span], expand[:, span])
        if part == 0:
            total[...] = found
        elif part < parts - 1:
            total[...] += found
        else:
            lifted[...] = (adapter_scale * (total[...] + found)).astype(bf16)


def weave_kernel(q_dev, hidden, rows, raised, left_rows, right_rows):
    count, depth = rows.shape
    step = depth // 8
    place = lax.broadcasted_iota(jnp.int32, (count, step), 0) // q_dev
    first = place % 2 == 0
    for at in range(0, depth, step):
        span = slice(at, at + step)
        given = rows[:, span].astype(f32)
        left_rows[:, span] = jnp.where(first, hidden[:, span].astype(f32), given).astype(bf16)
        right_rows[:, span] = jnp.where(first, given, raised[:, span].astype(f32)).astype(bf16)


def summed(terms, shape):
    example = lax.broadcasted_iota(jnp.int32, (shape[0], terms.shape[1]), 0)
    position = lax.broadcasted_iota(jnp.int32, (shape[0], terms.shape[1]), 1)
    ones = jnp.where(position // SLOT == example, 1.0, 0.0)
    return dot_nt(ones, terms, lax.Precision.HIGHEST)


def weighed(weights, blocks, at, rows, lifted):
    ranks = jnp.concatenate([block[at : at + rows, :].astype(f32) for block in blocks])
    ranks = ranks.astype(bf16)
    return weights * jnp.concatenate([dot_nt(ranks, part[...]) for part in lifted], axis=1)


def by_layer(own, other):
    upper = jnp.full(own.shape, lax.axis_index("pipe") % 2, jnp.int32) == 1
    own, other = own.astype(f32), other.astype(f32)
    return jnp.where(upper, other, own), jnp.where(upper, own, other)


def early_kernel(chips, rows, left, right, others, *refs):
    lifted, ups, blocks, sums = refs[:2], refs[2 : 2 + chips], refs[2 + chips : -1], refs[-1]
    terms = left[...] * right[...]
    for slot in range(chips - 1):
        lower, upper = by_layer(ups[slot][...], others[slot])
        if slot == 0:
            terms += weighed(lower, blocks, 0, rows, lifted)
        else:
            at = rows * (2 * slot - 1)
            terms += weighed(lower, blocks, at, rows, lifted)
            terms += weighed(upper, blocks, at + rows, rows, lifted)
    sums[...] = summed(terms, sums.shape)


def late_kernel(chips, rows, own, others, early, *refs):
    lifted, blocks, sums = refs[:2], refs[2:-1], refs[-1]
    lower, upper = by_layer(own[...], others[chips - 1])
    terms = weighed(lower, blocks, 0, rows, lifted)
    terms += weighed(upper, blocks, rows, rows, lifted)
    sums[...] = early[...] + summed(terms, sums.shape)


def final_kernel(q_dev, queries, *refs):
    parts, scores = refs[:-1], refs[-1]
    total = parts[0][...]
    for part in parts[1:]:
        total += part[...]
    ex_dev, q_all = scores.shape
    shape = (total.shape[1], q_all)
    laid = picks(shape, q_dev, 0) + picks(shape, q_dev, 1)
    total = dot_nn(total, laid, lax.Precision.HIGHEST)[:ex_dev]
    example = lax.axis_index("dp") * ex_dev + lax.broadcasted_iota(jnp.int32, scores.shape, 0)
    keep = example != jnp.broadcast_to(queries[...], scores.shape)
    scores[...] = jnp.where(keep, total * SLOT ** (-0.5), 0.0)


def local(
    activations,
    cotangent,
    adapter_down,
    adapter_expand,
    value_rows,
    input_rows,
    hidden_cols,
    inner_cols,
    lengths,
    query_example,
):
    columns = lax.axis_size("dp")
    chips = lax.axis_size("pipe") // 2
    top = chips - 1
    tok_dev = activations.shape[1]
    ex_dev = tok_dev // SLOT
    q_dev = value_rows.shape[1]
    rows = 2 * q_dev
    count = columns * rows
    width, rank = adapter_down.shape[1:]
    weight_bytes = 2 * width * rank
    pass_flops = 2 * rows * width * rank

    offsets = lax.broadcasted_iota(jnp.int32, (ex_dev, SLOT), 1)
    live = (offsets < lengths[:, None]).astype(f32).reshape(1, tok_dev)

    def through(turn, arrived, before):
        return call(
            functools.partial(through_kernel, turn),
            (arrived, before, *down, expand),
            "vvvvv",
            [(before.shape, bf16), (arrived.shape, bf16)],
            flops=2 * pass_flops,
            moved=weight_bytes,
        )

    head = width // PARTS
    expand, first, raised, own = call(
        prime_kernel,
        (inner_cols[0], value_rows[0], adapter_expand[0], adapter_down[0]),
        "hhhh",
        [
            ((rank, width), bf16),
            ((head, rank), bf16),
            ((count, width), bf16),
            ((rows, width), bf16),
        ],
        [
            VMEM(inner_cols.shape[1:], bf16),
            VMEM((q_dev, width), bf16),
            pltpu.SemaphoreType.DMA((2,)),
            pltpu.SemaphoreType.DMA((PARTS + 1,)),
        ],
        flops=pass_flops,
        moved=2 * weight_bytes,
    )

    arrived = upward(own, 0, 1, 2)
    (source,) = tie([adapter_down[0]], own)
    (rest,) = call(
        keep_kernel,
        (source,),
        "h",
        [((width - head, rank), bf16)],
        [pltpu.SemaphoreType.DMA],
        moved=2 * weight_bytes,
    )
    arrived, rest = lax.optimization_barrier((arrived, rest))
    down = (first, rest)
    lower_ranks, leaving = through(1, arrived, jnp.zeros((rows, rank), bf16))
    moving = jnp.concatenate([leaving, own])

    cut = tok_dev * 5 // 8

    def lift(start, end, token):
        (cot,) = tie([cotangent], token)
        return call(
            functools.partial(lift_kernel, start),
            (cot, expand),
            "hv",
            [((end - start, rank), bf16)],
            [
                VMEM((end - start, width), bf16),
                VMEM((end - start, rank), f32),
                pltpu.SemaphoreType.DMA((PARTS,)),
            ],
            flops=2 * (end - start) * width * rank,
            moved=weight_bytes,
        )[0]

    arrived = upward(moving, 1, 1, 2)
    wide = tie([value_rows[0], input_rows[0]], moving)
    wide = spread(jnp.concatenate(wide), "dp")
    lifted = [lift(0, cut, moving)]
    arrived, lifted[0] = lax.optimization_barrier((arrived, lifted[0]))

    slots = []
    empty = jnp.zeros((2 * rows, rank), bf16)
    for slot in range(1, chips):
        found, leaving = through(0, arrived, empty)
        arrived = upward(leaving, 0, 1, 2)
        if slot == 1:
            (hid,) = tie([hidden_cols[0]], leaving)
            (hidden,) = call(
                functools.partial(hidden_kernel, q_dev),
                (hid, *down),
                "hvv",
                [((count, width), bf16)],
                [VMEM(hidden_cols.shape[1:], bf16), pltpu.SemaphoreType.DMA((1,))],
                flops=2 * count * width * rank,
                moved=weight_bytes,
            )
            wide = jnp.concatenate(tie(wide, hidden))
            arrived, wide = lax.optimization_barrier((arrived, wide))
        if slot == 2:
            (cot,) = tie([cotangent], leaving)
            right = dot_nt(right_rows, cot)
            arrived, right, *left_up = lax.optimization_barrier((arrived, right, *left_up))
        if slot == top:
            others = swap(jnp.stack(tie(left_up, leaving)), "pipe", 1)
            arrived, others = lax.optimization_barrier((arrived, others))
            break
        found, leaving = through(1, arrived, found)
        slots.append(found)
        arrived = upward(leaving, 1, 1, 2)
        if slot == 1:
            left_rows, right_rows = call(
                functools.partial(weave_kernel, q_dev),
                (hidden, wide, raised),
                "vvv",
                [((count, width), bf16), ((count, width), bf16)],
                flops=2 * count * width,
                moved=weight_bytes // 2,
            )
            left = dot_nt(left_rows, activations[0]) * live
            left_own = left.astype(bf16)
            left_up = [left_own] + [upward(left_own, 0, 2 * hop, 1) for hop in range(1, chips)]
            arrived, left_own = lax.optimization_barrier((arrived, left_own))
        if slot == top - 1:
            (early,) = tie([jnp.concatenate([lower_ranks] + slots)], leaving)
            early = spread(early, "dp")
            lifted.append(lift(cut, tok_dev, leaving))
            arrived, lifted[1], *early = lax.optimization_barrier((arrived, lifted[1], *early))

    (late,) = call(
        last_kernel,
        (arrived, found, *down),
        "vvvv",
        [((2 * rows, rank), bf16)],
        flops=pass_flops,
        moved=weight_bytes,
    )
    (right,) = tie([right], late)
    (sums,) = call(
        functools.partial(early_kernel, chips, rows),
        (left, right, others, *lifted, *left_up, *early),
        "v" * (5 + chips + columns),
        [((max(ex_dev, 8), count), f32)],
        flops=2 * count * rank * tok_dev * (2 * chips),
        moved=weight_bytes,
    )
    late = spread(late, "dp")
    (sums,) = call(
        functools.partial(late_kernel, chips, rows),
        (left_up[-1], others, sums, *lifted, *late),
        "v" * (5 + columns),
        [(sums.shape, f32)],
        flops=2 * count * rank * tok_dev * 2,
        moved=weight_bytes // 8,
    )
    sums = sums + swap(sums, "pipe", 1)
    parts = [sums] + [around(sums, hop) for hop in range(1, chips)]
    (scores,) = call(
        functools.partial(final_kernel, q_dev),
        (query_example[None], *parts),
        "v" * (1 + chips),
        [((ex_dev, columns * q_dev), f32)],
        kept=jax.ShapeDtypeStruct,
    )
    return scores


def solution(mesh):
    in_specs = (
        P("pipe", "dp", None),
        P("dp", None),
        P("pipe", None, None),
        P("pipe", None, None),
        P("pipe", "dp", None),
        P("pipe", "dp", None),
        P("pipe", None, None),
        P("pipe", None, None),
        P("dp"),
        P(),
    )
    out_specs = P("dp", None)
    return jax.shard_map(local, mesh=mesh, in_specs=in_specs, out_specs=out_specs, check_vma=False)
```

```python
import functools

import jax
import jax.numpy as jnp
from jax import lax
from jax.experimental import pallas as pl
from jax.experimental.pallas import tpu as pltpu
from jax.sharding import PartitionSpec as P

SLOT = 128
PARTS = 4
AHEAD = 3


adapter_scale = 0.25
bf16 = jnp.bfloat16
f32 = jnp.float32
VMEM = pltpu.VMEM


def dot_nn(a, b, precision=None):
    return lax.dot_general(
        a, b, (((1,), (0,)), ((), ())), preferred_element_type=f32, precision=precision
    )


def dot_nt(a, b, precision=None):
    return lax.dot_general(
        a, b, (((1,), (1,)), ((), ())), preferred_element_type=f32, precision=precision
    )


def swap(value, axis, distance):
    count = lax.axis_size(axis)
    return lax.ppermute(value, axis, [(source, source ^ distance) for source in range(count)])


def spread(value, axis):
    far = [swap(value, axis, d) for d in reversed(range(1, lax.axis_size(axis)))]
    return [value] + far[::-1]


def upward(value, first, hop, stride):
    count = lax.axis_size("pipe")
    return lax.ppermute(
        value, "pipe", [(source, source + hop) for source in range(first, count - hop, stride)]
    )


def around(value, hop):
    count = lax.axis_size("pipe")
    return lax.ppermute(
        value, "pipe", [(source, (source + 2 * hop) % count) for source in range(count)]
    )


def tie(values, token):
    *values, _ = lax.optimization_barrier((*values, token))
    return values


def call(kernel, operands, places, outs, scratch=(), flops=0, moved=0, kept=VMEM):
    space = {"v": VMEM, "s": pltpu.SMEM, "h": pltpu.HBM}
    operands = [
        x if place == "s" else pltpu.with_memory_space_constraint(x, space[place])
        for x, place in zip(operands, places)
    ]
    return pl.pallas_call(
        kernel,
        in_specs=[pl.BlockSpec(memory_space=space[place]) for place in places],
        out_specs=[pl.BlockSpec(memory_space=VMEM) for _ in outs],
        out_shape=[kept(shape, dtype) for shape, dtype in outs],
        scratch_shapes=list(scratch),
        cost_estimate=pl.CostEstimate(flops=flops, bytes_accessed=moved, transcendentals=0),
        compiler_params=pltpu.CompilerParams(vmem_limit_bytes=16 * 2**20),
    )(*operands)


def picks(shape, q_dev, place):
    row = lax.broadcasted_iota(jnp.int32, shape, 0)
    query = lax.broadcasted_iota(jnp.int32, shape, 1)
    block = lax.axis_index("dp") ^ (row // (2 * q_dev))
    wanted = block * q_dev + row % q_dev
    found = (query == wanted) & ((row // q_dev) % 2 == place)
    return jnp.where(found, 1.0, 0.0)


def fetch(pairs, sems):
    return [
        pltpu.make_async_copy(source, target, sems.at[at])
        for at, (source, target) in enumerate(pairs)
    ]


def begin(copies):
    for copy in copies[:AHEAD]:
        copy.start()


def arrive(copies, part):
    copies[part].wait()
    if part + AHEAD < len(copies):
        copies[part + AHEAD].start()


def prime_kernel(
    cols_hbm, values_hbm, expand, down, kept, head, raised, own, cols, values, few, sems
):
    step = expand.shape[1] // PARTS
    small = fetch([(cols_hbm, cols), (values_hbm, values)], few)
    begin(small)
    spans = [pl.ds(part * step, step) for part in range(PARTS)]
    pairs = [(expand.at[:, span], kept.at[:, span]) for span in spans]
    copies = fetch(pairs + [(down.at[pl.ds(0, head.shape[0])], head)], sems)
    begin(copies)
    rows = own.shape[0]
    q_dev = rows // 2
    laid = picks((raised.shape[0], cols.shape[0]), q_dev, 1).astype(bf16)
    for copy in small:
        copy.wait()
    laid = dot_nn(laid, cols[...]).astype(bf16)
    for part in range(PARTS):
        span = slice(part * step, (part + 1) * step)
        arrive(copies, part)
        found = adapter_scale * dot_nn(laid, kept[:, span])
        raised[:, span] = found.astype(bf16)
        above = jnp.concatenate([values[:, span].astype(f32), found[q_dev:rows]])
        own[:, span] = above.astype(bf16)
    arrive(copies, PARTS)


def keep_kernel(down, rest, sem):
    count = rest.shape[0]
    copy = pltpu.make_async_copy(down.at[pl.ds(down.shape[0] - count, count)], rest, sem)
    copy.start()
    copy.wait()


def down_rows(head, rest, at, count):
    if at < head.shape[0]:
        return head[at : at + count, :]
    return rest[at - head.shape[0] : at - head.shape[0] + count, :]


def hidden_kernel(q_dev, cols_hbm, head, rest, raised, cols, few):
    step = raised.shape[1] // PARTS
    small = fetch([(cols_hbm, cols)], few)
    begin(small)
    laid = picks((raised.shape[0], cols.shape[0]), q_dev, 0).astype(bf16)
    small[0].wait()
    laid = dot_nn(laid, cols[...]).astype(bf16)
    for part in range(PARTS):
        span = slice(part * step, (part + 1) * step)
        raised[:, span] = (adapter_scale * dot_nt(laid, down_rows(head, rest, part * step, step))).astype(bf16)


def through_kernel(turn, arrived, before, head, rest, expand, ranks, leaving):
    depth = arrived.shape[1]
    step = 2 * ranks.shape[1]
    mine = lax.axis_index("pipe") % 2 == turn

    @pl.when(jnp.logical_not(mine))
    def _():
        ranks[...] = before[...]

    @pl.when(mine)
    def _():
        total = jnp.zeros(ranks.shape, f32)
        for at in range(0, depth, step):
            total += dot_nn(arrived[:, at : at + step], down_rows(head, rest, at, step))
        found = total.astype(bf16)
        ranks[...] = found
        for at in range(0, depth, step):
            more = adapter_scale * dot_nn(found, expand[:, at : at + step])
            leaving[:, at : at + step] = (arrived[:, at : at + step].astype(f32) + more).astype(bf16)


def last_kernel(arrived, before, head, rest, ranks):
    depth = arrived.shape[1]
    step = 2 * ranks.shape[1]
    mine = lax.axis_index("pipe") % 2 == 1

    @pl.when(jnp.logical_not(mine))
    def _():
        ranks[...] = before[...]

    @pl.when(mine)
    def _():
        total = jnp.zeros(ranks.shape, f32)
        for at in range(0, depth, step):
            total += dot_nn(arrived[:, at : at + step], down_rows(head, rest, at, step))
        ranks[...] = total.astype(bf16)


def lift_kernel(start, cotangent, expand, lifted, buffer, total, sems):
    count, depth = buffer.shape
    parts = PARTS
    step = depth // parts
    spans = [pl.ds(part * step, step) for part in range(parts)]
    rows = pl.ds(start, count)
    copies = fetch([(cotangent.at[rows, span], buffer.at[:, span]) for span in spans], sems)
    begin(copies)
    for part in range(parts):
        span = slice(part * step, (part + 1) * step)
        arrive(copies, part)
        found = dot_nt(buffer[:, span], expand[:, span])
        if part == 0:
            total[...] = found
        elif part < parts - 1:
            total[...] += found
        else:
            lifted[...] = (adapter_scale * (total[...] + found)).astype(bf16)


def weave_kernel(q_dev, hidden, rows, raised, left_rows, right_rows):
    count, depth = rows.shape
    step = depth // 8
    place = lax.broadcasted_iota(jnp.int32, (count, step), 0) // q_dev
    first = place % 2 == 0
    for at in range(0, depth, step):
        span = slice(at, at + step)
        given = rows[:, span].astype(f32)
        left_rows[:, span] = jnp.where(first, hidden[:, span].astype(f32), given).astype(bf16)
        right_rows[:, span] = jnp.where(first, given, raised[:, span].astype(f32)).astype(bf16)


def summed(terms, shape):
    example = lax.broadcasted_iota(jnp.int32, (shape[0], terms.shape[1]), 0)
    position = lax.broadcasted_iota(jnp.int32, (shape[0], terms.shape[1]), 1)
    ones = jnp.where(position // SLOT == example, 1.0, 0.0)
    return dot_nt(ones, terms, lax.Precision.HIGHEST)


def weighed(weights, blocks, at, rows, lifted):
    ranks = jnp.concatenate([block[at : at + rows, :].astype(f32) for block in blocks])
    ranks = ranks.astype(bf16)
    return weights * jnp.concatenate([dot_nt(ranks, part[...]) for part in lifted], axis=1)


def by_layer(own, other):
    upper = jnp.full(own.shape, lax.axis_index("pipe") % 2, jnp.int32) == 1
    own, other = own.astype(f32), other.astype(f32)
    return jnp.where(upper, other, own), jnp.where(upper, own, other)


def early_kernel(chips, rows, left, right, others, *refs):
    lifted, ups, blocks, sums = refs[:2], refs[2 : 2 + chips], refs[2 + chips : -1], refs[-1]
    terms = left[...] * right[...]
    for slot in range(chips - 1):
        lower, upper = by_layer(ups[slot][...], others[slot])
        if slot == 0:
            terms += weighed(lower, blocks, 0, rows, lifted)
        else:
            at = rows * (2 * slot - 1)
            terms += weighed(lower, blocks, at, rows, lifted)
            terms += weighed(upper, blocks, at + rows, rows, lifted)
    sums[...] = summed(terms, sums.shape)


def late_kernel(chips, rows, own, others, early, *refs):
    lifted, blocks, sums = refs[:2], refs[2:-1], refs[-1]
    lower, upper = by_layer(own[...], others[chips - 1])
    terms = weighed(lower, blocks, 0, rows, lifted)
    terms += weighed(upper, blocks, rows, rows, lifted)
    sums[...] = early[...] + summed(terms, sums.shape)


def final_kernel(q_dev, queries, *refs):
    parts, scores = refs[:-1], refs[-1]
    total = parts[0][...]
    for part in parts[1:]:
        total += part[...]
    ex_dev, q_all = scores.shape
    shape = (total.shape[1], q_all)
    laid = picks(shape, q_dev, 0) + picks(shape, q_dev, 1)
    total = dot_nn(total, laid, lax.Precision.HIGHEST)[:ex_dev]
    example = lax.axis_index("dp") * ex_dev + lax.broadcasted_iota(jnp.int32, scores.shape, 0)
    keep = example != jnp.broadcast_to(queries[...], scores.shape)
    scores[...] = jnp.where(keep, total * SLOT ** (-0.5), 0.0)


def local(
    activations,
    cotangent,
    adapter_down,
    adapter_expand,
    value_rows,
    input_rows,
    hidden_cols,
    inner_cols,
    lengths,
    query_example,
):
    columns = lax.axis_size("dp")
    chips = lax.axis_size("pipe") // 2
    top = chips - 1
    tok_dev = activations.shape[1]
    ex_dev = tok_dev // SLOT
    q_dev = value_rows.shape[1]
    rows = 2 * q_dev
    count = columns * rows
    width, rank = adapter_down.shape[1:]
    weight_bytes = 2 * width * rank
    pass_flops = 2 * rows * width * rank

    offsets = lax.broadcasted_iota(jnp.int32, (ex_dev, SLOT), 1)
    live = (offsets < lengths[:, None]).astype(f32).reshape(1, tok_dev)

    def through(turn, arrived, before):
        return call(
            functools.partial(through_kernel, turn),
            (arrived, before, *down, expand),
            "vvvvv",
            [(before.shape, bf16), (arrived.shape, bf16)],
            flops=2 * pass_flops,
            moved=weight_bytes,
        )

    head = width // PARTS
    expand, first, raised, own = call(
        prime_kernel,
        (inner_cols[0], value_rows[0], adapter_expand[0], adapter_down[0]),
        "hhhh",
        [
            ((rank, width), bf16),
            ((head, rank), bf16),
            ((count, width), bf16),
            ((rows, width), bf16),
        ],
        [
            VMEM(inner_cols.shape[1:], bf16),
            VMEM((q_dev, width), bf16),
            pltpu.SemaphoreType.DMA((2,)),
            pltpu.SemaphoreType.DMA((PARTS + 1,)),
        ],
        flops=pass_flops,
        moved=2 * weight_bytes,
    )

    arrived = upward(own, 0, 1, 2)
    (source,) = tie([adapter_down[0]], own)
    (rest,) = call(
        keep_kernel,
        (source,),
        "h",
        [((width - head, rank), bf16)],
        [pltpu.SemaphoreType.DMA],
        moved=2 * weight_bytes,
    )
    arrived, rest = lax.optimization_barrier((arrived, rest))
    down = (first, rest)
    lower_ranks, leaving = through(1, arrived, jnp.zeros((rows, rank), bf16))
    moving = jnp.concatenate([leaving, own])

    cut = tok_dev * 5 // 8

    def lift(start, end, token):
        (cot,) = tie([cotangent], token)
        return call(
            functools.partial(lift_kernel, start),
            (cot, expand),
            "hv",
            [((end - start, rank), bf16)],
            [
                VMEM((end - start, width), bf16),
                VMEM((end - start, rank), f32),
                pltpu.SemaphoreType.DMA((PARTS,)),
            ],
            flops=2 * (end - start) * width * rank,
            moved=weight_bytes,
        )[0]

    arrived = upward(moving, 1, 1, 2)
    wide = tie([value_rows[0], input_rows[0]], moving)
    wide = spread(jnp.concatenate(wide), "dp")
    lifted = [lift(0, cut, moving)]
    arrived, lifted[0] = lax.optimization_barrier((arrived, lifted[0]))

    slots = []
    empty = jnp.zeros((2 * rows, rank), bf16)
    for slot in range(1, chips):
        found, leaving = through(0, arrived, empty)
        arrived = upward(leaving, 2 * slot, 1, 2)
        if slot == 1:
            (hid,) = tie([hidden_cols[0]], leaving)
            (hidden,) = call(
                functools.partial(hidden_kernel, q_dev),
                (hid, *down),
                "hvv",
                [((count, width), bf16)],
                [VMEM(hidden_cols.shape[1:], bf16), pltpu.SemaphoreType.DMA((1,))],
                flops=2 * count * width * rank,
                moved=weight_bytes,
            )
            wide = jnp.concatenate(tie(wide, hidden))
            arrived, wide = lax.optimization_barrier((arrived, wide))
        if slot == 2:
            (cot,) = tie([cotangent], leaving)
            right = dot_nt(right_rows, cot)
            arrived, right, *left_up = lax.optimization_barrier((arrived, right, *left_up))
        if slot == top:
            others = swap(jnp.stack(tie(left_up, leaving)), "pipe", 1)
            arrived, others = lax.optimization_barrier((arrived, others))
            break
        found, leaving = through(1, arrived, found)
        slots.append(found)
        arrived = upward(leaving, 2 * slot + 1, 1, 2)
        if slot == 1:
            left_rows, right_rows = call(
                functools.partial(weave_kernel, q_dev),
                (hidden, wide, raised),
                "vvv",
                [((count, width), bf16), ((count, width), bf16)],
                flops=2 * count * width,
                moved=weight_bytes // 2,
            )
            left = dot_nt(left_rows, activations[0]) * live
            left_own = left.astype(bf16)
            left_up = [left_own] + [upward(left_own, 0, 2 * hop, 1) for hop in range(1, chips)]
            arrived, left_own = lax.optimization_barrier((arrived, left_own))
        if slot == top - 1:
            (early,) = tie([jnp.concatenate([lower_ranks] + slots)], leaving)
            early = spread(early, "dp")
            lifted.append(lift(cut, tok_dev, leaving))
            arrived, lifted[1], *early = lax.optimization_barrier((arrived, lifted[1], *early))

    (late,) = call(
        last_kernel,
        (arrived, found, *down),
        "vvvv",
        [((2 * rows, rank), bf16)],
        flops=pass_flops,
        moved=weight_bytes,
    )
    (right,) = tie([right], late)
    (sums,) = call(
        functools.partial(early_kernel, chips, rows),
        (left, right, others, *lifted, *left_up, *early),
        "v" * (5 + chips + columns),
        [((max(ex_dev, 8), count), f32)],
        flops=2 * count * rank * tok_dev * (2 * chips),
        moved=weight_bytes,
    )
    late = spread(late, "dp")
    (sums,) = call(
        functools.partial(late_kernel, chips, rows),
        (left_up[-1], others, sums, *lifted, *late),
        "v" * (5 + columns),
        [(sums.shape, f32)],
        flops=2 * count * rank * tok_dev * 2,
        moved=weight_bytes // 8,
    )
    sums = sums + swap(sums, "pipe", 1)
    parts = [sums] + [around(sums, hop) for hop in range(1, chips)]
    (scores,) = call(
        functools.partial(final_kernel, q_dev),
        (query_example[None], *parts),
        "v" * (1 + chips),
        [((ex_dev, columns * q_dev), f32)],
        kept=jax.ShapeDtypeStruct,
    )
    return scores


def solution(mesh):
    in_specs = (
        P("pipe", "dp", None),
        P("dp", None),
        P("pipe", None, None),
        P("pipe", None, None),
        P("pipe", "dp", None),
        P("pipe", "dp", None),
        P("pipe", None, None),
        P("pipe", None, None),
        P("dp"),
        P(),
    )
    out_specs = P("dp", None)
    return jax.shard_map(local, mesh=mesh, in_specs=in_specs, out_specs=out_specs, check_vma=False)
```

```python
import functools

import jax
import jax.numpy as jnp
from jax import lax
from jax.experimental import pallas as pl
from jax.experimental.pallas import tpu as pltpu
from jax.sharding import PartitionSpec as P

SLOT = 128
PARTS = 4
AHEAD = 3


adapter_scale = 0.25
bf16 = jnp.bfloat16
f32 = jnp.float32
VMEM = pltpu.VMEM


def dot_nn(a, b, precision=None):
    return lax.dot_general(
        a, b, (((1,), (0,)), ((), ())), preferred_element_type=f32, precision=precision
    )


def dot_nt(a, b, precision=None):
    return lax.dot_general(
        a, b, (((1,), (1,)), ((), ())), preferred_element_type=f32, precision=precision
    )


def swap(value, axis, distance):
    count = lax.axis_size(axis)
    return lax.ppermute(value, axis, [(source, source ^ distance) for source in range(count)])


def spread(value, axis):
    far = [swap(value, axis, d) for d in reversed(range(1, lax.axis_size(axis)))]
    return [value] + far[::-1]


def upward(value, first, hop, stride):
    count = lax.axis_size("pipe")
    return lax.ppermute(
        value, "pipe", [(source, source + hop) for source in range(first, count - hop, stride)]
    )


def around(value, hop):
    count = lax.axis_size("pipe")
    return lax.ppermute(
        value, "pipe", [(source, (source + 2 * hop) % count) for source in range(count)]
    )


def tie(values, token):
    *values, _ = lax.optimization_barrier((*values, token))
    return values


def call(kernel, operands, places, outs, scratch=(), flops=0, moved=0, kept=VMEM):
    space = {"v": VMEM, "s": pltpu.SMEM, "h": pltpu.HBM}
    operands = [
        x if place == "s" else pltpu.with_memory_space_constraint(x, space[place])
        for x, place in zip(operands, places)
    ]
    return pl.pallas_call(
        kernel,
        in_specs=[pl.BlockSpec(memory_space=space[place]) for place in places],
        out_specs=[pl.BlockSpec(memory_space=VMEM) for _ in outs],
        out_shape=[kept(shape, dtype) for shape, dtype in outs],
        scratch_shapes=list(scratch),
        cost_estimate=pl.CostEstimate(flops=flops, bytes_accessed=moved, transcendentals=0),
        compiler_params=pltpu.CompilerParams(vmem_limit_bytes=16 * 2**20),
    )(*operands)


def picks(shape, q_dev, place):
    row = lax.broadcasted_iota(jnp.int32, shape, 0)
    query = lax.broadcasted_iota(jnp.int32, shape, 1)
    block = lax.axis_index("dp") ^ (row // (2 * q_dev))
    wanted = block * q_dev + row % q_dev
    found = (query == wanted) & ((row // q_dev) % 2 == place)
    return jnp.where(found, 1.0, 0.0)


def fetch(pairs, sems):
    return [
        pltpu.make_async_copy(source, target, sems.at[at])
        for at, (source, target) in enumerate(pairs)
    ]


def begin(copies):
    for copy in copies[:AHEAD]:
        copy.start()


def arrive(copies, part):
    copies[part].wait()
    if part + AHEAD < len(copies):
        copies[part + AHEAD].start()


def prime_kernel(
    cols_hbm, values_hbm, expand, down, kept, head, raised, own, cols, values, few, sems
):
    step = expand.shape[1] // PARTS
    small = fetch([(cols_hbm, cols), (values_hbm, values)], few)
    begin(small)
    spans = [pl.ds(part * step, step) for part in range(PARTS)]
    pairs = [(expand.at[:, span], kept.at[:, span]) for span in spans]
    copies = fetch(pairs + [(down.at[pl.ds(0, head.shape[0])], head)], sems)
    begin(copies)
    rows = own.shape[0]
    q_dev = rows // 2
    laid = picks((raised.shape[0], cols.shape[0]), q_dev, 1).astype(bf16)
    for copy in small:
        copy.wait()
    laid = dot_nn(laid, cols[...]).astype(bf16)
    for part in range(PARTS):
        span = slice(part * step, (part + 1) * step)
        arrive(copies, part)
        found = adapter_scale * dot_nn(laid, kept[:, span])
        raised[:, span] = found.astype(bf16)
        above = jnp.concatenate([values[:, span].astype(f32), found[q_dev:rows]])
        own[:, span] = above.astype(bf16)
    arrive(copies, PARTS)


def keep_kernel(down, rest, sem):
    count = rest.shape[0]
    copy = pltpu.make_async_copy(down.at[pl.ds(down.shape[0] - count, count)], rest, sem)
    copy.start()
    copy.wait()


def down_rows(head, rest, at, count):
    if at < head.shape[0]:
        return head[at : at + count, :]
    return rest[at - head.shape[0] : at - head.shape[0] + count, :]


def hidden_kernel(q_dev, cols_hbm, head, rest, raised, cols, few):
    step = raised.shape[1] // PARTS
    small = fetch([(cols_hbm, cols)], few)
    begin(small)
    laid = picks((raised.shape[0], cols.shape[0]), q_dev, 0).astype(bf16)
    small[0].wait()
    laid = dot_nn(laid, cols[...]).astype(bf16)
    for part in range(PARTS):
        span = slice(part * step, (part + 1) * step)
        raised[:, span] = (adapter_scale * dot_nt(laid, down_rows(head, rest, part * step, step))).astype(bf16)


def on_turn(core, slot):
    layer = lax.axis_index("pipe")
    return jnp.logical_and(layer % 2 == core, layer // 2 >= slot)


def through_kernel(core, slot, arrived, before, head, rest, expand, ranks, leaving):
    depth = arrived.shape[1]
    step = 2 * ranks.shape[1]
    mine = on_turn(core, slot)

    @pl.when(jnp.logical_not(mine))
    def _():
        ranks[...] = before[...]

    @pl.when(mine)
    def _():
        total = jnp.zeros(ranks.shape, f32)
        for at in range(0, depth, step):
            total += dot_nn(arrived[:, at : at + step], down_rows(head, rest, at, step))
        found = total.astype(bf16)
        ranks[...] = found
        for at in range(0, depth, step):
            more = adapter_scale * dot_nn(found, expand[:, at : at + step])
            leaving[:, at : at + step] = (arrived[:, at : at + step].astype(f32) + more).astype(bf16)


def last_kernel(slot, arrived, before, head, rest, ranks):
    depth = arrived.shape[1]
    step = 2 * ranks.shape[1]
    mine = on_turn(1, slot)

    @pl.when(jnp.logical_not(mine))
    def _():
        ranks[...] = before[...]

    @pl.when(mine)
    def _():
        total = jnp.zeros(ranks.shape, f32)
        for at in range(0, depth, step):
            total += dot_nn(arrived[:, at : at + step], down_rows(head, rest, at, step))
        ranks[...] = total.astype(bf16)


def lift_kernel(start, cotangent, expand, lifted, buffer, total, sems):
    count, depth = buffer.shape
    parts = PARTS
    step = depth // parts
    spans = [pl.ds(part * step, step) for part in range(parts)]
    rows = pl.ds(start, count)
    copies = fetch([(cotangent.at[rows, span], buffer.at[:, span]) for span in spans], sems)
    begin(copies)
    for part in range(parts):
        span = slice(part * step, (part + 1) * step)
        arrive(copies, part)
        found = dot_nt(buffer[:, span], expand[:, span])
        if part == 0:
            total[...] = found
        elif part < parts - 1:
            total[...] += found
        else:
            lifted[...] = (adapter_scale * (total[...] + found)).astype(bf16)


def weave_kernel(q_dev, hidden, rows, raised, left_rows, right_rows):
    count, depth = rows.shape
    step = depth // 8
    place = lax.broadcasted_iota(jnp.int32, (count, step), 0) // q_dev
    first = place % 2 == 0
    for at in range(0, depth, step):
        span = slice(at, at + step)
        given = rows[:, span].astype(f32)
        left_rows[:, span] = jnp.where(first, hidden[:, span].astype(f32), given).astype(bf16)
        right_rows[:, span] = jnp.where(first, given, raised[:, span].astype(f32)).astype(bf16)


def summed(terms, shape):
    example = lax.broadcasted_iota(jnp.int32, (shape[0], terms.shape[1]), 0)
    position = lax.broadcasted_iota(jnp.int32, (shape[0], terms.shape[1]), 1)
    ones = jnp.where(position // SLOT == example, 1.0, 0.0)
    return dot_nt(ones, terms, lax.Precision.HIGHEST)


def weighed(weights, blocks, at, rows, lifted):
    ranks = jnp.concatenate([block[at : at + rows, :].astype(f32) for block in blocks])
    ranks = ranks.astype(bf16)
    return weights * jnp.concatenate([dot_nt(ranks, part[...]) for part in lifted], axis=1)


def by_layer(own, other):
    upper = jnp.full(own.shape, lax.axis_index("pipe") % 2, jnp.int32) == 1
    own, other = own.astype(f32), other.astype(f32)
    return jnp.where(upper, other, own), jnp.where(upper, own, other)


def early_kernel(chips, rows, left, right, others, *refs):
    lifted, ups, blocks, sums = refs[:2], refs[2 : 2 + chips], refs[2 + chips : -1], refs[-1]
    terms = left[...] * right[...]
    for slot in range(chips - 1):
        lower, upper = by_layer(ups[slot][...], others[slot])
        if slot == 0:
            terms += weighed(lower, blocks, 0, rows, lifted)
        else:
            at = rows * (2 * slot - 1)
            terms += weighed(lower, blocks, at, rows, lifted)
            terms += weighed(upper, blocks, at + rows, rows, lifted)
    sums[...] = summed(terms, sums.shape)


def late_kernel(chips, rows, own, others, early, *refs):
    lifted, blocks, sums = refs[:2], refs[2:-1], refs[-1]
    lower, upper = by_layer(own[...], others[chips - 1])
    terms = weighed(lower, blocks, 0, rows, lifted)
    terms += weighed(upper, blocks, rows, rows, lifted)
    sums[...] = early[...] + summed(terms, sums.shape)


def final_kernel(q_dev, queries, *refs):
    parts, scores = refs[:-1], refs[-1]
    total = parts[0][...]
    for part in parts[1:]:
        total += part[...]
    ex_dev, q_all = scores.shape
    shape = (total.shape[1], q_all)
    laid = picks(shape, q_dev, 0) + picks(shape, q_dev, 1)
    total = dot_nn(total, laid, lax.Precision.HIGHEST)[:ex_dev]
    example = lax.axis_index("dp") * ex_dev + lax.broadcasted_iota(jnp.int32, scores.shape, 0)
    keep = example != jnp.broadcast_to(queries[...], scores.shape)
    scores[...] = jnp.where(keep, total * SLOT ** (-0.5), 0.0)


def local(
    activations,
    cotangent,
    adapter_down,
    adapter_expand,
    value_rows,
    input_rows,
    hidden_cols,
    inner_cols,
    lengths,
    query_example,
):
    columns = lax.axis_size("dp")
    chips = lax.axis_size("pipe") // 2
    top = chips - 1
    tok_dev = activations.shape[1]
    ex_dev = tok_dev // SLOT
    q_dev = value_rows.shape[1]
    rows = 2 * q_dev
    count = columns * rows
    width, rank = adapter_down.shape[1:]
    weight_bytes = 2 * width * rank
    pass_flops = 2 * rows * width * rank

    offsets = lax.broadcasted_iota(jnp.int32, (ex_dev, SLOT), 1)
    live = (offsets < lengths[:, None]).astype(f32).reshape(1, tok_dev)

    def through(core, slot, arrived, before):
        return call(
            functools.partial(through_kernel, core, slot),
            (arrived, before, *down, expand),
            "vvvvv",
            [(before.shape, bf16), (arrived.shape, bf16)],
            flops=2 * pass_flops,
            moved=weight_bytes,
        )

    head = width // PARTS
    expand, first, raised, own = call(
        prime_kernel,
        (inner_cols[0], value_rows[0], adapter_expand[0], adapter_down[0]),
        "hhhh",
        [
            ((rank, width), bf16),
            ((head, rank), bf16),
            ((count, width), bf16),
            ((rows, width), bf16),
        ],
        [
            VMEM(inner_cols.shape[1:], bf16),
            VMEM((q_dev, width), bf16),
            pltpu.SemaphoreType.DMA((2,)),
            pltpu.SemaphoreType.DMA((PARTS + 1,)),
        ],
        flops=pass_flops,
        moved=2 * weight_bytes,
    )

    arrived = upward(own, 0, 1, 2)
    (source,) = tie([adapter_down[0]], own)
    (rest,) = call(
        keep_kernel,
        (source,),
        "h",
        [((width - head, rank), bf16)],
        [pltpu.SemaphoreType.DMA],
        moved=2 * weight_bytes,
    )
    arrived, rest = lax.optimization_barrier((arrived, rest))
    down = (first, rest)
    lower_ranks, leaving = through(1, 0, arrived, jnp.zeros((rows, rank), bf16))
    moving = jnp.concatenate([leaving, own])

    cut = tok_dev * 5 // 8

    def lift(start, end, token):
        (cot,) = tie([cotangent], token)
        return call(
            functools.partial(lift_kernel, start),
            (cot, expand),
            "hv",
            [((end - start, rank), bf16)],
            [
                VMEM((end - start, width), bf16),
                VMEM((end - start, rank), f32),
                pltpu.SemaphoreType.DMA((PARTS,)),
            ],
            flops=2 * (end - start) * width * rank,
            moved=weight_bytes,
        )[0]

    arrived = upward(moving, 1, 1, 2)
    wide = tie([value_rows[0], input_rows[0]], moving)
    wide = spread(jnp.concatenate(wide), "dp")
    lifted = [lift(0, cut, moving)]
    arrived, lifted[0] = lax.optimization_barrier((arrived, lifted[0]))

    slots = []
    empty = jnp.zeros((2 * rows, rank), bf16)
    for slot in range(1, chips):
        found, leaving = through(0, slot, arrived, empty)
        arrived = upward(leaving, 2 * slot, 1, 2)
        if slot == 1:
            (hid,) = tie([hidden_cols[0]], leaving)
            (hidden,) = call(
                functools.partial(hidden_kernel, q_dev),
                (hid, *down),
                "hvv",
                [((count, width), bf16)],
                [VMEM(hidden_cols.shape[1:], bf16), pltpu.SemaphoreType.DMA((1,))],
                flops=2 * count * width * rank,
                moved=weight_bytes,
            )
            wide = jnp.concatenate(tie(wide, hidden))
            arrived, wide = lax.optimization_barrier((arrived, wide))
        if slot == 2:
            (cot,) = tie([cotangent], leaving)
            right = dot_nt(right_rows, cot)
            arrived, right, *left_up = lax.optimization_barrier((arrived, right, *left_up))
        if slot == top:
            others = swap(jnp.stack(tie(left_up, leaving)), "pipe", 1)
            arrived, others = lax.optimization_barrier((arrived, others))
            break
        found, leaving = through(1, slot, arrived, found)
        slots.append(found)
        arrived = upward(leaving, 2 * slot + 1, 1, 2)
        if slot == 1:
            left_rows, right_rows = call(
                functools.partial(weave_kernel, q_dev),
                (hidden, wide, raised),
                "vvv",
                [((count, width), bf16), ((count, width), bf16)],
                flops=2 * count * width,
                moved=weight_bytes // 2,
            )
            left = dot_nt(left_rows, activations[0]) * live
            left_own = left.astype(bf16)
            left_up = [left_own] + [upward(left_own, 0, 2 * hop, 1) for hop in range(1, chips)]
            arrived, left_own = lax.optimization_barrier((arrived, left_own))
        if slot == top - 1:
            (early,) = tie([jnp.concatenate([lower_ranks] + slots)], leaving)
            early = spread(early, "dp")
            lifted.append(lift(cut, tok_dev, leaving))
            arrived, lifted[1], *early = lax.optimization_barrier((arrived, lifted[1], *early))

    (late,) = call(
        functools.partial(last_kernel, top),
        (arrived, found, *down),
        "vvvv",
        [((2 * rows, rank), bf16)],
        flops=pass_flops,
        moved=weight_bytes,
    )
    (right,) = tie([right], late)
    (sums,) = call(
        functools.partial(early_kernel, chips, rows),
        (left, right, others, *lifted, *left_up, *early),
        "v" * (5 + chips + columns),
        [((max(ex_dev, 8), count), f32)],
        flops=2 * count * rank * tok_dev * (2 * chips),
        moved=weight_bytes,
    )
    late = spread(late, "dp")
    (sums,) = call(
        functools.partial(late_kernel, chips, rows),
        (left_up[-1], others, sums, *lifted, *late),
        "v" * (5 + columns),
        [(sums.shape, f32)],
        flops=2 * count * rank * tok_dev * 2,
        moved=weight_bytes // 8,
    )
    sums = sums + swap(sums, "pipe", 1)
    parts = [sums] + [around(sums, hop) for hop in range(1, chips)]
    (scores,) = call(
        functools.partial(final_kernel, q_dev),
        (query_example[None], *parts),
        "v" * (1 + chips),
        [((ex_dev, columns * q_dev), f32)],
        kept=jax.ShapeDtypeStruct,
    )
    return scores


def solution(mesh):
    in_specs = (
        P("pipe", "dp", None),
        P("dp", None),
        P("pipe", None, None),
        P("pipe", None, None),
        P("pipe", "dp", None),
        P("pipe", "dp", None),
        P("pipe", None, None),
        P("pipe", None, None),
        P("dp"),
        P(),
    )
    out_specs = P("dp", None)
    return jax.shard_map(local, mesh=mesh, in_specs=in_specs, out_specs=out_specs, check_vma=False)
```

```python
import functools

import jax
import jax.numpy as jnp
from jax import lax
from jax.experimental import pallas as pl
from jax.experimental.pallas import tpu as pltpu
from jax.sharding import PartitionSpec as P

SLOT = 128
PARTS = 4
AHEAD = 3


adapter_scale = 0.25
bf16 = jnp.bfloat16
f32 = jnp.float32
VMEM = pltpu.VMEM


def dot_nn(a, b, precision=None):
    return lax.dot_general(
        a, b, (((1,), (0,)), ((), ())), preferred_element_type=f32, precision=precision
    )


def dot_nt(a, b, precision=None):
    return lax.dot_general(
        a, b, (((1,), (1,)), ((), ())), preferred_element_type=f32, precision=precision
    )


def swap(value, axis, distance):
    count = lax.axis_size(axis)
    return lax.ppermute(value, axis, [(source, source ^ distance) for source in range(count)])


def spread(value, axis):
    far = [swap(value, axis, d) for d in reversed(range(1, lax.axis_size(axis)))]
    return [value] + far[::-1]


def upward(value, first, hop, stride):
    count = lax.axis_size("pipe")
    return lax.ppermute(
        value, "pipe", [(source, source + hop) for source in range(first, count - hop, stride)]
    )


def between(value, chips):
    pairs = [(2 * source + core, 2 * target + core) for source, target in chips for core in (0, 1)]
    return lax.ppermute(value, "pipe", pairs)


def tie(values, token):
    *values, _ = lax.optimization_barrier((*values, token))
    return values


def call(kernel, operands, places, outs, scratch=(), flops=0, moved=0, kept=VMEM):
    space = {"v": VMEM, "s": pltpu.SMEM, "h": pltpu.HBM}
    operands = [
        x if place == "s" else pltpu.with_memory_space_constraint(x, space[place])
        for x, place in zip(operands, places)
    ]
    return pl.pallas_call(
        kernel,
        in_specs=[pl.BlockSpec(memory_space=space[place]) for place in places],
        out_specs=[pl.BlockSpec(memory_space=VMEM) for _ in outs],
        out_shape=[kept(shape, dtype) for shape, dtype in outs],
        scratch_shapes=list(scratch),
        cost_estimate=pl.CostEstimate(flops=flops, bytes_accessed=moved, transcendentals=0),
        compiler_params=pltpu.CompilerParams(vmem_limit_bytes=16 * 2**20),
    )(*operands)


def picks(shape, q_dev, place):
    row = lax.broadcasted_iota(jnp.int32, shape, 0)
    query = lax.broadcasted_iota(jnp.int32, shape, 1)
    block = lax.axis_index("dp") ^ (row // (2 * q_dev))
    wanted = block * q_dev + row % q_dev
    found = (query == wanted) & ((row // q_dev) % 2 == place)
    return jnp.where(found, 1.0, 0.0)


def fetch(pairs, sems):
    return [
        pltpu.make_async_copy(source, target, sems.at[at])
        for at, (source, target) in enumerate(pairs)
    ]


def begin(copies):
    for copy in copies[:AHEAD]:
        copy.start()


def arrive(copies, part):
    copies[part].wait()
    if part + AHEAD < len(copies):
        copies[part + AHEAD].start()


def prime_kernel(
    cols_hbm, values_hbm, expand, down, kept, head, raised, own, cols, values, few, sems
):
    step = expand.shape[1] // PARTS
    small = fetch([(cols_hbm, cols), (values_hbm, values)], few)
    begin(small)
    spans = [pl.ds(part * step, step) for part in range(PARTS)]
    pairs = [(expand.at[:, span], kept.at[:, span]) for span in spans]
    copies = fetch(pairs + [(down.at[pl.ds(0, head.shape[0])], head)], sems)
    begin(copies)
    rows = own.shape[0]
    q_dev = rows // 2
    laid = picks((raised.shape[0], cols.shape[0]), q_dev, 1).astype(bf16)
    for copy in small:
        copy.wait()
    laid = dot_nn(laid, cols[...]).astype(bf16)
    for part in range(PARTS):
        span = slice(part * step, (part + 1) * step)
        arrive(copies, part)
        found = adapter_scale * dot_nn(laid, kept[:, span])
        raised[:, span] = found.astype(bf16)
        above = jnp.concatenate([values[:, span].astype(f32), found[q_dev:rows]])
        own[:, span] = above.astype(bf16)
    arrive(copies, PARTS)


def keep_kernel(down, rest, sem):
    count = rest.shape[0]
    copy = pltpu.make_async_copy(down.at[pl.ds(down.shape[0] - count, count)], rest, sem)
    copy.start()
    copy.wait()


def down_rows(head, rest, at, count):
    if at < head.shape[0]:
        return head[at : at + count, :]
    return rest[at - head.shape[0] : at - head.shape[0] + count, :]


def hidden_kernel(q_dev, cols_hbm, head, rest, raised, cols, few):
    step = raised.shape[1] // PARTS
    small = fetch([(cols_hbm, cols)], few)
    begin(small)
    laid = picks((raised.shape[0], cols.shape[0]), q_dev, 0).astype(bf16)
    small[0].wait()
    laid = dot_nn(laid, cols[...]).astype(bf16)
    for part in range(PARTS):
        span = slice(part * step, (part + 1) * step)
        raised[:, span] = (adapter_scale * dot_nt(laid, down_rows(head, rest, part * step, step))).astype(bf16)


def on_turn(core, slot):
    layer = lax.axis_index("pipe")
    return jnp.logical_and(layer % 2 == core, layer // 2 >= slot)


def through_kernel(core, slot, arrived, before, head, rest, expand, ranks, leaving):
    depth = arrived.shape[1]
    step = 2 * ranks.shape[1]
    mine = on_turn(core, slot)

    @pl.when(jnp.logical_not(mine))
    def _():
        ranks[...] = before[...]

    @pl.when(mine)
    def _():
        total = jnp.zeros(ranks.shape, f32)
        for at in range(0, depth, step):
            total += dot_nn(arrived[:, at : at + step], down_rows(head, rest, at, step))
        found = total.astype(bf16)
        ranks[...] = found
        for at in range(0, depth, step):
            more = adapter_scale * dot_nn(found, expand[:, at : at + step])
            leaving[:, at : at + step] = (arrived[:, at : at + step].astype(f32) + more).astype(bf16)


def last_kernel(slot, arrived, before, head, rest, ranks):
    depth = arrived.shape[1]
    step = 2 * ranks.shape[1]
    mine = on_turn(1, slot)

    @pl.when(jnp.logical_not(mine))
    def _():
        ranks[...] = before[...]

    @pl.when(mine)
    def _():
        total = jnp.zeros(ranks.shape, f32)
        for at in range(0, depth, step):
            total += dot_nn(arrived[:, at : at + step], down_rows(head, rest, at, step))
        ranks[...] = total.astype(bf16)


def lift_kernel(start, cotangent, expand, lifted, buffer, total, sems):
    count, depth = buffer.shape
    parts = PARTS
    step = depth // parts
    spans = [pl.ds(part * step, step) for part in range(parts)]
    rows = pl.ds(start, count)
    copies = fetch([(cotangent.at[rows, span], buffer.at[:, span]) for span in spans], sems)
    begin(copies)
    for part in range(parts):
        span = slice(part * step, (part + 1) * step)
        arrive(copies, part)
        found = dot_nt(buffer[:, span], expand[:, span])
        if part == 0:
            total[...] = found
        elif part < parts - 1:
            total[...] += found
        else:
            lifted[...] = (adapter_scale * (total[...] + found)).astype(bf16)


def weave_kernel(q_dev, hidden, rows, raised, left_rows, right_rows):
    count, depth = rows.shape
    step = depth // 8
    place = lax.broadcasted_iota(jnp.int32, (count, step), 0) // q_dev
    first = place % 2 == 0
    for at in range(0, depth, step):
        span = slice(at, at + step)
        given = rows[:, span].astype(f32)
        left_rows[:, span] = jnp.where(first, hidden[:, span].astype(f32), given).astype(bf16)
        right_rows[:, span] = jnp.where(first, given, raised[:, span].astype(f32)).astype(bf16)


def summed(terms, shape):
    example = lax.broadcasted_iota(jnp.int32, (shape[0], terms.shape[1]), 0)
    position = lax.broadcasted_iota(jnp.int32, (shape[0], terms.shape[1]), 1)
    ones = jnp.where(position // SLOT == example, 1.0, 0.0)
    return dot_nt(ones, terms, lax.Precision.HIGHEST)


def weighed(weights, blocks, at, rows, lifted):
    ranks = jnp.concatenate([block[at : at + rows, :].astype(f32) for block in blocks])
    ranks = ranks.astype(bf16)
    return weights * jnp.concatenate([dot_nt(ranks, part[...]) for part in lifted], axis=1)


def by_layer(own, other):
    upper = jnp.full(own.shape, lax.axis_index("pipe") % 2, jnp.int32) == 1
    own, other = own.astype(f32), other.astype(f32)
    return jnp.where(upper, other, own), jnp.where(upper, own, other)


def early_kernel(chips, rows, left, right, others, *refs):
    lifted, ups, blocks, sums = refs[:2], refs[2 : 2 + chips], refs[2 + chips : -1], refs[-1]
    terms = left[...] * right[...]
    for slot in range(chips - 1):
        lower, upper = by_layer(ups[slot][...], others[slot])
        if slot == 0:
            terms += weighed(lower, blocks, 0, rows, lifted)
        else:
            at = rows * (2 * slot - 1)
            terms += weighed(lower, blocks, at, rows, lifted)
            terms += weighed(upper, blocks, at + rows, rows, lifted)
    sums[...] = summed(terms, sums.shape)


def late_kernel(chips, rows, own, others, early, *refs):
    lifted, blocks, sums = refs[:2], refs[2:-1], refs[-1]
    lower, upper = by_layer(own[...], others[chips - 1])
    terms = weighed(lower, blocks, 0, rows, lifted)
    terms += weighed(upper, blocks, rows, rows, lifted)
    sums[...] = early[...] + summed(terms, sums.shape)


def final_kernel(q_dev, queries, *refs):
    parts, scores = refs[:-1], refs[-1]
    total = parts[0][...]
    for part in parts[1:]:
        total += part[...]
    ex_dev, q_all = scores.shape
    shape = (total.shape[1], q_all)
    laid = picks(shape, q_dev, 0) + picks(shape, q_dev, 1)
    total = dot_nn(total, laid, lax.Precision.HIGHEST)[:ex_dev]
    example = lax.axis_index("dp") * ex_dev + lax.broadcasted_iota(jnp.int32, scores.shape, 0)
    keep = example != jnp.broadcast_to(queries[...], scores.shape)
    scores[...] = jnp.where(keep, total * SLOT ** (-0.5), 0.0)


def local(
    activations,
    cotangent,
    adapter_down,
    adapter_expand,
    value_rows,
    input_rows,
    hidden_cols,
    inner_cols,
    lengths,
    query_example,
):
    columns = lax.axis_size("dp")
    chips = lax.axis_size("pipe") // 2
    top = chips - 1
    tok_dev = activations.shape[1]
    ex_dev = tok_dev // SLOT
    q_dev = value_rows.shape[1]
    rows = 2 * q_dev
    count = columns * rows
    width, rank = adapter_down.shape[1:]
    weight_bytes = 2 * width * rank
    pass_flops = 2 * rows * width * rank

    offsets = lax.broadcasted_iota(jnp.int32, (ex_dev, SLOT), 1)
    live = (offsets < lengths[:, None]).astype(f32).reshape(1, tok_dev)

    def through(core, slot, arrived, before):
        return call(
            functools.partial(through_kernel, core, slot),
            (arrived, before, *down, expand),
            "vvvvv",
            [(before.shape, bf16), (arrived.shape, bf16)],
            flops=2 * pass_flops,
            moved=weight_bytes,
        )

    head = width // PARTS
    expand, first, raised, own = call(
        prime_kernel,
        (inner_cols[0], value_rows[0], adapter_expand[0], adapter_down[0]),
        "hhhh",
        [
            ((rank, width), bf16),
            ((head, rank), bf16),
            ((count, width), bf16),
            ((rows, width), bf16),
        ],
        [
            VMEM(inner_cols.shape[1:], bf16),
            VMEM((q_dev, width), bf16),
            pltpu.SemaphoreType.DMA((2,)),
            pltpu.SemaphoreType.DMA((PARTS + 1,)),
        ],
        flops=pass_flops,
        moved=2 * weight_bytes,
    )

    arrived = upward(own, 0, 1, 2)
    (source,) = tie([adapter_down[0]], own)
    (rest,) = call(
        keep_kernel,
        (source,),
        "h",
        [((width - head, rank), bf16)],
        [pltpu.SemaphoreType.DMA],
        moved=2 * weight_bytes,
    )
    arrived, rest = lax.optimization_barrier((arrived, rest))
    down = (first, rest)
    lower_ranks, leaving = through(1, 0, arrived, jnp.zeros((rows, rank), bf16))
    moving = jnp.concatenate([leaving, own])

    cut = tok_dev * 5 // 8

    def lift(start, end, token):
        (cot,) = tie([cotangent], token)
        return call(
            functools.partial(lift_kernel, start),
            (cot, expand),
            "hv",
            [((end - start, rank), bf16)],
            [
                VMEM((end - start, width), bf16),
                VMEM((end - start, rank), f32),
                pltpu.SemaphoreType.DMA((PARTS,)),
            ],
            flops=2 * (end - start) * width * rank,
            moved=weight_bytes,
        )[0]

    arrived = upward(moving, 1, 1, 2)
    wide = tie([value_rows[0], input_rows[0]], moving)
    wide = spread(jnp.concatenate(wide), "dp")
    lifted = [lift(0, cut, moving)]
    arrived, lifted[0] = lax.optimization_barrier((arrived, lifted[0]))

    slots = []
    empty = jnp.zeros((2 * rows, rank), bf16)
    for slot in range(1, chips):
        found, leaving = through(0, slot, arrived, empty)
        arrived = upward(leaving, 2 * slot, 1, 2)
        if slot == 1:
            (hid,) = tie([hidden_cols[0]], leaving)
            (hidden,) = call(
                functools.partial(hidden_kernel, q_dev),
                (hid, *down),
                "hvv",
                [((count, width), bf16)],
                [VMEM(hidden_cols.shape[1:], bf16), pltpu.SemaphoreType.DMA((1,))],
                flops=2 * count * width * rank,
                moved=weight_bytes,
            )
            wide = jnp.concatenate(tie(wide, hidden))
            arrived, wide = lax.optimization_barrier((arrived, wide))
        if slot == 2:
            (cot,) = tie([cotangent], leaving)
            right = dot_nt(right_rows, cot)
            arrived, right, *left_up = lax.optimization_barrier((arrived, right, *left_up))
        if slot == top:
            others = swap(jnp.stack(tie(left_up, leaving)), "pipe", 1)
            arrived, others = lax.optimization_barrier((arrived, others))
            break
        found, leaving = through(1, slot, arrived, found)
        slots.append(found)
        arrived = upward(leaving, 2 * slot + 1, 1, 2)
        if slot == 1:
            left_rows, right_rows = call(
                functools.partial(weave_kernel, q_dev),
                (hidden, wide, raised),
                "vvv",
                [((count, width), bf16), ((count, width), bf16)],
                flops=2 * count * width,
                moved=weight_bytes // 2,
            )
            left = dot_nt(left_rows, activations[0]) * live
            left_own = left.astype(bf16)
            left_up = [left_own] + [upward(left_own, 0, 2 * hop, 1) for hop in range(1, chips)]
            arrived, left_own = lax.optimization_barrier((arrived, left_own))
        if slot == top - 1:
            (early,) = tie([jnp.concatenate([lower_ranks] + slots)], leaving)
            early = spread(early, "dp")
            lifted.append(lift(cut, tok_dev, leaving))
            arrived, lifted[1], *early = lax.optimization_barrier((arrived, lifted[1], *early))

    (late,) = call(
        functools.partial(last_kernel, top),
        (arrived, found, *down),
        "vvvv",
        [((2 * rows, rank), bf16)],
        flops=pass_flops,
        moved=weight_bytes,
    )
    (right,) = tie([right], late)
    (sums,) = call(
        functools.partial(early_kernel, chips, rows),
        (left, right, others, *lifted, *left_up, *early),
        "v" * (5 + chips + columns),
        [((max(ex_dev, 8), count), f32)],
        flops=2 * count * rank * tok_dev * (2 * chips),
        moved=weight_bytes,
    )
    late = spread(late, "dp")
    (sums,) = call(
        functools.partial(late_kernel, chips, rows),
        (left_up[-1], others, sums, *lifted, *late),
        "v" * (5 + columns),
        [(sums.shape, f32)],
        flops=2 * count * rank * tok_dev * 2,
        moved=weight_bytes // 8,
    )
    sums = sums + swap(sums, "pipe", 1)
    below = [between(sums, [(z, (z + hop) % top) for z in range(top)]) for hop in range(1, top)]
    for part in below:
        sums = sums + part
    crossing = [[(top, z)] for z in range(top)]
    crossing[-1].append((top - 1, top))
    parts = [sums] + [between(sums, chosen) for chosen in crossing]
    (scores,) = call(
        functools.partial(final_kernel, q_dev),
        (query_example[None], *parts),
        "v" * (1 + len(parts)),
        [((ex_dev, columns * q_dev), f32)],
        kept=jax.ShapeDtypeStruct,
    )
    return scores


def solution(mesh):
    in_specs = (
        P("pipe", "dp", None),
        P("dp", None),
        P("pipe", None, None),
        P("pipe", None, None),
        P("pipe", "dp", None),
        P("pipe", "dp", None),
        P("pipe", None, None),
        P("pipe", None, None),
        P("dp"),
        P(),
    )
    out_specs = P("dp", None)
    return jax.shard_map(local, mesh=mesh, in_specs=in_specs, out_specs=out_specs, check_vma=False)
```

```python
import functools

import jax
import jax.numpy as jnp
from jax import lax
from jax.experimental import pallas as pl
from jax.experimental.pallas import tpu as pltpu
from jax.sharding import PartitionSpec as P

SLOT = 128
PARTS = 4
AHEAD = 3


adapter_scale = 0.25
bf16 = jnp.bfloat16
f32 = jnp.float32
VMEM = pltpu.VMEM


def dot_nn(a, b, precision=None):
    return lax.dot_general(
        a, b, (((1,), (0,)), ((), ())), preferred_element_type=f32, precision=precision
    )


def dot_nt(a, b, precision=None):
    return lax.dot_general(
        a, b, (((1,), (1,)), ((), ())), preferred_element_type=f32, precision=precision
    )


def swap(value, axis, distance):
    count = lax.axis_size(axis)
    return lax.ppermute(value, axis, [(source, source ^ distance) for source in range(count)])


def spread(value, axis):
    far = [swap(value, axis, d) for d in reversed(range(1, lax.axis_size(axis)))]
    return [value] + far[::-1]


def upward(value, first, hop, stride):
    count = lax.axis_size("pipe")
    return lax.ppermute(
        value, "pipe", [(source, source + hop) for source in range(first, count - hop, stride)]
    )


def between(value, chips):
    pairs = [(2 * source + core, 2 * target + core) for source, target in chips for core in (0, 1)]
    return lax.ppermute(value, "pipe", pairs)


def tie(values, token):
    *values, _ = lax.optimization_barrier((*values, token))
    return values


def call(kernel, operands, places, outs, scratch=(), flops=0, moved=0, kept=VMEM):
    space = {"v": VMEM, "s": pltpu.SMEM, "h": pltpu.HBM}
    operands = [
        x if place == "s" else pltpu.with_memory_space_constraint(x, space[place])
        for x, place in zip(operands, places)
    ]
    return pl.pallas_call(
        kernel,
        in_specs=[pl.BlockSpec(memory_space=space[place]) for place in places],
        out_specs=[pl.BlockSpec(memory_space=VMEM) for _ in outs],
        out_shape=[kept(shape, dtype) for shape, dtype in outs],
        scratch_shapes=list(scratch),
        cost_estimate=pl.CostEstimate(flops=flops, bytes_accessed=moved, transcendentals=0),
        compiler_params=pltpu.CompilerParams(vmem_limit_bytes=16 * 2**20),
    )(*operands)


def picks(shape, q_dev, place):
    row = lax.broadcasted_iota(jnp.int32, shape, 0)
    query = lax.broadcasted_iota(jnp.int32, shape, 1)
    block = lax.axis_index("dp") ^ (row // (2 * q_dev))
    wanted = block * q_dev + row % q_dev
    found = (query == wanted) & ((row // q_dev) % 2 == place)
    return jnp.where(found, 1.0, 0.0)


def fetch(pairs, sems):
    return [
        pltpu.make_async_copy(source, target, sems.at[at])
        for at, (source, target) in enumerate(pairs)
    ]


def begin(copies):
    for copy in copies[:AHEAD]:
        copy.start()


def arrive(copies, part):
    copies[part].wait()
    if part + AHEAD < len(copies):
        copies[part + AHEAD].start()


def prime_kernel(
    cols_hbm, values_hbm, expand, down, kept, head, raised, own, cols, values, few, sems
):
    step = expand.shape[1] // PARTS
    small = fetch([(cols_hbm, cols), (values_hbm, values)], few)
    begin(small)
    spans = [pl.ds(part * step, step) for part in range(PARTS)]
    pairs = [(expand.at[:, span], kept.at[:, span]) for span in spans]
    copies = fetch(pairs + [(down.at[pl.ds(0, head.shape[0])], head)], sems)
    begin(copies)
    rows = own.shape[0]
    q_dev = rows // 2
    laid = picks((raised.shape[0], cols.shape[0]), q_dev, 1).astype(bf16)
    for copy in small:
        copy.wait()
    laid = dot_nn(laid, cols[...]).astype(bf16)
    for part in range(PARTS):
        span = slice(part * step, (part + 1) * step)
        arrive(copies, part)
        found = adapter_scale * dot_nn(laid, kept[:, span])
        raised[:, span] = found.astype(bf16)
        above = jnp.concatenate([values[:, span].astype(f32), found[q_dev:rows]])
        own[:, span] = above.astype(bf16)
    arrive(copies, PARTS)


def keep_kernel(down, rest, sem):
    count = rest.shape[0]
    copy = pltpu.make_async_copy(down.at[pl.ds(down.shape[0] - count, count)], rest, sem)
    copy.start()
    copy.wait()


def down_rows(head, rest, at, count):
    if at < head.shape[0]:
        return head[at : at + count, :]
    return rest[at - head.shape[0] : at - head.shape[0] + count, :]


def hidden_kernel(q_dev, cols_hbm, head, rest, raised, cols, few):
    step = raised.shape[1] // PARTS
    small = fetch([(cols_hbm, cols)], few)
    begin(small)
    laid = picks((raised.shape[0], cols.shape[0]), q_dev, 0).astype(bf16)
    small[0].wait()
    laid = dot_nn(laid, cols[...]).astype(bf16)
    for part in range(PARTS):
        span = slice(part * step, (part + 1) * step)
        raised[:, span] = (adapter_scale * dot_nt(laid, down_rows(head, rest, part * step, step))).astype(bf16)


def on_turn(core, slot):
    layer = lax.axis_index("pipe")
    return jnp.logical_and(layer % 2 == core, layer // 2 >= slot)


def through_kernel(core, slot, arrived, before, head, rest, expand, ranks, leaving):
    depth = arrived.shape[1]
    step = 2 * ranks.shape[1]
    mine = on_turn(core, slot)

    @pl.when(jnp.logical_not(mine))
    def _():
        ranks[...] = before[...]

    @pl.when(mine)
    def _():
        total = jnp.zeros(ranks.shape, f32)
        for at in range(0, depth, step):
            total += dot_nn(arrived[:, at : at + step], down_rows(head, rest, at, step))
        found = total.astype(bf16)
        ranks[...] = found
        for at in range(0, depth, step):
            more = adapter_scale * dot_nn(found, expand[:, at : at + step])
            leaving[:, at : at + step] = (arrived[:, at : at + step].astype(f32) + more).astype(bf16)


def last_kernel(slot, arrived, before, head, rest, ranks):
    depth = arrived.shape[1]
    step = 2 * ranks.shape[1]
    mine = on_turn(1, slot)

    @pl.when(jnp.logical_not(mine))
    def _():
        ranks[...] = before[...]

    @pl.when(mine)
    def _():
        total = jnp.zeros(ranks.shape, f32)
        for at in range(0, depth, step):
            total += dot_nn(arrived[:, at : at + step], down_rows(head, rest, at, step))
        ranks[...] = total.astype(bf16)


def lift_kernel(start, cotangent, expand, lifted, buffer, total, sems):
    count, depth = buffer.shape
    parts = PARTS
    step = depth // parts
    spans = [pl.ds(part * step, step) for part in range(parts)]
    rows = pl.ds(start, count)
    copies = fetch([(cotangent.at[rows, span], buffer.at[:, span]) for span in spans], sems)
    begin(copies)
    for part in range(parts):
        span = slice(part * step, (part + 1) * step)
        arrive(copies, part)
        found = dot_nt(buffer[:, span], expand[:, span])
        if part == 0:
            total[...] = found
        elif part < parts - 1:
            total[...] += found
        else:
            lifted[...] = (adapter_scale * (total[...] + found)).astype(bf16)


def weave_kernel(q_dev, hidden, rows, raised, left_rows, right_rows):
    count, depth = rows.shape
    step = depth // 8
    place = lax.broadcasted_iota(jnp.int32, (count, step), 0) // q_dev
    first = place % 2 == 0
    for at in range(0, depth, step):
        span = slice(at, at + step)
        given = rows[:, span].astype(f32)
        left_rows[:, span] = jnp.where(first, hidden[:, span].astype(f32), given).astype(bf16)
        right_rows[:, span] = jnp.where(first, given, raised[:, span].astype(f32)).astype(bf16)


def summed(terms, shape):
    example = lax.broadcasted_iota(jnp.int32, (shape[0], terms.shape[1]), 0)
    position = lax.broadcasted_iota(jnp.int32, (shape[0], terms.shape[1]), 1)
    ones = jnp.where(position // SLOT == example, 1.0, 0.0)
    return dot_nt(ones, terms, lax.Precision.HIGHEST)


def weighed(weights, blocks, at, rows, lifted):
    ranks = jnp.concatenate([block[at : at + rows, :].astype(f32) for block in blocks])
    ranks = ranks.astype(bf16)
    return weights * jnp.concatenate([dot_nt(ranks, part[...]) for part in lifted], axis=1)


def by_layer(own, other):
    upper = jnp.full(own.shape, lax.axis_index("pipe") % 2, jnp.int32) == 1
    own, other = own.astype(f32), other.astype(f32)
    return jnp.where(upper, other, own), jnp.where(upper, own, other)


def early_kernel(chips, rows, left, right, others, *refs):
    lifted, ups, blocks, sums = refs[:2], refs[2 : 2 + chips], refs[2 + chips : -1], refs[-1]
    terms = left[...] * right[...]
    for slot in range(chips - 1):
        lower, upper = by_layer(ups[slot][...], others[slot])
        if slot == 0:
            terms += weighed(lower, blocks, 0, rows, lifted)
        else:
            at = rows * (2 * slot - 1)
            terms += weighed(lower, blocks, at, rows, lifted)
            terms += weighed(upper, blocks, at + rows, rows, lifted)
    sums[...] = summed(terms, sums.shape)


def late_kernel(chips, rows, own, others, early, *refs):
    lifted, blocks, sums = refs[:2], refs[2:-1], refs[-1]
    lower, upper = by_layer(own[...], others[chips - 1])
    terms = weighed(lower, blocks, 0, rows, lifted)
    terms += weighed(upper, blocks, rows, rows, lifted)
    sums[...] = early[...] + summed(terms, sums.shape)


def final_kernel(q_dev, queries, *refs):
    parts, scores = refs[:-1], refs[-1]
    total = parts[0][...]
    for part in parts[1:]:
        total += part[...]
    ex_dev, q_all = scores.shape
    shape = (total.shape[1], q_all)
    laid = picks(shape, q_dev, 0) + picks(shape, q_dev, 1)
    total = dot_nn(total, laid, lax.Precision.HIGHEST)[:ex_dev]
    example = lax.axis_index("dp") * ex_dev + lax.broadcasted_iota(jnp.int32, scores.shape, 0)
    keep = example != jnp.broadcast_to(queries[...], scores.shape)
    scores[...] = jnp.where(keep, total * SLOT ** (-0.5), 0.0)


def local(
    activations,
    cotangent,
    adapter_down,
    adapter_expand,
    value_rows,
    input_rows,
    hidden_cols,
    inner_cols,
    lengths,
    query_example,
):
    columns = lax.axis_size("dp")
    chips = lax.axis_size("pipe") // 2
    top = chips - 1
    tok_dev = activations.shape[1]
    ex_dev = tok_dev // SLOT
    q_dev = value_rows.shape[1]
    rows = 2 * q_dev
    count = columns * rows
    width, rank = adapter_down.shape[1:]
    weight_bytes = 2 * width * rank
    pass_flops = 2 * rows * width * rank

    offsets = lax.broadcasted_iota(jnp.int32, (ex_dev, SLOT), 1)
    live = (offsets < lengths[:, None]).astype(f32).reshape(1, tok_dev)

    def through(core, slot, arrived, before):
        return call(
            functools.partial(through_kernel, core, slot),
            (arrived, before, *down, expand),
            "vvvvv",
            [(before.shape, bf16), (arrived.shape, bf16)],
            flops=2 * pass_flops,
            moved=weight_bytes,
        )

    head = width // 2
    expand, first, raised, own = call(
        prime_kernel,
        (inner_cols[0], value_rows[0], adapter_expand[0], adapter_down[0]),
        "hhhh",
        [
            ((rank, width), bf16),
            ((head, rank), bf16),
            ((count, width), bf16),
            ((rows, width), bf16),
        ],
        [
            VMEM(inner_cols.shape[1:], bf16),
            VMEM((q_dev, width), bf16),
            pltpu.SemaphoreType.DMA((2,)),
            pltpu.SemaphoreType.DMA((PARTS + 1,)),
        ],
        flops=pass_flops,
        moved=2 * weight_bytes,
    )

    arrived = upward(own, 0, 1, 2)
    (source,) = tie([adapter_down[0]], own)
    (rest,) = call(
        keep_kernel,
        (source,),
        "h",
        [((width - head, rank), bf16)],
        [pltpu.SemaphoreType.DMA],
        moved=2 * weight_bytes,
    )
    arrived, rest = lax.optimization_barrier((arrived, rest))
    down = (first, rest)
    lower_ranks, leaving = through(1, 0, arrived, jnp.zeros((rows, rank), bf16))
    moving = jnp.concatenate([leaving, own])

    cut = tok_dev * 5 // 8

    def lift(start, end, token):
        (cot,) = tie([cotangent], token)
        return call(
            functools.partial(lift_kernel, start),
            (cot, expand),
            "hv",
            [((end - start, rank), bf16)],
            [
                VMEM((end - start, width), bf16),
                VMEM((end - start, rank), f32),
                pltpu.SemaphoreType.DMA((PARTS,)),
            ],
            flops=2 * (end - start) * width * rank,
            moved=weight_bytes,
        )[0]

    arrived = upward(moving, 1, 1, 2)
    wide = tie([value_rows[0], input_rows[0]], moving)
    wide = spread(jnp.concatenate(wide), "dp")
    lifted = [lift(0, cut, moving)]
    arrived, lifted[0] = lax.optimization_barrier((arrived, lifted[0]))

    slots = []
    empty = jnp.zeros((2 * rows, rank), bf16)
    for slot in range(1, chips):
        found, leaving = through(0, slot, arrived, empty)
        arrived = upward(leaving, 2 * slot, 1, 2)
        if slot == 1:
            (hid,) = tie([hidden_cols[0]], leaving)
            (hidden,) = call(
                functools.partial(hidden_kernel, q_dev),
                (hid, *down),
                "hvv",
                [((count, width), bf16)],
                [VMEM(hidden_cols.shape[1:], bf16), pltpu.SemaphoreType.DMA((1,))],
                flops=2 * count * width * rank,
                moved=weight_bytes,
            )
            wide = jnp.concatenate(tie(wide, hidden))
            arrived, wide = lax.optimization_barrier((arrived, wide))
        if slot == 2:
            (cot,) = tie([cotangent], leaving)
            right = dot_nt(right_rows, cot)
            arrived, right, *left_up = lax.optimization_barrier((arrived, right, *left_up))
        if slot == top:
            others = swap(jnp.stack(tie(left_up, leaving)), "pipe", 1)
            arrived, others = lax.optimization_barrier((arrived, others))
            break
        found, leaving = through(1, slot, arrived, found)
        slots.append(found)
        arrived = upward(leaving, 2 * slot + 1, 1, 2)
        if slot == 1:
            left_rows, right_rows = call(
                functools.partial(weave_kernel, q_dev),
                (hidden, wide, raised),
                "vvv",
                [((count, width), bf16), ((count, width), bf16)],
                flops=2 * count * width,
                moved=weight_bytes // 2,
            )
            left = dot_nt(left_rows, activations[0]) * live
            left_own = left.astype(bf16)
            left_up = [left_own] + [upward(left_own, 0, 2 * hop, 1) for hop in range(1, chips)]
            arrived, left_own = lax.optimization_barrier((arrived, left_own))
        if slot == top - 1:
            (early,) = tie([jnp.concatenate([lower_ranks] + slots)], leaving)
            early = spread(early, "dp")
            lifted.append(lift(cut, tok_dev, leaving))
            arrived, lifted[1], *early = lax.optimization_barrier((arrived, lifted[1], *early))

    (late,) = call(
        functools.partial(last_kernel, top),
        (arrived, found, *down),
        "vvvv",
        [((2 * rows, rank), bf16)],
        flops=pass_flops,
        moved=weight_bytes,
    )
    (right,) = tie([right], late)
    (sums,) = call(
        functools.partial(early_kernel, chips, rows),
        (left, right, others, *lifted, *left_up, *early),
        "v" * (5 + chips + columns),
        [((max(ex_dev, 8), count), f32)],
        flops=2 * count * rank * tok_dev * (2 * chips),
        moved=weight_bytes,
    )
    late = spread(late, "dp")
    (sums,) = call(
        functools.partial(late_kernel, chips, rows),
        (left_up[-1], others, sums, *lifted, *late),
        "v" * (5 + columns),
        [(sums.shape, f32)],
        flops=2 * count * rank * tok_dev * 2,
        moved=weight_bytes // 8,
    )
    sums = sums + swap(sums, "pipe", 1)
    below = [[(z, (z + hop) % top) for z in range(top)] for hop in range(1, top)]
    crossing = [[(top, z), (z, top)] for z in range(top)]
    parts = [sums] + [between(sums, chosen) for chosen in below + crossing]
    (scores,) = call(
        functools.partial(final_kernel, q_dev),
        (query_example[None], *parts),
        "v" * (1 + len(parts)),
        [((ex_dev, columns * q_dev), f32)],
        kept=jax.ShapeDtypeStruct,
    )
    return scores


def solution(mesh):
    in_specs = (
        P("pipe", "dp", None),
        P("dp", None),
        P("pipe", None, None),
        P("pipe", None, None),
        P("pipe", "dp", None),
        P("pipe", "dp", None),
        P("pipe", None, None),
        P("pipe", None, None),
        P("dp"),
        P(),
    )
    out_specs = P("dp", None)
    return jax.shard_map(local, mesh=mesh, in_specs=in_specs, out_specs=out_specs, check_vma=False)
```

```python
import functools

import jax
import jax.numpy as jnp
from jax import lax
from jax.experimental import pallas as pl
from jax.experimental.pallas import tpu as pltpu
from jax.sharding import PartitionSpec as P

SLOT = 128
PARTS = 4
AHEAD = 3


adapter_scale = 0.25
bf16 = jnp.bfloat16
f32 = jnp.float32
VMEM = pltpu.VMEM


def dot_nn(a, b, precision=None):
    return lax.dot_general(
        a, b, (((1,), (0,)), ((), ())), preferred_element_type=f32, precision=precision
    )


def dot_nt(a, b, precision=None):
    return lax.dot_general(
        a, b, (((1,), (1,)), ((), ())), preferred_element_type=f32, precision=precision
    )


def swap(value, axis, distance):
    count = lax.axis_size(axis)
    return lax.ppermute(value, axis, [(source, source ^ distance) for source in range(count)])


def spread(value, axis):
    far = [swap(value, axis, d) for d in reversed(range(1, lax.axis_size(axis)))]
    return [value] + far[::-1]


def upward(value, first, hop, stride):
    count = lax.axis_size("pipe")
    return lax.ppermute(
        value, "pipe", [(source, source + hop) for source in range(first, count - hop, stride)]
    )


def around(value, hop):
    count = lax.axis_size("pipe")
    return lax.ppermute(
        value, "pipe", [(source, (source + 2 * hop) % count) for source in range(count)]
    )


def tie(values, token):
    *values, _ = lax.optimization_barrier((*values, token))
    return values


def call(kernel, operands, places, outs, scratch=(), flops=0, moved=0, kept=VMEM):
    space = {"v": VMEM, "s": pltpu.SMEM, "h": pltpu.HBM}
    operands = [
        x if place == "s" else pltpu.with_memory_space_constraint(x, space[place])
        for x, place in zip(operands, places)
    ]
    return pl.pallas_call(
        kernel,
        in_specs=[pl.BlockSpec(memory_space=space[place]) for place in places],
        out_specs=[pl.BlockSpec(memory_space=VMEM) for _ in outs],
        out_shape=[kept(shape, dtype) for shape, dtype in outs],
        scratch_shapes=list(scratch),
        cost_estimate=pl.CostEstimate(flops=flops, bytes_accessed=moved, transcendentals=0),
        compiler_params=pltpu.CompilerParams(vmem_limit_bytes=16 * 2**20),
    )(*operands)


def picks(shape, q_dev, place):
    row = lax.broadcasted_iota(jnp.int32, shape, 0)
    query = lax.broadcasted_iota(jnp.int32, shape, 1)
    block = lax.axis_index("dp") ^ (row // (2 * q_dev))
    wanted = block * q_dev + row % q_dev
    found = (query == wanted) & ((row // q_dev) % 2 == place)
    return jnp.where(found, 1.0, 0.0)


def fetch(pairs, sems):
    return [
        pltpu.make_async_copy(source, target, sems.at[at])
        for at, (source, target) in enumerate(pairs)
    ]


def begin(copies):
    for copy in copies[:AHEAD]:
        copy.start()


def arrive(copies, part):
    copies[part].wait()
    if part + AHEAD < len(copies):
        copies[part + AHEAD].start()


def prime_kernel(
    cols_hbm, values_hbm, expand, down, kept, head, raised, own, cols, values, few, sems
):
    step = expand.shape[1] // PARTS
    small = fetch([(cols_hbm, cols), (values_hbm, values)], few)
    begin(small)
    spans = [pl.ds(part * step, step) for part in range(PARTS)]
    pairs = [(expand.at[:, span], kept.at[:, span]) for span in spans]
    copies = fetch(pairs + [(down.at[pl.ds(0, head.shape[0])], head)], sems)
    begin(copies)
    rows = own.shape[0]
    q_dev = rows // 2
    laid = picks((raised.shape[0], cols.shape[0]), q_dev, 1).astype(bf16)
    for copy in small:
        copy.wait()
    laid = dot_nn(laid, cols[...]).astype(bf16)
    for part in range(PARTS):
        span = slice(part * step, (part + 1) * step)
        arrive(copies, part)
        found = adapter_scale * dot_nn(laid, kept[:, span])
        raised[:, span] = found.astype(bf16)
        above = jnp.concatenate([values[:, span].astype(f32), found[q_dev:rows]])
        own[:, span] = above.astype(bf16)
    arrive(copies, PARTS)


def keep_kernel(down, rest, sem):
    count = rest.shape[0]
    copy = pltpu.make_async_copy(down.at[pl.ds(down.shape[0] - count, count)], rest, sem)
    copy.start()
    copy.wait()


def down_rows(head, rest, at, count):
    if at < head.shape[0]:
        return head[at : at + count, :]
    return rest[at - head.shape[0] : at - head.shape[0] + count, :]


def hidden_kernel(q_dev, cols_hbm, head, rest, raised, cols, few):
    step = raised.shape[1] // PARTS
    small = fetch([(cols_hbm, cols)], few)
    begin(small)
    laid = picks((raised.shape[0], cols.shape[0]), q_dev, 0).astype(bf16)
    small[0].wait()
    laid = dot_nn(laid, cols[...]).astype(bf16)
    for part in range(PARTS):
        span = slice(part * step, (part + 1) * step)
        raised[:, span] = (adapter_scale * dot_nt(laid, down_rows(head, rest, part * step, step))).astype(bf16)


def on_turn(core, slot):
    layer = lax.axis_index("pipe")
    return jnp.logical_and(layer % 2 == core, layer // 2 >= slot)


def through_kernel(core, slot, arrived, before, head, rest, expand, ranks, leaving):
    depth = arrived.shape[1]
    step = 2 * ranks.shape[1]
    mine = on_turn(core, slot)

    @pl.when(jnp.logical_not(mine))
    def _():
        ranks[...] = before[...]

    @pl.when(mine)
    def _():
        total = jnp.zeros(ranks.shape, f32)
        for at in range(0, depth, step):
            total += dot_nn(arrived[:, at : at + step], down_rows(head, rest, at, step))
        found = total.astype(bf16)
        ranks[...] = found
        for at in range(0, depth, step):
            more = adapter_scale * dot_nn(found, expand[:, at : at + step])
            leaving[:, at : at + step] = (arrived[:, at : at + step].astype(f32) + more).astype(bf16)


def last_kernel(slot, arrived, before, head, rest, ranks):
    depth = arrived.shape[1]
    step = 2 * ranks.shape[1]
    mine = on_turn(1, slot)

    @pl.when(jnp.logical_not(mine))
    def _():
        ranks[...] = before[...]

    @pl.when(mine)
    def _():
        total = jnp.zeros(ranks.shape, f32)
        for at in range(0, depth, step):
            total += dot_nn(arrived[:, at : at + step], down_rows(head, rest, at, step))
        ranks[...] = total.astype(bf16)


def lift_kernel(start, cotangent, expand, lifted, buffer, total, sems):
    count, depth = buffer.shape
    parts = PARTS
    step = depth // parts
    spans = [pl.ds(part * step, step) for part in range(parts)]
    rows = pl.ds(start, count)
    copies = fetch([(cotangent.at[rows, span], buffer.at[:, span]) for span in spans], sems)
    begin(copies)
    for part in range(parts):
        span = slice(part * step, (part + 1) * step)
        arrive(copies, part)
        found = dot_nt(buffer[:, span], expand[:, span])
        if part == 0:
            total[...] = found
        elif part < parts - 1:
            total[...] += found
        else:
            lifted[...] = (adapter_scale * (total[...] + found)).astype(bf16)


def weave_kernel(q_dev, hidden, rows, raised, left_rows, right_rows):
    count, depth = rows.shape
    step = depth // 8
    place = lax.broadcasted_iota(jnp.int32, (count, step), 0) // q_dev
    first = place % 2 == 0
    for at in range(0, depth, step):
        span = slice(at, at + step)
        given = rows[:, span].astype(f32)
        left_rows[:, span] = jnp.where(first, hidden[:, span].astype(f32), given).astype(bf16)
        right_rows[:, span] = jnp.where(first, given, raised[:, span].astype(f32)).astype(bf16)


def summed(terms, shape):
    example = lax.broadcasted_iota(jnp.int32, (shape[0], terms.shape[1]), 0)
    position = lax.broadcasted_iota(jnp.int32, (shape[0], terms.shape[1]), 1)
    ones = jnp.where(position // SLOT == example, 1.0, 0.0)
    return dot_nt(ones, terms, lax.Precision.HIGHEST)


def weighed(weights, blocks, at, rows, lifted):
    ranks = jnp.concatenate([block[at : at + rows, :].astype(f32) for block in blocks])
    ranks = ranks.astype(bf16)
    return weights * jnp.concatenate([dot_nt(ranks, part[...]) for part in lifted], axis=1)


def by_layer(own, other):
    upper = jnp.full(own.shape, lax.axis_index("pipe") % 2, jnp.int32) == 1
    own, other = own.astype(f32), other.astype(f32)
    return jnp.where(upper, other, own), jnp.where(upper, own, other)


def early_kernel(chips, rows, left, right, others, *refs):
    lifted, ups, blocks, sums = refs[:2], refs[2 : 2 + chips], refs[2 + chips : -1], refs[-1]
    terms = left[...] * right[...]
    for slot in range(chips - 1):
        lower, upper = by_layer(ups[slot][...], others[slot])
        if slot == 0:
            terms += weighed(lower, blocks, 0, rows, lifted)
        else:
            at = rows * (2 * slot - 1)
            terms += weighed(lower, blocks, at, rows, lifted)
            terms += weighed(upper, blocks, at + rows, rows, lifted)
    sums[...] = summed(terms, sums.shape)


def late_kernel(chips, rows, own, others, early, *refs):
    lifted, blocks, sums = refs[:2], refs[2:-1], refs[-1]
    lower, upper = by_layer(own[...], others[chips - 1])
    terms = weighed(lower, blocks, 0, rows, lifted)
    terms += weighed(upper, blocks, rows, rows, lifted)
    sums[...] = early[...] + summed(terms, sums.shape)


def final_kernel(q_dev, queries, *refs):
    parts, scores = refs[:-1], refs[-1]
    total = parts[0][...]
    for part in parts[1:]:
        total += part[...]
    ex_dev, q_all = scores.shape
    shape = (total.shape[1], q_all)
    laid = picks(shape, q_dev, 0) + picks(shape, q_dev, 1)
    total = dot_nn(total, laid, lax.Precision.HIGHEST)[:ex_dev]
    example = lax.axis_index("dp") * ex_dev + lax.broadcasted_iota(jnp.int32, scores.shape, 0)
    keep = example != jnp.broadcast_to(queries[...], scores.shape)
    scores[...] = jnp.where(keep, total * SLOT ** (-0.5), 0.0)


def local(
    activations,
    cotangent,
    adapter_down,
    adapter_expand,
    value_rows,
    input_rows,
    hidden_cols,
    inner_cols,
    lengths,
    query_example,
):
    columns = lax.axis_size("dp")
    chips = lax.axis_size("pipe") // 2
    top = chips - 1
    tok_dev = activations.shape[1]
    ex_dev = tok_dev // SLOT
    q_dev = value_rows.shape[1]
    rows = 2 * q_dev
    count = columns * rows
    width, rank = adapter_down.shape[1:]
    weight_bytes = 2 * width * rank
    pass_flops = 2 * rows * width * rank

    offsets = lax.broadcasted_iota(jnp.int32, (ex_dev, SLOT), 1)
    live = (offsets < lengths[:, None]).astype(f32).reshape(1, tok_dev)

    def through(core, slot, arrived, before):
        return call(
            functools.partial(through_kernel, core, slot),
            (arrived, before, *down, expand),
            "vvvvv",
            [(before.shape, bf16), (arrived.shape, bf16)],
            flops=2 * pass_flops,
            moved=weight_bytes,
        )

    head = width // 2
    expand, first, raised, own = call(
        prime_kernel,
        (inner_cols[0], value_rows[0], adapter_expand[0], adapter_down[0]),
        "hhhh",
        [
            ((rank, width), bf16),
            ((head, rank), bf16),
            ((count, width), bf16),
            ((rows, width), bf16),
        ],
        [
            VMEM(inner_cols.shape[1:], bf16),
            VMEM((q_dev, width), bf16),
            pltpu.SemaphoreType.DMA((2,)),
            pltpu.SemaphoreType.DMA((PARTS + 1,)),
        ],
        flops=pass_flops,
        moved=2 * weight_bytes,
    )

    arrived = upward(own, 0, 1, 2)
    (source,) = tie([adapter_down[0]], own)
    (rest,) = call(
        keep_kernel,
        (source,),
        "h",
        [((width - head, rank), bf16)],
        [pltpu.SemaphoreType.DMA],
        moved=2 * weight_bytes,
    )
    arrived, rest = lax.optimization_barrier((arrived, rest))
    down = (first, rest)
    lower_ranks, leaving = through(1, 0, arrived, jnp.zeros((rows, rank), bf16))
    moving = jnp.concatenate([leaving, own])

    cut = tok_dev * 5 // 8

    def lift(start, end, token):
        (cot,) = tie([cotangent], token)
        return call(
            functools.partial(lift_kernel, start),
            (cot, expand),
            "hv",
            [((end - start, rank), bf16)],
            [
                VMEM((end - start, width), bf16),
                VMEM((end - start, rank), f32),
                pltpu.SemaphoreType.DMA((PARTS,)),
            ],
            flops=2 * (end - start) * width * rank,
            moved=weight_bytes,
        )[0]

    arrived = upward(moving, 1, 1, 2)
    wide = tie([value_rows[0], input_rows[0]], moving)
    wide = spread(jnp.concatenate(wide), "dp")
    lifted = [lift(0, cut, moving)]
    arrived, lifted[0] = lax.optimization_barrier((arrived, lifted[0]))

    slots = []
    empty = jnp.zeros((2 * rows, rank), bf16)
    for slot in range(1, chips):
        found, leaving = through(0, slot, arrived, empty)
        arrived = upward(leaving, 2 * slot, 1, 2)
        if slot == 1:
            (hid,) = tie([hidden_cols[0]], leaving)
            (hidden,) = call(
                functools.partial(hidden_kernel, q_dev),
                (hid, *down),
                "hvv",
                [((count, width), bf16)],
                [VMEM(hidden_cols.shape[1:], bf16), pltpu.SemaphoreType.DMA((1,))],
                flops=2 * count * width * rank,
                moved=weight_bytes,
            )
            wide = jnp.concatenate(tie(wide, hidden))
            arrived, wide = lax.optimization_barrier((arrived, wide))
        if slot == 2:
            (cot,) = tie([cotangent], leaving)
            right = dot_nt(right_rows, cot)
            arrived, right, *left_up = lax.optimization_barrier((arrived, right, *left_up))
        if slot == top:
            others = swap(jnp.stack(tie(left_up, leaving)), "pipe", 1)
            arrived, others = lax.optimization_barrier((arrived, others))
            break
        found, leaving = through(1, slot, arrived, found)
        slots.append(found)
        arrived = upward(leaving, 2 * slot + 1, 1, 2)
        if slot == 1:
            left_rows, right_rows = call(
                functools.partial(weave_kernel, q_dev),
                (hidden, wide, raised),
                "vvv",
                [((count, width), bf16), ((count, width), bf16)],
                flops=2 * count * width,
                moved=weight_bytes // 2,
            )
            left = dot_nt(left_rows, activations[0]) * live
            left_own = left.astype(bf16)
            left_up = [left_own] + [upward(left_own, 0, 2 * hop, 1) for hop in range(1, chips)]
            arrived, left_own = lax.optimization_barrier((arrived, left_own))
        if slot == top - 1:
            (early,) = tie([jnp.concatenate([lower_ranks] + slots)], leaving)
            early = spread(early, "dp")
            lifted.append(lift(cut, tok_dev, leaving))
            arrived, lifted[1], *early = lax.optimization_barrier((arrived, lifted[1], *early))

    (late,) = call(
        functools.partial(last_kernel, top),
        (arrived, found, *down),
        "vvvv",
        [((2 * rows, rank), bf16)],
        flops=pass_flops,
        moved=weight_bytes,
    )
    (right,) = tie([right], late)
    (sums,) = call(
        functools.partial(early_kernel, chips, rows),
        (left, right, others, *lifted, *left_up, *early),
        "v" * (5 + chips + columns),
        [((max(ex_dev, 8), count), f32)],
        flops=2 * count * rank * tok_dev * (2 * chips),
        moved=weight_bytes,
    )
    late = spread(late, "dp")
    (sums,) = call(
        functools.partial(late_kernel, chips, rows),
        (left_up[-1], others, sums, *lifted, *late),
        "v" * (5 + columns),
        [(sums.shape, f32)],
        flops=2 * count * rank * tok_dev * 2,
        moved=weight_bytes // 8,
    )
    sums = sums + swap(sums, "pipe", 1)
    parts = [sums] + [around(sums, hop) for hop in range(1, chips)]
    (scores,) = call(
        functools.partial(final_kernel, q_dev),
        (query_example[None], *parts),
        "v" * (1 + chips),
        [((ex_dev, columns * q_dev), f32)],
        kept=jax.ShapeDtypeStruct,
    )
    return scores


def solution(mesh):
    in_specs = (
        P("pipe", "dp", None),
        P("dp", None),
        P("pipe", None, None),
        P("pipe", None, None),
        P("pipe", "dp", None),
        P("pipe", "dp", None),
        P("pipe", None, None),
        P("pipe", None, None),
        P("dp"),
        P(),
    )
    out_specs = P("dp", None)
    return jax.shard_map(local, mesh=mesh, in_specs=in_specs, out_specs=out_specs, check_vma=False)
```
